32 devices in a mesh: ctx: 16 (over z, y, x), head: 2 (over core).
Axes of the slice: x: 2, y: 2, z: 4, core: 2. Of those that a mesh axis runs over, the one named last changes fastest.
Arguments:
- queries: bfloat16 [2048, 2048], P('ctx', 'head'), may hold values from -16 to 16
- key_rows: bfloat16 [2048, 2048], P('ctx', 'head'), may hold values from -16 to 16
- value_rows: bfloat16 [2048, 2048], P('ctx', 'head'), may hold values from -16 to 16
- out_weight: bfloat16 [2048, 2048], P('head'), may hold values from -0.125 to 0.125
- cotangent: bfloat16 [2048, 2048], P('ctx', 'head'), may hold values from -48 to 48
Outputs:
- output: bfloat16 [2048, 2048], P('ctx', 'head')
- grad_queries: bfloat16 [2048, 2048], P('ctx', 'head')
- grad_keys: bfloat16 [2048, 2048], P('ctx', 'head')
- grad_values: bfloat16 [2048, 2048], P('ctx', 'head')
The draws below stay inside these ranges and needn't reach their ends.
All inputs are finite; a program needn't handle non-finite values.
Results may differ from the reference program's by a relative error of at most 0.025.
Values may be sent and summed in bfloat16 or wider, within the bound.
No kernel may reach another device: no remote copies, remote signals or barrier semaphores. Data moves between devices by JAX's collectives and lax.ppermute only.
A program may use at most 64 MiB of HBM per device.

```python
import jax
import jax.numpy as jnp
from jax import lax

D = 2048
HEADS = 16
DH = 128
LEAF = 128
TOKENS = 2048
HD = 2048


def regional_sample(key):
    first_key, second_key = jax.random.split(key, 2)
    rough_part = jax.random.normal(first_key, (TOKENS, HD), jnp.float32)
    region = jax.random.normal(second_key, (TOKENS // LEAF, HD), jnp.float32)
    return rough_part + jnp.repeat(region, LEAF, axis=0)


def draw_queries(key, part):
    sample = regional_sample(jax.random.fold_in(key, 11))
    return jnp.clip(sample, -16.0, 16.0).astype(jnp.bfloat16)


def draw_key_rows(key, part):
    sample = regional_sample(jax.random.fold_in(key, 12))
    return jnp.clip(sample, -16.0, 16.0).astype(jnp.bfloat16)


def draw_value_rows(key, part):
    sample = regional_sample(jax.random.fold_in(key, 13))
    return jnp.clip(sample, -16.0, 16.0).astype(jnp.bfloat16)


def shard_levels(rng, extent, pieces, low, high):
    level = 1.0
    for position, shards_of in pieces:
        heights = jax.random.uniform(jax.random.fold_in(jax.random.fold_in(rng, 6), position), (shards_of,), jnp.float32, low / len(pieces), high / len(pieces))
        level = level * jnp.repeat(jnp.exp(heights), extent[position] // shards_of).reshape((-1,) + (1,) * (len(extent) - 1 - position))
    return level


def centred(key, extent, scale, bound, shards=(), held_as=jnp.bfloat16):
    level = shard_levels(key, extent, shards, -0.22, 0.18) if shards else 1.0
    array = jax.random.normal(key, extent, jnp.float32) * scale * level
    return jnp.minimum(jnp.maximum(array, -bound), bound).astype(held_as)


def setup_inputs(seed: int = 0) -> dict:
    keys = jax.random.split(jax.random.key(seed), 6)
    queries = draw_queries(jax.random.fold_in(keys[5], 71), 0)
    key_rows = draw_key_rows(jax.random.fold_in(keys[5], 71), 0)
    value_rows = draw_value_rows(jax.random.fold_in(keys[5], 71), 0)
    out_weight = centred(keys[3], (HD, D), HD ** -0.5, 0.125, ((0, 2),))
    cotangent = centred(keys[4], (TOKENS, D), 8.0, 48.0, ((0, 16), (1, 2)))
    return {"queries": queries, "key_rows": key_rows, "value_rows": value_rows, "out_weight": out_weight, "cotangent": cotangent}


def pool_pairs(matrix):
    shaped = matrix.reshape((matrix.shape[0] // 2, 2) + matrix.shape[1:]).astype(jnp.float32)
    return ((shaped[:, 0] + shaped[:, 1]) * 0.5).astype(jnp.bfloat16)


def spread_pairs(gradient):
    halved = gradient * 0.5
    doubled = jnp.broadcast_to(halved[:, None], (halved.shape[0], 2) + halved.shape[1:])
    return doubled.reshape((halved.shape[0] * 2,) + halved.shape[1:])


def flip_blocks(matrix):
    paired = matrix.reshape((matrix.shape[0] // (2 * LEAF), 2, LEAF) + matrix.shape[1:])
    return jnp.flip(paired, 1).reshape((matrix.shape[0] // LEAF, LEAF) + matrix.shape[1:])


def key_sets_of(key_head, value_head):
    levels = (TOKENS // LEAF).bit_length() - 1
    key_sets = [(key_head.reshape(-1, LEAF, DH), value_head.reshape(-1, LEAF, DH))]
    level_keys, level_values = key_head, value_head
    for level_index in range(1, levels + 1):
        if level_index > 1:
            level_keys = pool_pairs(level_keys)
            level_values = pool_pairs(level_values)
        key_sets.append((flip_blocks(level_keys), flip_blocks(level_values)))
    return key_sets


def softmax_parts(query_head, key_sets):
    scores = []
    for key_blocks, value_blocks in key_sets:
        queried = query_head.reshape(key_blocks.shape[0], -1, DH).astype(jnp.float32)
        scored = jnp.einsum("cwd,cbd->cwb", queried, key_blocks.astype(jnp.float32))
        scores.append(scored.reshape(TOKENS, LEAF) * (DH ** -0.5))
    row_max = jnp.max(scores[0], -1)
    for scored in scores[1:]:
        row_max = jnp.maximum(row_max, jnp.max(scored, -1))
    weights = [jnp.exp(scored - row_max[:, None]) for scored in scores]
    row_total = jnp.zeros((TOKENS,), jnp.float32)
    for weight_block in weights:
        row_total = row_total + jnp.sum(weight_block, -1)
    return weights, row_total


def round_trip(values):
    return lax.optimization_barrier(values.astype(jnp.bfloat16)).astype(jnp.float32)


def head_forward(query_head, key_head, value_head):
    key_sets = key_sets_of(key_head, value_head)
    weights, row_total = softmax_parts(query_head, key_sets)
    numerator = jnp.zeros((TOKENS, DH), jnp.float32)
    for weight_block, (key_blocks, value_blocks) in zip(weights, key_sets):
        block_count = key_blocks.shape[0]
        rounded = round_trip(weight_block).reshape(block_count, -1, LEAF)
        numerator = numerator + jnp.einsum("cwb,cbd->cwd", rounded, value_blocks.astype(jnp.float32)).reshape(TOKENS, DH)
    return (numerator / row_total[:, None]).astype(jnp.bfloat16)


def head_backward(query_head, key_head, value_head, attended_head, grad_head):
    key_sets = key_sets_of(key_head, value_head)
    weights, row_total = softmax_parts(query_head, key_sets)
    grad_float = grad_head.astype(jnp.float32)
    row_delta = jnp.sum(grad_float * attended_head.astype(jnp.float32), -1)
    query_grad = jnp.zeros((TOKENS, DH), jnp.float32)
    key_grads = []
    value_grads = []
    for weight_block, (key_blocks, value_blocks) in zip(weights, key_sets):
        block_count = key_blocks.shape[0]
        probabilities = weight_block / row_total[:, None]
        grad_blocks = grad_float.reshape(block_count, -1, DH)
        query_blocks = query_head.astype(jnp.float32).reshape(block_count, -1, DH)
        value_dots = jnp.einsum("cwd,cbd->cwb", grad_blocks, value_blocks.astype(jnp.float32)).reshape(TOKENS, LEAF)
        score_grad = round_trip(probabilities * (value_dots - row_delta[:, None])).reshape(block_count, -1, LEAF)
        query_grad = query_grad + jnp.einsum("cwb,cbd->cwd", score_grad, key_blocks.astype(jnp.float32)).reshape(TOKENS, DH)
        key_grads.append(jnp.einsum("cwb,cwd->cbd", score_grad, query_blocks) * (DH ** -0.5))
        rounded_probs = round_trip(probabilities).reshape(block_count, -1, LEAF)
        value_grads.append(jnp.einsum("cwb,cwd->cbd", rounded_probs, grad_blocks))
    levels = len(key_sets) - 1
    carried_keys = flip_blocks(key_grads[levels].reshape(-1, DH)).reshape(-1, DH)
    carried_values = flip_blocks(value_grads[levels].reshape(-1, DH)).reshape(-1, DH)
    for level_index in range(levels - 1, 0, -1):
        carried_keys = flip_blocks(key_grads[level_index].reshape(-1, DH)).reshape(-1, DH) + spread_pairs(carried_keys)
        carried_values = flip_blocks(value_grads[level_index].reshape(-1, DH)).reshape(-1, DH) + spread_pairs(carried_values)
    grad_queries = (query_grad * (DH ** -0.5)).astype(jnp.bfloat16)
    grad_keys = (key_grads[0].reshape(TOKENS, DH) + carried_keys).astype(jnp.bfloat16)
    grad_values = (value_grads[0].reshape(TOKENS, DH) + carried_values).astype(jnp.bfloat16)
    return grad_queries, grad_keys, grad_values


def split_heads(matrix):
    return matrix.reshape(TOKENS, HEADS, DH).transpose(1, 0, 2)


def join_heads(matrix):
    return matrix.transpose(1, 0, 2).reshape(TOKENS, HD)


def reference(queries, key_rows, value_rows, out_weight, cotangent):
    query_split = split_heads(queries)
    key_split = split_heads(key_rows)
    value_split = split_heads(value_rows)
    attended = lax.map(lambda packed: head_forward(packed[0], packed[1], packed[2]), (query_split, key_split, value_split))
    output = jnp.dot(join_heads(attended), out_weight, preferred_element_type=jnp.float32).astype(jnp.bfloat16)
    grad_attended = lax.dot_general(cotangent, out_weight, (((1,), (1,)), ((), ())), preferred_element_type=jnp.float32).astype(jnp.bfloat16)
    gradient = lax.map(lambda packed: head_backward(packed[0], packed[1], packed[2], packed[3], packed[4]), (query_split, key_split, value_split, attended, split_heads(grad_attended)))
    return output, join_heads(gradient[0]), join_heads(gradient[1]), join_heads(gradient[2])
```

```python
import jax
import jax.numpy as jnp
from jax import lax
from jax.experimental import pallas as pl
from jax.experimental.pallas import tpu as pltpu
from jax.sharding import PartitionSpec as P

DH = 128
PLANE = 4
SCALE = DH ** (-0.5)
BF16 = jnp.bfloat16
F32 = jnp.float32


def xor_permute(block, mask, axis="ctx"):
    count = lax.axis_size(axis)
    return lax.ppermute(block, axis, [(i, i ^ mask) for i in range(count)])


def dot(a, b, contract_a=1, contract_b=0):
    return lax.dot_general(
        a, b, (((contract_a,), (contract_b,)), ((), ())), preferred_element_type=F32
    )


def pool_matrix(rows):
    out = lax.broadcasted_iota(jnp.int32, (rows // 2, rows), 0)
    src = lax.broadcasted_iota(jnp.int32, (rows // 2, rows), 1)
    return jnp.where(src // 2 == out, 0.5, 0.0).astype(BF16)


def spread_matrix(rows, times):
    out = lax.broadcasted_iota(jnp.int32, (rows * times, rows), 0)
    src = lax.broadcasted_iota(jnp.int32, (rows * times, rows), 1)
    return jnp.where(out // times == src, 1.0 / times, 0.0).astype(BF16)


def pool(block):
    return dot(pool_matrix(block.shape[0]), block).astype(BF16)


def spread(block, times):
    return dot(spread_matrix(block.shape[0], times), block.astype(BF16))


def call(kernel, outs, *args, flops=0, name=None):
    vmem = pl.BlockSpec(memory_space=pltpu.VMEM)
    moved = sum(a.size * a.dtype.itemsize for a in args)
    return pl.pallas_call(
        kernel,
        out_shape=outs,
        in_specs=[vmem] * len(args),
        out_specs=[vmem] * len(outs),
        compiler_params=pltpu.CompilerParams(vmem_limit_bytes=32 * 1024 * 1024),
        cost_estimate=pl.CostEstimate(flops=flops, bytes_accessed=moved, transcendentals=0),
        name=name,
    )(*args)


def columns(r, width):
    place = (lax.axis_index("ctx") & (PLANE - 1)) ^ r
    return pl.ds(pl.multiple_of(place * width, width), width)


def split_kernel(q_ref, k_ref, v_ref, *outs):
    width = q_ref.shape[1] // PLANE
    rows = q_ref.shape[0]
    q_out, kv_out, top_out = outs[:PLANE], outs[PLANE : 2 * PLANE], outs[2 * PLANE :]
    for r in range(PLANE):
        here = columns(r, width)
        k, v = k_ref[:, here], v_ref[:, here]
        q_out[r][...] = q_ref[:, here]
        kv_out[r][:rows, :] = k
        kv_out[r][rows:, :] = v
        top_out[r][: rows // 4, :] = pool(pool(k))
        top_out[r][rows // 4 :, :] = pool(pool(v))


def far_kernel(*refs):
    tops, (near_out, far_out) = refs[:PLANE], refs[PLANE:]
    half = tops[0].shape[0] // 2
    rows = half * PLANE
    for part in range(2):
        whole = jnp.concatenate([top[part * half : (part + 1) * half, :] for top in tops], 0)
        near_out[part * rows : (part + 1) * rows, :] = whole
        far_out[part * rows // 2 : (part + 1) * rows // 2, :] = pool(whole)


def cotangent_kernel(own_ref, other_ref, w_ref, *outs):
    width = w_ref.shape[0] // PLANE
    half = own_ref.shape[1]
    head = lax.axis_index("head")
    own_at = pl.ds(pl.multiple_of(head * half, half), half)
    other_at = pl.ds(pl.multiple_of((1 - head) * half, half), half)
    for r in range(PLANE):
        here = columns(r, width)
        outs[r][...] = (
            dot(own_ref[...], w_ref[here, own_at], 1, 1)
            + dot(other_ref[...], w_ref[here, other_at], 1, 1)
        ).astype(BF16)


def attention_kernel(n_far, *refs):
    q_refs, kv_refs, g_refs = refs[:PLANE], refs[PLANE : 2 * PLANE], refs[2 * PLANE : 3 * PLANE]
    far_refs = refs[3 * PLANE : 3 * PLANE + n_far]
    outs = refs[3 * PLANE + n_far :]
    att_out, dq_out, dkv_out = outs[:PLANE], outs[PLANE : 2 * PLANE], outs[2 * PLANE : 3 * PLANE]
    far_out = outs[3 * PLANE :]
    rows = q_refs[0].shape[0]
    pair = 2 * rows
    width = q_refs[0].shape[1]
    for first in range(0, width, DH):
        lanes = slice(first, first + DH)
        leaf_k = [kv[:rows, lanes] for kv in kv_refs]
        leaf_v = [kv[rows:, lanes] for kv in kv_refs]
        far_k = [far[: far.shape[0] // 2, lanes] for far in far_refs]
        far_v = [far[far.shape[0] // 2 :, lanes] for far in far_refs]
        key_grads, value_grads = [], []
        for p in range(2):
            ours, theirs = (2 * p, 2 * p + 1), (2 - 2 * p, 3 - 2 * p)
            q = jnp.concatenate([q_refs[r][:, lanes] for r in ours], 0)
            g = jnp.concatenate([g_refs[r][:, lanes] for r in ours], 0)
            keys = jnp.concatenate(
                [leaf_k[r] for r in ours] + [pool(leaf_k[r]) for r in theirs] + far_k, 0
            )
            values = jnp.concatenate(
                [leaf_v[r] for r in ours] + [pool(leaf_v[r]) for r in theirs] + far_v, 0
            )
            scores = dot(keys, q, 1, 1) * SCALE
            weights = jnp.exp(scores - jnp.max(scores, 0, keepdims=True))
            total = jnp.sum(weights, 0, keepdims=True)
            inverse = 1.0 / total
            numerator = dot(values, weights.astype(BF16), 0, 0)
            attended = (numerator * inverse).astype(BF16)
            delta = jnp.sum(
                g.T.astype(F32) * attended.astype(F32), 0, keepdims=True
            )
            probabilities = weights * inverse
            value_dots = dot(values, g, 1, 1)
            score_grad = (probabilities * (value_dots - delta)).astype(BF16)
            dq = (dot(keys, score_grad, 0, 0) * SCALE).astype(BF16).T
            attended = attended.T
            for n, r in enumerate(ours):
                att_out[r][:, lanes] = attended[n * rows : (n + 1) * rows]
                dq_out[r][:, lanes] = dq[n * rows : (n + 1) * rows]
            key_grads.append(dot(score_grad, q) * SCALE)
            value_grads.append(dot(probabilities.astype(BF16), g))
        for part, grads in enumerate((key_grads, value_grads)):
            for p in range(2):
                pooled = grads[1 - p][pair : pair + rows]
                for n in range(2):
                    whole = grads[p][n * rows : (n + 1) * rows] + spread(
                        pooled[n * rows // 2 : (n + 1) * rows // 2], 2
                    )
                    dkv_out[2 * p + n][part * rows : (part + 1) * rows, lanes] = whole.astype(BF16)
            at = pair + rows
            for far in far_out:
                size = far.shape[0] // 2
                far[part * size : (part + 1) * size, lanes] = (
                    grads[0][at : at + size] + grads[1][at : at + size]
                ).astype(BF16)
                at += size


def carry_kernel(near_ref, far2_ref, far3_ref, *refs):
    extra, outs = refs[:-PLANE], refs[-PLANE:]
    rows = near_ref.shape[0] // 2
    for part in range(2):
        low = slice(part * rows // 2, (part + 1) * rows // 2)
        upper = far2_ref[low, :].astype(F32) + far3_ref[low, :].astype(F32)
        for ref in extra:
            upper = upper + ref[low, :].astype(F32)
        whole = near_ref[part * rows : (part + 1) * rows, :].astype(F32) + spread(upper, 2)
        size = rows // PLANE
        for r in range(PLANE):
            outs[r][part * size : (part + 1) * size, :] = whole[r * size : (r + 1) * size].astype(
                BF16
            )


def output_kernel(*refs):
    atts, w_ref, (own_out, other_out) = refs[:PLANE], refs[PLANE], refs[PLANE + 1 :]
    width = atts[0].shape[1]
    half = own_out.shape[1]
    head = lax.axis_index("head")
    for out, place in ((other_out, 1 - head), (own_out, head)):
        at = pl.ds(pl.multiple_of(place * half, half), half)
        total = dot(atts[0][...], w_ref[columns(0, width), at])
        for r in range(1, PLANE):
            total = total + dot(atts[r][...], w_ref[columns(r, width), at])
        out[...] = total.astype(out.dtype)


def join_kernel(*refs):
    dqs, dkvs, tops = refs[:PLANE], refs[PLANE : 2 * PLANE], refs[2 * PLANE : 3 * PLANE]
    gq_out, gk_out, gv_out = refs[3 * PLANE :]
    rows = dqs[0].shape[0]
    width = dqs[0].shape[1]
    for r in range(PLANE):
        here = columns(r, width)
        gq_out[:, here] = dqs[r][...]
        for part, out in enumerate((gk_out, gv_out)):
            top = tops[r][part * rows // 4 : (part + 1) * rows // 4, :]
            out[:, here] = (
                dkvs[r][part * rows : (part + 1) * rows, :].astype(F32) + spread(top, 4)
            ).astype(BF16)


def plane_exchange(blocks):
    return [blocks[0]] + [xor_permute(blocks[r], r) for r in range(1, PLANE)]


def pool_both(block):
    shaped = block.reshape((2, block.shape[0] // 4, 2) + block.shape[1:]).astype(F32)
    return ((shaped[:, :, 0] + shaped[:, :, 1]) * 0.5).astype(BF16).reshape(
        (block.shape[0] // 2,) + block.shape[1:]
    )


def spread_both(block):
    halved = block.astype(F32) * 0.5
    return jnp.repeat(halved, 2, axis=0)


def join_both(blocks):
    halves = [b.reshape((2, b.shape[0] // 2) + b.shape[1:]) for b in blocks]
    joined = jnp.concatenate(halves, 1)
    return joined.reshape((-1,) + joined.shape[2:])


def part_both(block, parts):
    shaped = block.reshape((2, parts, block.shape[0] // (2 * parts)) + block.shape[1:])
    return [shaped[:, n].reshape((-1,) + block.shape[1:]) for n in range(parts)]


def body(queries, key_rows, value_rows, out_weight, cotangent):
    rows, features = queries.shape
    width = features // PLANE
    top_rounds = lax.axis_size("ctx").bit_length() - 1 - 4
    shape = lambda n, w=width, t=BF16: jax.ShapeDtypeStruct((n, w), t)

    other_cotangent = xor_permute(cotangent, 1, "head")
    parts = call(
        split_kernel,
        [shape(rows)] * PLANE + [shape(2 * rows)] * PLANE + [shape(rows // 2)] * PLANE,
        queries, key_rows, value_rows, name="split",
    )
    tops = plane_exchange(parts[2 * PLANE :])
    key_values = plane_exchange(parts[PLANE : 2 * PLANE])
    query_parts = plane_exchange(parts[:PLANE])
    near, pooled = call(far_kernel, [shape(2 * rows), shape(rows)], *tops, name="pool_plane")
    fars = [xor_permute(near, PLANE), xor_permute(pooled, 2 * PLANE), xor_permute(pooled, 3 * PLANE)]
    if top_rounds > 0:
        span = pool_both(join_both([pooled, pool_both(fars[0]), fars[1], fars[2]]))
        for n in range(top_rounds):
            fars.append(xor_permute(span, 4 * PLANE << n))
            span = pool_both(join_both([span, fars[-1]]))
    grad_parts = plane_exchange(
        call(
            cotangent_kernel, [shape(rows)] * PLANE, cotangent, other_cotangent, out_weight,
            flops=4 * rows * features * features, name="grad_attended",
        )
    )
    results = call(
        lambda *refs: attention_kernel(len(fars), *refs),
        [shape(rows)] * (2 * PLANE)
        + [shape(2 * rows)] * PLANE
        + [shape(far.shape[0]) for far in fars],
        *query_parts, *key_values, *grad_parts, *fars,
        flops=12 * PLANE * rows * 5 * rows * width, name="attention",
    )
    far_grads = list(results[3 * PLANE :])
    extra = []
    if top_rounds > 0:
        up = None
        for n in reversed(range(top_rounds)):
            send = far_grads[3 + n].astype(F32)
            if up is not None:
                own_up, their_up = part_both(spread_both(up), 2)
                send = send + their_up
            back = xor_permute(send.astype(BF16), 4 * PLANE << n).astype(F32)
            up = back if up is None else back + own_up
        ups = part_both(spread_both(up), PLANE)
        extra = [ups[0].astype(BF16)]
        far_grads[0] = (far_grads[0].astype(F32) + spread_both(ups[1])).astype(BF16)
        far_grads[1] = (far_grads[1].astype(F32) + ups[2]).astype(BF16)
        far_grads[2] = (far_grads[2].astype(F32) + ups[3]).astype(BF16)
    backs = [xor_permute(far_grads[n], (n + 1) * PLANE) for n in range(3)]
    atts = plane_exchange(results[:PLANE])
    dqs = plane_exchange(results[PLANE : 2 * PLANE])
    dkvs = plane_exchange(results[2 * PLANE : 3 * PLANE])
    carried = plane_exchange(
        call(carry_kernel, [shape(rows // 2)] * PLANE, *backs, *extra, name="carry")
    )
    own_sum, other_sum = call(
        output_kernel, [shape(rows, features, F32), shape(rows, features)], *atts, out_weight,
        flops=4 * rows * features * features, name="project",
    )
    output = (own_sum + xor_permute(other_sum, 1, "head").astype(F32)).astype(BF16)
    grad_queries, grad_keys, grad_values = call(
        join_kernel, [shape(rows, features)] * 3, *dqs, *dkvs, *carried, name="join"
    )
    return (output, grad_queries, grad_keys, grad_values)


def solution(mesh):
    rows = P("ctx", "head")
    return jax.shard_map(
        body,
        mesh=mesh,
        in_specs=(rows, rows, rows, P("head", None), rows),
        out_specs=(rows, rows, rows, rows),
        check_vma=False,
    )
```

```python
import jax
import jax.numpy as jnp
from jax import lax
from jax.experimental import pallas as pl
from jax.experimental.pallas import tpu as pltpu
from jax.sharding import PartitionSpec as P

DH = 128
PLANE = 4
PIECES = 2
SCALE = DH ** (-0.5)
BF16 = jnp.bfloat16
F32 = jnp.float32


def xor_permute(block, mask, axis="ctx"):
    count = lax.axis_size(axis)
    return lax.ppermute(block, axis, [(i, i ^ mask) for i in range(count)])


def dot(a, b, contract_a=1, contract_b=0):
    return lax.dot_general(
        a, b, (((contract_a,), (contract_b,)), ((), ())), preferred_element_type=F32
    )


def pool_matrix(rows):
    out = lax.broadcasted_iota(jnp.int32, (rows // 2, rows), 0)
    src = lax.broadcasted_iota(jnp.int32, (rows // 2, rows), 1)
    return jnp.where(src // 2 == out, 0.5, 0.0).astype(BF16)


def spread_matrix(rows, times):
    out = lax.broadcasted_iota(jnp.int32, (rows * times, rows), 0)
    src = lax.broadcasted_iota(jnp.int32, (rows * times, rows), 1)
    return jnp.where(out // times == src, 1.0 / times, 0.0).astype(BF16)


def pool(block):
    return dot(pool_matrix(block.shape[0]), block).astype(BF16)


def spread(block, times):
    return dot(spread_matrix(block.shape[0], times), block.astype(BF16))


def call(kernel, outs, *args, after=(), hbm=(), hbm_out=False, scratch=(), cost_us=1.0, name=None):
    vmem = pl.BlockSpec(memory_space=pltpu.VMEM)
    in_hbm = pl.BlockSpec(memory_space=pltpu.HBM)
    space = pltpu.HBM if hbm_out else pltpu.VMEM
    args = [
        pltpu.with_memory_space_constraint(a, pltpu.HBM) if n in hbm else a
        for n, a in enumerate(args)
    ]
    count = len(args)
    return pl.pallas_call(
        lambda *refs: kernel(*refs[:count], *refs[count + len(after) :]),
        out_shape=[space(out.shape, out.dtype) for out in outs],
        in_specs=[in_hbm if n in hbm else vmem for n in range(count)]
        + [pl.BlockSpec(memory_space=pl.ANY)] * len(after),
        scratch_shapes=scratch,
        out_specs=[in_hbm if hbm_out else vmem] * len(outs),
        compiler_params=pltpu.CompilerParams(vmem_limit_bytes=24 * 1024 * 1024),
        cost_estimate=pl.CostEstimate(
            flops=int(cost_us * 1e9), bytes_accessed=0, transcendentals=0
        ),
        name=name,
    )(*args, *after)


def part(n, width):
    return slice(n * width, (n + 1) * width)


def start_all(pairs, sems):
    copies = [pltpu.make_async_copy(a, b, sems.at[n]) for n, (a, b) in enumerate(pairs)]
    for copy in copies:
        copy.start()
    return copies


def columns(r, width):
    place = (lax.axis_index("ctx") & (PLANE - 1)) ^ r
    return pl.ds(pl.multiple_of(place * width, width), width)


def key_value_kernel(k_ref, v_ref, *refs):
    outs, sems = refs[:PLANE], refs[PLANE]
    rows, width = k_ref.shape[0], k_ref.shape[1] // PLANE
    pairs = []
    for r in range(PLANE):
        pairs.append((k_ref.at[:, columns(r, width)], outs[r].at[part(0, rows), :]))
        pairs.append((v_ref.at[:, columns(r, width)], outs[r].at[part(1, rows), :]))
    for copy in start_all(pairs, sems):
        copy.wait()


def cotangent_kernel(q_ref, own_ref, other_ref, w_ref, *refs):
    outs, w, own, sems, w_sems = refs[:PLANE], refs[PLANE], *refs[PLANE + 1 :]
    rows, width = q_ref.shape[0], q_ref.shape[1] // PLANE
    half = own_ref.shape[1]
    head = lax.axis_index("head")
    own_at = pl.ds(pl.multiple_of(head * half, half), half)
    other_at = pl.ds(pl.multiple_of((1 - head) * half, half), half)
    here = [columns(r, width) for r in range(PLANE)]
    w_copies = [
        pltpu.make_async_copy(w_ref.at[here[r], :], w.at[here[r], :], w_sems.at[r])
        for r in range(PLANE)
    ]
    pairs = [(own_ref, own)]
    pairs += [(q_ref.at[:, here[r]], outs[r].at[part(0, rows), :]) for r in range(PLANE)]
    copies = start_all(pairs, sems)
    w_copies[0].start()
    w_copies[1].start()
    copies[0].wait()
    for r in range(PLANE):
        w_copies[r].wait()
        if r + 2 < PLANE:
            w_copies[r + 2].start()
        outs[r][rows:, :] = (
            dot(own[...], w[here[r], own_at], 1, 1)
            + dot(other_ref[...], w[here[r], other_at], 1, 1)
        ).astype(BF16)
    for copy in copies[1:]:
        copy.wait()


def far_kernel(*refs):
    kvs, (near_out, far_out) = refs[:PLANE], refs[PLANE:]
    rows, width = kvs[0].shape[0] // 2, kvs[0].shape[1]
    wide = jnp.concatenate([kv[part(m, rows), :] for m in range(2) for kv in kvs], 1)
    near = pool(pool(wide))
    far = pool(near)
    for out, pooled in ((near_out, near), (far_out, far)):
        size = pooled.shape[0]
        for n in range(2 * PLANE):
            out[part(n, size), :] = pooled[:, part(n, width)]


def key_sets(kvs, fars, p, lanes, m):
    rows = kvs[0].shape[0] // 2
    ours, theirs = kvs[2 * p : 2 * p + 2], kvs[2 - 2 * p : 4 - 2 * p]
    return jnp.concatenate(
        [kv[part(m, rows), lanes] for kv in ours]
        + [pool(kv[part(m, rows), lanes]) for kv in theirs]
        + [far[part(m, far.shape[0] // 2), lanes] for far in fars],
        0,
    )


def attention_kernel(n_far, *refs):
    kvs, qgs, fars = refs[:PLANE], refs[PLANE : 2 * PLANE], refs[2 * PLANE : 2 * PLANE + n_far]
    outs = refs[2 * PLANE + n_far :]
    atts, grad_out, prob_out = outs[:PLANE], outs[PLANE], outs[PLANE + 1]
    far_out = outs[PLANE + 2 :]
    rows, width = qgs[0].shape[0] // 2, qgs[0].shape[1]
    start = 3 * rows
    for h in range(width // DH):
        lanes = part(h, DH)
        key_grads, value_grads = [], []
        for p in range(2):
            ours = (2 * p, 2 * p + 1)
            q = jnp.concatenate([qgs[r][:rows, lanes] for r in ours], 0)
            g = jnp.concatenate([qgs[r][rows:, lanes] for r in ours], 0)
            keys = key_sets(kvs, fars, p, lanes, 0)
            values = key_sets(kvs, fars, p, lanes, 1)
            scores = dot(keys, q, 1, 1) * SCALE
            weights = jnp.exp(scores - jnp.max(scores, 0, keepdims=True))
            inverse = 1.0 / jnp.sum(weights, 0, keepdims=True)
            numerator = dot(values, weights.astype(BF16), 0, 0)
            attended = (numerator * inverse).astype(BF16)
            delta = jnp.sum(g.T.astype(F32) * attended.astype(F32), 0, keepdims=True)
            probabilities = weights * inverse
            value_dots = dot(values, g, 1, 1)
            score_grad = (probabilities * (value_dots - delta)).astype(BF16)
            rounded = probabilities.astype(BF16)
            attended = attended.T
            for n, r in enumerate(ours):
                atts[r][:, lanes] = attended[part(n, rows)]
            grad_out[2 * h + p] = score_grad
            prob_out[2 * h + p] = rounded
            key_grads.append(dot(score_grad[start:], q) * SCALE)
            value_grads.append(dot(rounded[start:], g))
        for m, grads in enumerate((key_grads, value_grads)):
            whole, at = grads[0] + grads[1], 0
            for far in far_out:
                size = far.shape[0] // 2
                far[part(m, size), lanes] = whole[at : at + size].astype(BF16)
                at += size


def plane_kernel(n_far, *refs):
    kvs, qgs, fars = refs[:PLANE], refs[PLANE : 2 * PLANE], refs[2 * PLANE : 2 * PLANE + n_far]
    refs = refs[2 * PLANE + n_far :]
    atts, grad_ref, prob_ref = refs[:PLANE], refs[PLANE], refs[PLANE + 1]
    ads, dkvs = refs[PLANE + 2 : 2 * PLANE + 2], refs[2 * PLANE + 2 :]
    rows, width = qgs[0].shape[0] // 2, qgs[0].shape[1]
    pair = 2 * rows
    near = pair + rows
    for r in range(PLANE):
        ads[r][:rows, :] = atts[r][...]
    for h in range(width // DH):
        lanes = part(h, DH)
        key_grads, value_grads = [], []
        for p in range(2):
            ours = (2 * p, 2 * p + 1)
            q = jnp.concatenate([qgs[r][:rows, lanes] for r in ours], 0)
            g = jnp.concatenate([qgs[r][rows:, lanes] for r in ours], 0)
            keys = key_sets(kvs, fars, p, lanes, 0)
            dq = (dot(keys, grad_ref[2 * h + p], 0, 0) * SCALE).astype(BF16).T
            for n, r in enumerate(ours):
                ads[r][rows:, lanes] = dq[part(n, rows)]
            key_grads.append(dot(grad_ref[2 * h + p, :near, :], q) * SCALE)
            value_grads.append(dot(prob_ref[2 * h + p, :near, :], g))
        for m, grads in enumerate((key_grads, value_grads)):
            for p in range(2):
                pooled = grads[1 - p][pair:]
                for n in range(2):
                    dkvs[2 * p + n][part(m, rows), lanes] = grads[p][part(n, rows)] + spread(
                        pooled[part(n, rows // 2)], 2
                    )


def carry_kernel(*refs):
    dkvs, (near_ref, far2_ref, far3_ref) = refs[:PLANE], refs[PLANE : PLANE + 3]
    extra, outs = refs[PLANE + 3 : -PLANE], refs[-PLANE:]
    rows, width = near_ref.shape[0] // 2, near_ref.shape[1]
    size = rows // PLANE
    wide = lambda block, size: jnp.concatenate(
        [block[part(n, size), :].astype(F32) for n in range(2 * PLANE)], 1
    )
    upper = far2_ref[...].astype(F32) + far3_ref[...].astype(F32)
    for ref in extra:
        upper = upper + ref[...].astype(F32)
    whole = wide(near_ref, size) + spread(wide(upper, size // 2), 2)
    carried = spread(whole, 4)
    for n in range(2 * PLANE):
        m, r = divmod(n, PLANE)
        outs[r][part(m, rows), :] = (
            dkvs[r][part(m, rows), :] + carried[:, part(n, width)]
        ).astype(BF16)


def output_kernel(*refs):
    ads, w_ref, own_out, others = refs[:PLANE], refs[PLANE], refs[PLANE + 1], refs[PLANE + 2 :]
    rows, width = ads[0].shape[0] // 2, ads[0].shape[1]
    half = own_out.shape[1]
    head = lax.axis_index("head")
    total = None
    for r in range(PLANE):
        term = dot(ads[r][:rows, :], w_ref[columns(r, width), :])
        total = term if total is None else total + term

    def write(own, other):
        own_out[...] = own
        for n, out in enumerate(others):
            out[...] = other[part(n, rows // PIECES)].astype(BF16)

    @pl.when(head == 0)
    def _():
        write(total[:, :half], total[:, half:])

    @pl.when(head == 1)
    def _():
        write(total[:, half:], total[:, :half])


def join_kernel(own_ref, *refs):
    others, refs = refs[:PIECES], refs[PIECES:]
    ads, dkvs = refs[:PLANE], refs[PLANE : 2 * PLANE]
    o_out, gq_out, gk_out, gv_out, total, sems = refs[2 * PLANE :]
    rows, width = ads[0].shape[0] // 2, ads[0].shape[1]
    pairs = []
    for r in range(PLANE):
        here = columns(r, width)
        pairs.append((ads[r].at[part(1, rows), :], gq_out.at[:, here]))
        pairs.append((dkvs[r].at[part(0, rows), :], gk_out.at[:, here]))
        pairs.append((dkvs[r].at[part(1, rows), :], gv_out.at[:, here]))
    copies = start_all(pairs, sems)
    for n, other in enumerate(others):
        piece = part(n, rows // PIECES)
        total[piece, :] = (own_ref[piece, :] + other[...].astype(F32)).astype(BF16)
    last = pltpu.make_async_copy(total, o_out, sems.at[len(pairs)])
    last.start()
    for copy in copies + [last]:
        copy.wait()


def plane_exchange(blocks):
    return [blocks[0]] + [xor_permute(blocks[r], r) for r in range(1, PLANE)]


def pool_both(block):
    shaped = block.reshape((2, block.shape[0] // 4, 2) + block.shape[1:]).astype(F32)
    return ((shaped[:, :, 0] + shaped[:, :, 1]) * 0.5).astype(BF16).reshape(
        (block.shape[0] // 2,) + block.shape[1:]
    )


def spread_both(block):
    halved = block.astype(F32) * 0.5
    return jnp.repeat(halved, 2, axis=0)


def join_both(blocks):
    halves = [b.reshape((2, b.shape[0] // 2) + b.shape[1:]) for b in blocks]
    joined = jnp.concatenate(halves, 1)
    return joined.reshape((-1,) + joined.shape[2:])


def part_both(block, parts):
    shaped = block.reshape((2, parts, block.shape[0] // (2 * parts)) + block.shape[1:])
    return [shaped[:, n].reshape((-1,) + block.shape[1:]) for n in range(parts)]


def body(queries, key_rows, value_rows, out_weight, cotangent):
    rows, features = queries.shape
    width = features // PLANE
    top_rounds = lax.axis_size("ctx").bit_length() - 1 - 4
    shape = lambda *dims, t=BF16: jax.ShapeDtypeStruct(dims, t)
    dma = lambda n: pltpu.SemaphoreType.DMA((n,))
    blocks = [shape(2 * rows, width)] * PLANE

    other_cotangent = xor_permute(cotangent, 1, "head")
    key_values = call(
        key_value_kernel, blocks, key_rows, value_rows,
        hbm=(0, 1), scratch=[dma(2 * PLANE)], name="pack_keys_values",
    )
    key_values = plane_exchange(key_values)
    *query_grads, weight = call(
        cotangent_kernel, blocks + [shape(*out_weight.shape)],
        queries, cotangent, other_cotangent, out_weight,
        hbm=(0, 1, 3), scratch=[pltpu.VMEM(cotangent.shape, BF16), dma(1 + PLANE), dma(PLANE)],
        cost_us=3.0, name="grad_attended",
    )
    query_grads = plane_exchange(query_grads)
    near, pooled = call(
        far_kernel, [shape(2 * rows, width), shape(rows, width)], *key_values,
        after=(query_grads[0],), name="pool_plane",
    )
    fars = [xor_permute(near, PLANE), xor_permute(pooled, 2 * PLANE), xor_permute(pooled, 3 * PLANE)]
    if top_rounds > 0:
        span = pool_both(join_both([pooled, pool_both(fars[0]), fars[1], fars[2]]))
        for n in range(top_rounds):
            fars.append(xor_permute(span, 4 * PLANE << n))
            span = pool_both(join_both([span, fars[-1]]))
    far_rows = sum(far.shape[0] for far in fars) // 2
    kept = shape(2 * width // DH, 3 * rows + far_rows, 2 * rows)
    results = call(
        lambda *refs: attention_kernel(len(fars), *refs),
        [shape(rows, width)] * PLANE + [kept, kept] + [shape(*far.shape) for far in fars],
        *key_values, *query_grads, *fars,
        cost_us=3.7, name="attention",
    )
    kept, far_grads = results[: PLANE + 2], list(results[PLANE + 2 :])
    results = call(
        lambda *refs: plane_kernel(len(fars), *refs),
        blocks + [shape(2 * rows, width, t=F32)] * PLANE,
        *key_values, *query_grads, *fars, *kept,
        cost_us=2.3, name="plane_grads",
    )
    att_dq, dkv = results[:PLANE], results[PLANE:]
    extra = []
    if top_rounds > 0:
        up = None
        for n in reversed(range(top_rounds)):
            send = far_grads[3 + n].astype(F32)
            if up is not None:
                own_up, their_up = part_both(spread_both(up), 2)
                send = send + their_up
            back = xor_permute(send.astype(BF16), 4 * PLANE << n).astype(F32)
            up = back if up is None else back + own_up
        ups = part_both(spread_both(up), PLANE)
        extra = [ups[0].astype(BF16)]
        far_grads[0] = (far_grads[0].astype(F32) + spread_both(ups[1])).astype(BF16)
        far_grads[1] = (far_grads[1].astype(F32) + ups[2]).astype(BF16)
        far_grads[2] = (far_grads[2].astype(F32) + ups[3]).astype(BF16)
    backs = [xor_permute(far_grads[n], (n + 1) * PLANE) for n in range(3)]
    att_dq = plane_exchange(att_dq)
    dkv = call(carry_kernel, blocks, *dkv, *backs, *extra, cost_us=5.0, name="carry")
    own_sum, *other_sum = call(
        output_kernel,
        [shape(rows, features, t=F32)] + [shape(rows // PIECES, features)] * PIECES,
        *att_dq, weight, after=(dkv[0],), cost_us=0.01, name="project",
    )
    dkv = plane_exchange(dkv)
    other_sum = [xor_permute(piece, 1, "head") for piece in other_sum]
    output, grad_queries, grad_keys, grad_values = call(
        join_kernel, [shape(rows, features)] * 4, own_sum, *other_sum, *att_dq, *dkv,
        hbm_out=True, scratch=[pltpu.VMEM((rows, features), BF16), dma(3 * PLANE + 1)],
        name="join",
    )
    return (output, grad_queries, grad_keys, grad_values)


def solution(mesh):
    rows = P("ctx", "head")
    return jax.shard_map(
        body,
        mesh=mesh,
        in_specs=(rows, rows, rows, P("head", None), rows),
        out_specs=(rows, rows, rows, rows),
        check_vma=False,
    )
```

```python
import jax
import jax.numpy as jnp
from jax import lax
from jax.experimental import pallas as pl
from jax.experimental.pallas import tpu as pltpu
from jax.sharding import PartitionSpec as P

DH = 128
PLANE = 4
PIECES = 2
SCALE = DH ** (-0.5)
SCALE2 = SCALE * 1.4426950408889634
BF16 = jnp.bfloat16
F32 = jnp.float32


def xor_permute(block, mask, axis="ctx"):
    count = lax.axis_size(axis)
    return lax.ppermute(block, axis, [(i, i ^ mask) for i in range(count)])


def dot(a, b, contract_a=1, contract_b=0):
    return lax.dot_general(
        a, b, (((contract_a,), (contract_b,)), ((), ())), preferred_element_type=F32
    )


def pool_matrix(rows):
    out = lax.broadcasted_iota(jnp.int32, (rows // 2, rows), 0)
    src = lax.broadcasted_iota(jnp.int32, (rows // 2, rows), 1)
    return jnp.where(src // 2 == out, 0.5, 0.0).astype(BF16)


def spread_matrix(rows, times):
    out = lax.broadcasted_iota(jnp.int32, (rows * times, rows), 0)
    src = lax.broadcasted_iota(jnp.int32, (rows * times, rows), 1)
    return jnp.where(out // times == src, 1.0 / times, 0.0).astype(BF16)


def pool(block):
    return dot(pool_matrix(block.shape[0]), block).astype(BF16)


def spread(block, times):
    return dot(spread_matrix(block.shape[0], times), block.astype(BF16))


def call(kernel, outs, *args, after=(), hbm=(), hbm_out=False, scratch=(), cost_us=1.0, name=None):
    vmem = pl.BlockSpec(memory_space=pltpu.VMEM)
    in_hbm = pl.BlockSpec(memory_space=pltpu.HBM)
    space = pltpu.HBM if hbm_out else pltpu.VMEM
    args = [
        pltpu.with_memory_space_constraint(a, pltpu.HBM) if n in hbm else a
        for n, a in enumerate(args)
    ]
    count = len(args)
    return pl.pallas_call(
        lambda *refs: kernel(*refs[:count], *refs[count + len(after) :]),
        out_shape=[space(out.shape, out.dtype) for out in outs],
        in_specs=[in_hbm if n in hbm else vmem for n in range(count)]
        + [pl.BlockSpec(memory_space=pl.ANY)] * len(after),
        scratch_shapes=scratch,
        out_specs=[in_hbm if hbm_out else vmem] * len(outs),
        compiler_params=pltpu.CompilerParams(vmem_limit_bytes=24 * 1024 * 1024),
        cost_estimate=pl.CostEstimate(
            flops=int(cost_us * 1e9), bytes_accessed=0, transcendentals=0
        ),
        name=name,
    )(*args, *after)


def part(n, width):
    return slice(n * width, (n + 1) * width)


def start_all(pairs, sems):
    copies = [pltpu.make_async_copy(a, b, sems.at[n]) for n, (a, b) in enumerate(pairs)]
    for copy in copies:
        copy.start()
    return copies


def columns(r, width):
    place = (lax.axis_index("ctx") & (PLANE - 1)) ^ r
    return pl.ds(pl.multiple_of(place * width, width), width)


def key_value_kernel(k_ref, v_ref, *refs):
    outs, sems = refs[:PLANE], refs[PLANE]
    rows, width = k_ref.shape[0], k_ref.shape[1] // PLANE
    pairs = []
    for r in range(PLANE):
        pairs.append((k_ref.at[:, columns(r, width)], outs[r].at[part(0, rows), :]))
        pairs.append((v_ref.at[:, columns(r, width)], outs[r].at[part(1, rows), :]))
    for copy in start_all(pairs, sems):
        copy.wait()


def cotangent_kernel(q_ref, own_ref, other_ref, w_ref, *refs):
    outs, own, sems = refs[:PLANE], *refs[PLANE:]
    rows, width = q_ref.shape[0], q_ref.shape[1] // PLANE
    half = own_ref.shape[1]
    head = lax.axis_index("head")
    own_at = pl.ds(pl.multiple_of(head * half, half), half)
    other_at = pl.ds(pl.multiple_of((1 - head) * half, half), half)
    here = [columns(r, width) for r in range(PLANE)]
    pairs = [(own_ref, own)]
    pairs += [(q_ref.at[:, here[r]], outs[r].at[part(0, rows), :]) for r in range(PLANE)]
    copies = start_all(pairs, sems)
    copies[0].wait()
    for r in range(PLANE):
        outs[r][rows:, :] = (
            dot(own[...], w_ref[here[r], own_at], 1, 1)
            + dot(other_ref[...], w_ref[here[r], other_at], 1, 1)
        ).astype(BF16)
    for copy in copies[1:]:
        copy.wait()


def far_kernel(*refs):
    kvs, (near_out, far_out) = refs[:PLANE], refs[PLANE:]
    rows, width = kvs[0].shape[0] // 2, kvs[0].shape[1]
    wide = jnp.concatenate([kv[part(m, rows), :] for m in range(2) for kv in kvs], 1)
    near = pool(pool(wide))
    far = pool(near)
    for out, pooled in ((near_out, near), (far_out, far)):
        size = pooled.shape[0]
        for n in range(2 * PLANE):
            out[part(n, size), :] = pooled[:, part(n, width)]


def both(blocks, p, rows, lanes):
    return jnp.concatenate([blocks[r][rows, lanes] for r in (2 * p, 2 * p + 1)], 0)


def near_set(kvs, p, lanes, m):
    rows = part(m, kvs[0].shape[0] // 2)
    other = [pool(kv[rows, lanes]) for kv in kvs[2 - 2 * p : 4 - 2 * p]]
    return jnp.concatenate([both(kvs, p, rows, lanes)] + other, 0)


def far_set(fars, lanes, m):
    return jnp.concatenate([far[part(m, far.shape[0] // 2), lanes] for far in fars], 0)


def near_kernel(*refs):
    kvs, qgs = refs[:PLANE], refs[PLANE : 2 * PLANE]
    weight_out, dots_out, sums_out, stats_out = refs[2 * PLANE :]
    rows, width = qgs[0].shape[0] // 2, qgs[0].shape[1]
    for h in range(width // DH):
        lanes = part(h, DH)
        for p in range(2):
            n = 2 * h + p
            q, g = both(qgs, p, part(0, rows), lanes), both(qgs, p, part(1, rows), lanes)
            values = near_set(kvs, p, lanes, 1)
            scores = dot(near_set(kvs, p, lanes, 0), q, 1, 1) * SCALE2
            row_max = jnp.max(scores, 0, keepdims=True)
            weights = jnp.exp2(scores - row_max)
            weight_out[n] = weights
            dots_out[n] = dot(values, g, 1, 1)
            sums_out[n] = dot(values, weights.astype(BF16), 0, 0)
            stats_out[n, 0:1, :] = row_max
            stats_out[n, 1:2, :] = jnp.sum(weights, 0, keepdims=True)


def far_grad_kernel(n_far, *refs):
    qgs, fars = refs[:PLANE], refs[PLANE : PLANE + n_far]
    sums_ref, stats_ref = refs[PLANE + n_far : PLANE + n_far + 2]
    outs = refs[PLANE + n_far + 2 :]
    atts, grad_out, stats_out, far_out = outs[:PLANE], outs[PLANE], outs[PLANE + 1], outs[PLANE + 2 :]
    rows, width = qgs[0].shape[0] // 2, qgs[0].shape[1]
    for h in range(width // DH):
        lanes = part(h, DH)
        keys, values = far_set(fars, lanes, 0), far_set(fars, lanes, 1)
        grads = []
        for p in range(2):
            n = 2 * h + p
            q, g = both(qgs, p, part(0, rows), lanes), both(qgs, p, part(1, rows), lanes)
            scores = dot(keys, q, 1, 1) * SCALE2
            near_max = stats_ref[n, 0:1, :]
            row_max = jnp.maximum(near_max, jnp.max(scores, 0, keepdims=True))
            weights = jnp.exp2(scores - row_max)
            near_part = jnp.exp2(near_max - row_max)
            inverse = 1.0 / (
                stats_ref[n, 1:2, :] * near_part + jnp.sum(weights, 0, keepdims=True)
            )
            numerator = sums_ref[n] * near_part + dot(values, weights.astype(BF16), 0, 0)
            attended = (numerator * inverse).astype(BF16)
            delta = jnp.sum(g.T.astype(F32) * attended.astype(F32), 0, keepdims=True)
            probabilities = weights * inverse
            score_grad = (probabilities * (dot(values, g, 1, 1) - delta)).astype(BF16)
            attended = attended.T
            for k in range(2):
                atts[2 * p + k][:, lanes] = attended[part(k, rows)]
            grad_out[n] = score_grad
            stats_out[n, 0:1, :] = near_part * inverse
            stats_out[n, 1:2, :] = delta
            grads.append((dot(score_grad, q) * SCALE, dot(probabilities.astype(BF16), g)))
        for m in range(2):
            whole, at = grads[0][m] + grads[1][m], 0
            for far in far_out:
                size = far.shape[0] // 2
                far[part(m, size), lanes] = whole[at : at + size].astype(BF16)
                at += size


def plane_kernel(n_far, *refs):
    kvs, qgs, fars = refs[:PLANE], refs[PLANE : 2 * PLANE], refs[2 * PLANE : 2 * PLANE + n_far]
    weight_ref, dots_ref = refs[2 * PLANE + n_far : 2 * PLANE + n_far + 2]
    refs = refs[2 * PLANE + n_far + 2 :]
    atts, grad_ref, stats_ref = refs[:PLANE], refs[PLANE], refs[PLANE + 1]
    ads, dkvs = refs[PLANE + 2 : 2 * PLANE + 2], refs[2 * PLANE + 2 :]
    rows, width = qgs[0].shape[0] // 2, qgs[0].shape[1]
    pair = 2 * rows
    for r in range(PLANE):
        ads[r][:rows, :] = atts[r][...]
    for h in range(width // DH):
        lanes = part(h, DH)
        far_keys = far_set(fars, lanes, 0)
        grads = []
        for p in range(2):
            n = 2 * h + p
            q, g = both(qgs, p, part(0, rows), lanes), both(qgs, p, part(1, rows), lanes)
            probabilities = weight_ref[n] * stats_ref[n, 0:1, :]
            score_grad = (probabilities * (dots_ref[n] - stats_ref[n, 1:2, :])).astype(BF16)
            dq = dot(near_set(kvs, p, lanes, 0), score_grad, 0, 0)
            dq = ((dq + dot(far_keys, grad_ref[n], 0, 0)) * SCALE).astype(BF16).T
            for k in range(2):
                ads[2 * p + k][rows:, lanes] = dq[part(k, rows)]
            grads.append((dot(score_grad, q) * SCALE, dot(probabilities.astype(BF16), g)))
        for m in range(2):
            for p in range(2):
                pooled = grads[1 - p][m][pair:]
                for k in range(2):
                    dkvs[2 * p + k][part(m, rows), lanes] = grads[p][m][part(k, rows)] + spread(
                        pooled[part(k, rows // 2)], 2
                    )


def carry_kernel(*refs):
    dkvs, (near_ref, far2_ref, far3_ref) = refs[:PLANE], refs[PLANE : PLANE + 3]
    extra, outs = refs[PLANE + 3 : -PLANE], refs[-PLANE:]
    rows, width = near_ref.shape[0] // 2, near_ref.shape[1]
    size = rows // PLANE
    wide = lambda block, size: jnp.concatenate(
        [block[part(n, size), :].astype(F32) for n in range(2 * PLANE)], 1
    )
    upper = far2_ref[...].astype(F32) + far3_ref[...].astype(F32)
    for ref in extra:
        upper = upper + ref[...].astype(F32)
    whole = wide(near_ref, size) + spread(wide(upper, size // 2), 2)
    carried = spread(whole, 4)
    for n in range(2 * PLANE):
        m, r = divmod(n, PLANE)
        outs[r][part(m, rows), :] = (
            dkvs[r][part(m, rows), :] + carried[:, part(n, width)]
        ).astype(BF16)


def output_kernel(*refs):
    ads, w_ref, own_out, others = refs[:PLANE], refs[PLANE], refs[PLANE + 1], refs[PLANE + 2 :]
    rows, width = ads[0].shape[0] // 2, ads[0].shape[1]
    half = own_out.shape[1]
    head = lax.axis_index("head")
    total = None
    for r in range(PLANE):
        term = dot(ads[r][:rows, :], w_ref[columns(r, width), :])
        total = term if total is None else total + term

    def write(own, other):
        own_out[...] = own
        for n, out in enumerate(others):
            out[...] = other[part(n, rows // PIECES)].astype(BF16)

    @pl.when(head == 0)
    def _():
        write(total[:, :half], total[:, half:])

    @pl.when(head == 1)
    def _():
        write(total[:, half:], total[:, :half])


def join_kernel(own_ref, *refs):
    others, refs = refs[:PIECES], refs[PIECES:]
    ads, dkvs = refs[:PLANE], refs[PLANE : 2 * PLANE]
    o_out, gq_out, gk_out, gv_out, total, sems = refs[2 * PLANE :]
    rows, width = ads[0].shape[0] // 2, ads[0].shape[1]
    pairs = []
    for r in range(PLANE):
        here = columns(r, width)
        pairs.append((ads[r].at[part(1, rows), :], gq_out.at[:, here]))
        pairs.append((dkvs[r].at[part(0, rows), :], gk_out.at[:, here]))
        pairs.append((dkvs[r].at[part(1, rows), :], gv_out.at[:, here]))
    copies = start_all(pairs, sems)
    for n, other in enumerate(others):
        piece = part(n, rows // PIECES)
        total[piece, :] = (own_ref[piece, :] + other[...].astype(F32)).astype(BF16)
    last = pltpu.make_async_copy(total, o_out, sems.at[len(pairs)])
    last.start()
    for copy in copies + [last]:
        copy.wait()


def plane_exchange(blocks):
    return [blocks[0]] + [xor_permute(blocks[r], r) for r in range(1, PLANE)]


def pool_both(block):
    shaped = block.reshape((2, block.shape[0] // 4, 2) + block.shape[1:]).astype(F32)
    return ((shaped[:, :, 0] + shaped[:, :, 1]) * 0.5).astype(BF16).reshape(
        (block.shape[0] // 2,) + block.shape[1:]
    )


def spread_both(block):
    halved = block.astype(F32) * 0.5
    return jnp.repeat(halved, 2, axis=0)


def join_both(blocks):
    halves = [b.reshape((2, b.shape[0] // 2) + b.shape[1:]) for b in blocks]
    joined = jnp.concatenate(halves, 1)
    return joined.reshape((-1,) + joined.shape[2:])


def part_both(block, parts):
    shaped = block.reshape((2, parts, block.shape[0] // (2 * parts)) + block.shape[1:])
    return [shaped[:, n].reshape((-1,) + block.shape[1:]) for n in range(parts)]


def body(queries, key_rows, value_rows, out_weight, cotangent):
    rows, features = queries.shape
    width = features // PLANE
    top_rounds = lax.axis_size("ctx").bit_length() - 1 - 4
    shape = lambda *dims, t=BF16: jax.ShapeDtypeStruct(dims, t)
    dma = lambda n: pltpu.SemaphoreType.DMA((n,))
    blocks = [shape(2 * rows, width)] * PLANE

    other_cotangent = xor_permute(cotangent, 1, "head")
    key_values = call(
        key_value_kernel, blocks, key_rows, value_rows,
        hbm=(0, 1), scratch=[dma(2 * PLANE)], cost_us=8, name="pack_keys_values",
    )
    key_values = plane_exchange(key_values)
    query_grads = call(
        cotangent_kernel, blocks, queries, cotangent, other_cotangent, out_weight,
        hbm=(0, 1), scratch=[pltpu.VMEM(cotangent.shape, BF16), dma(1 + PLANE)],
        cost_us=3.0, name="grad_attended",
    )
    query_grads = plane_exchange(query_grads)
    near, pooled = call(
        far_kernel, [shape(2 * rows, width), shape(rows, width)], *key_values,
        after=(query_grads[0],), name="pool_plane",
    )
    fars = [xor_permute(near, PLANE), xor_permute(pooled, 2 * PLANE), xor_permute(pooled, 3 * PLANE)]
    if top_rounds > 0:
        span = pool_both(join_both([pooled, pool_both(fars[0]), fars[1], fars[2]]))
        for n in range(top_rounds):
            fars.append(xor_permute(span, 4 * PLANE << n))
            span = pool_both(join_both([span, fars[-1]]))
    far_rows = sum(far.shape[0] for far in fars) // 2
    cases = 2 * width // DH
    weights, dots, sums, stats = call(
        near_kernel,
        [shape(cases, 3 * rows, 2 * rows, t=F32)] * 2
        + [shape(cases, DH, 2 * rows, t=F32), shape(cases, 2, 2 * rows, t=F32)],
        *key_values, *query_grads, cost_us=2.0, name="near_attention",
    )
    results = call(
        lambda *refs: far_grad_kernel(len(fars), *refs),
        [shape(rows, width)] * PLANE
        + [shape(cases, far_rows, 2 * rows), shape(cases, 2, 2 * rows, t=F32)]
        + [shape(*far.shape) for far in fars],
        *query_grads, *fars, sums, stats, cost_us=2.0, name="far_attention",
    )
    kept, far_grads = results[: PLANE + 2], list(results[PLANE + 2 :])
    results = call(
        lambda *refs: plane_kernel(len(fars), *refs),
        blocks + [shape(2 * rows, width, t=F32)] * PLANE,
        *key_values, *query_grads, *fars, weights, dots, *kept,
        cost_us=2.3, name="plane_grads",
    )
    att_dq, dkv = results[:PLANE], results[PLANE:]
    extra = []
    if top_rounds > 0:
        up = None
        for n in reversed(range(top_rounds)):
            send = far_grads[3 + n].astype(F32)
            if up is not None:
                own_up, their_up = part_both(spread_both(up), 2)
                send = send + their_up
            back = xor_permute(send.astype(BF16), 4 * PLANE << n).astype(F32)
            up = back if up is None else back + own_up
        ups = part_both(spread_both(up), PLANE)
        extra = [ups[0].astype(BF16)]
        far_grads[0] = (far_grads[0].astype(F32) + spread_both(ups[1])).astype(BF16)
        far_grads[1] = (far_grads[1].astype(F32) + ups[2]).astype(BF16)
        far_grads[2] = (far_grads[2].astype(F32) + ups[3]).astype(BF16)
    backs = [xor_permute(far_grads[n], (n + 1) * PLANE) for n in range(3)]
    att_dq = plane_exchange(att_dq)
    dkv = call(carry_kernel, blocks, *dkv, *backs, *extra, cost_us=5.0, name="carry")
    own_sum, *other_sum = call(
        output_kernel,
        [shape(rows, features, t=F32)] + [shape(rows // PIECES, features)] * PIECES,
        *att_dq, out_weight, after=(dkv[0],), cost_us=0.01, name="project",
    )
    dkv = plane_exchange(dkv)
    other_sum = [xor_permute(piece, 1, "head") for piece in other_sum]
    output, grad_queries, grad_keys, grad_values = call(
        join_kernel, [shape(rows, features)] * 4, own_sum, *other_sum, *att_dq, *dkv,
        hbm_out=True, scratch=[pltpu.VMEM((rows, features), BF16), dma(3 * PLANE + 1)],
        name="join",
    )
    return (output, grad_queries, grad_keys, grad_values)


def solution(mesh):
    rows = P("ctx", "head")
    return jax.shard_map(
        body,
        mesh=mesh,
        in_specs=(rows, rows, rows, P("head", None), rows),
        out_specs=(rows, rows, rows, rows),
        check_vma=False,
    )
```

```python
import jax
import jax.numpy as jnp
from jax import lax
from jax.experimental import pallas as pl
from jax.experimental.pallas import tpu as pltpu
from jax.sharding import PartitionSpec as P

DH = 128
PLANE = 4
PIECES = 2
SCALE = DH ** (-0.5)
SCALE2 = SCALE * 1.4426950408889634
BF16 = jnp.bfloat16
F32 = jnp.float32


def xor_permute(block, mask, axis="ctx"):
    count = lax.axis_size(axis)
    return lax.ppermute(block, axis, [(i, i ^ mask) for i in range(count)])


def dot(a, b, contract_a=1, contract_b=0):
    return lax.dot_general(
        a, b, (((contract_a,), (contract_b,)), ((), ())), preferred_element_type=F32
    )


def pool_matrix(rows):
    out = lax.broadcasted_iota(jnp.int32, (rows // 2, rows), 0)
    src = lax.broadcasted_iota(jnp.int32, (rows // 2, rows), 1)
    return jnp.where(src // 2 == out, 0.5, 0.0).astype(BF16)


def spread_matrix(rows, times):
    out = lax.broadcasted_iota(jnp.int32, (rows * times, rows), 0)
    src = lax.broadcasted_iota(jnp.int32, (rows * times, rows), 1)
    return jnp.where(out // times == src, 1.0 / times, 0.0).astype(BF16)


def pool(block):
    return dot(pool_matrix(block.shape[0]), block).astype(BF16)


def spread(block, times):
    return dot(spread_matrix(block.shape[0], times), block.astype(BF16))


def call(kernel, outs, *args, after=(), aliases={}, hbm=(), hbm_out=False, scratch=(), cost_us=1.0, name=None):
    vmem = pl.BlockSpec(memory_space=pltpu.VMEM)
    in_hbm = pl.BlockSpec(memory_space=pltpu.HBM)
    space = pltpu.HBM if hbm_out else pltpu.VMEM
    args = [
        pltpu.with_memory_space_constraint(a, pltpu.HBM) if n in hbm else a
        for n, a in enumerate(args)
    ]
    count = len(args)
    return pl.pallas_call(
        lambda *refs: kernel(*refs[:count], *refs[count + len(after) :]),
        out_shape=[space(out.shape, out.dtype) for out in outs],
        in_specs=[in_hbm if n in hbm else vmem for n in range(count)]
        + [pl.BlockSpec(memory_space=pl.ANY)] * len(after),
        scratch_shapes=scratch,
        input_output_aliases=aliases,
        out_specs=[in_hbm if hbm_out else vmem] * len(outs),
        compiler_params=pltpu.CompilerParams(vmem_limit_bytes=24 * 1024 * 1024),
        cost_estimate=pl.CostEstimate(
            flops=int(cost_us * 1e9), bytes_accessed=0, transcendentals=0
        ),
        name=name,
    )(*args, *after)


def part(n, width):
    return slice(n * width, (n + 1) * width)


def start_all(pairs, sems):
    copies = [pltpu.make_async_copy(a, b, sems.at[n]) for n, (a, b) in enumerate(pairs)]
    for copy in copies:
        copy.start()
    return copies


def columns(r, width):
    place = (lax.axis_index("ctx") & (PLANE - 1)) ^ r
    return pl.ds(pl.multiple_of(place * width, width), width)


def key_value_kernel(k_ref, v_ref, *refs):
    outs, sems = refs[:PLANE], refs[PLANE]
    rows, width = k_ref.shape[0], k_ref.shape[1] // PLANE
    pairs = []
    for r in range(PLANE):
        pairs.append((k_ref.at[:, columns(r, width)], outs[r].at[part(0, rows), :]))
        pairs.append((v_ref.at[:, columns(r, width)], outs[r].at[part(1, rows), :]))
    for copy in start_all(pairs, sems):
        copy.wait()


def cotangent_kernel(q_ref, own_ref, other_ref, w_ref, *refs):
    outs, own, sems = refs[:PLANE], *refs[PLANE:]
    rows, width = q_ref.shape[0], q_ref.shape[1] // PLANE
    half = own_ref.shape[1]
    head = lax.axis_index("head")
    own_at = pl.ds(pl.multiple_of(head * half, half), half)
    other_at = pl.ds(pl.multiple_of((1 - head) * half, half), half)
    here = [columns(r, width) for r in range(PLANE)]
    pairs = [(own_ref, own)]
    pairs += [(q_ref.at[:, here[r]], outs[r].at[part(0, rows), :]) for r in range(PLANE)]
    copies = start_all(pairs, sems)
    copies[0].wait()
    for r in range(PLANE):
        outs[r][rows:, :] = (
            dot(own[...], w_ref[here[r], own_at], 1, 1)
            + dot(other_ref[...], w_ref[here[r], other_at], 1, 1)
        ).astype(BF16)
    for copy in copies[1:]:
        copy.wait()


def far_kernel(*refs):
    kvs, (near_out, far_out) = refs[:PLANE], refs[PLANE:]
    rows, width = kvs[0].shape[0] // 2, kvs[0].shape[1]
    wide = jnp.concatenate([kv[part(m, rows), :] for m in range(2) for kv in kvs], 1)
    near = pool(pool(wide))
    far = pool(near)
    for out, pooled in ((near_out, near), (far_out, far)):
        size = pooled.shape[0]
        for n in range(2 * PLANE):
            out[part(n, size), :] = pooled[:, part(n, width)]


def both(blocks, p, rows, lanes):
    return jnp.concatenate([blocks[r][rows, lanes] for r in (2 * p, 2 * p + 1)], 0)


def near_set(kvs, p, lanes, m):
    rows = part(m, kvs[0].shape[0] // 2)
    other = [pool(kv[rows, lanes]) for kv in kvs[2 - 2 * p : 4 - 2 * p]]
    return jnp.concatenate([both(kvs, p, rows, lanes)] + other, 0)


def far_set(fars, lanes, m):
    return jnp.concatenate([far[part(m, far.shape[0] // 2), lanes] for far in fars], 0)


def token_rows(qgs, m, lanes):
    rows = part(m, qgs[0].shape[0] // 2)
    return jnp.concatenate([qg[rows, lanes] for qg in qgs], 0)


def near_kernel(*refs):
    kvs, qgs, level3 = refs[:PLANE], refs[PLANE : 2 * PLANE], refs[2 * PLANE]
    weight_out, dots_out, sums_out, stats_out, keys_out = refs[2 * PLANE + 1 :]
    rows, width = qgs[0].shape[0] // 2, qgs[0].shape[1]
    cases = [(h, p) for h in range(width // DH) for p in range(2)]
    tokens = [part(p, 2 * rows) for h, p in cases]
    keys, values = [
        [
            jnp.concatenate(
                [near_set(kvs, p, part(h, DH), m), level3[part(m, rows), part(h, DH)]], 0
            )
            for h, p in cases
        ]
        for m in range(2)
    ]
    scores = [
        dot(k, both(qgs, p, part(0, rows), part(h, DH)), 1, 1) * SCALE2
        for k, (h, p) in zip(keys, cases)
    ]
    for (h, p), v, t in zip(cases, values, tokens):
        dots_out[h, :, t] = dot(v, both(qgs, p, part(1, rows), part(h, DH)), 1, 1)
    for n, ((h, p), t) in enumerate(zip(cases, tokens)):
        row_max = jnp.max(scores[n], 0, keepdims=True)
        weights = jnp.exp2(scores[n] - row_max)
        weight_out[h, :, t] = weights
        sums_out[h, :, t] = dot(values[n], weights.astype(BF16), 0, 0)
        stats_out[h, 0:1, t] = row_max
        stats_out[h, 1:2, t] = jnp.sum(weights, 0, keepdims=True)
        keys_out[n] = keys[n]


def far_grad_kernel(n_far, *refs):
    qgs, fars = refs[:PLANE], refs[PLANE : PLANE + n_far]
    weight_ref, dots_ref, sums_ref, stats_ref = refs[PLANE + n_far : PLANE + n_far + 4]
    outs = refs[PLANE + n_far + 4 :]
    ads, grad_out, stats_out, far_out = outs[:PLANE], outs[PLANE], outs[PLANE + 1], outs[PLANE + 2 :]
    rows, width = qgs[0].shape[0] // 2, qgs[0].shape[1]
    level3 = slice(3 * rows, 4 * rows)
    heads = range(width // DH)
    lanes = [part(h, DH) for h in heads]
    queries = [token_rows(qgs, 0, at) for at in lanes]
    grads = [token_rows(qgs, 1, at) for at in lanes]
    keys = [far_set(fars, at, 0) for at in lanes]
    values = [far_set(fars, at, 1) for at in lanes]
    scores = [dot(k, q, 1, 1) * SCALE2 for k, q in zip(keys, queries)]
    dots = [dot(v, g, 1, 1) for v, g in zip(values, grads)]
    weights, near_parts, inverses, sums = [], [], [], []
    for h in heads:
        near_max = stats_ref[h, 0:1, :]
        row_max = jnp.maximum(near_max, jnp.max(scores[h], 0, keepdims=True))
        weights.append(jnp.exp2(scores[h] - row_max))
        near_parts.append(jnp.exp2(near_max - row_max))
        sums.append(dot(values[h], weights[h].astype(BF16), 0, 0))
        inverses.append(
            1.0 / (stats_ref[h, 1:2, :] * near_parts[h] + jnp.sum(weights[h], 0, keepdims=True))
        )
    score_grads, probs = [], []
    for h in heads:
        attended = ((sums_ref[h] * near_parts[h] + sums[h]) * inverses[h]).astype(BF16)
        delta = jnp.sum(grads[h].T.astype(F32) * attended.astype(F32), 0, keepdims=True)
        near_scale = near_parts[h] * inverses[h]
        near_probs = weight_ref[h, level3, :] * near_scale
        far_probs = weights[h] * inverses[h]
        score_grads.append(
            jnp.concatenate(
                [
                    (near_probs * (dots_ref[h, level3, :] - delta)).astype(BF16),
                    (far_probs * (dots[h] - delta)).astype(BF16),
                ],
                0,
            )
        )
        probs.append(jnp.concatenate([near_probs.astype(BF16), far_probs.astype(BF16)], 0))
        grad_out[h] = score_grads[h][rows:]
        stats_out[h, 0:1, :] = near_scale
        stats_out[h, 1:2, :] = delta
        attended = attended.T
        for r in range(PLANE):
            ads[r][:rows, lanes[h]] = attended[part(r, rows)]
    for h in heads:
        for m, whole in enumerate(
            (dot(score_grads[h], queries[h]) * SCALE, dot(probs[h], grads[h]))
        ):
            at = 0
            for far in far_out:
                size = far.shape[0] // 2
                far[part(m, size), lanes[h]] = whole[at : at + size].astype(BF16)
                at += size


def plane_kernel(n_far, *refs):
    qgs, fars = refs[:PLANE], refs[PLANE : PLANE + n_far]
    keys_ref, weight_ref, dots_ref, grad_ref, stats_ref = refs[PLANE + n_far : PLANE + n_far + 5]
    refs = refs[2 * PLANE + n_far + 5 :]
    ads, dkvs = refs[:PLANE], refs[PLANE:]
    rows, width = qgs[0].shape[0] // 2, qgs[0].shape[1]
    pair = 2 * rows
    cases = [(h, p) for h in range(width // DH) for p in range(2)]
    score_grads, probs = [], []
    for h, p in cases:
        tokens = part(p, pair)
        probabilities = weight_ref[h, :, tokens] * stats_ref[h, 0:1, tokens]
        probs.append(probabilities.astype(BF16))
        score_grads.append(
            (probabilities * (dots_ref[h, :, tokens] - stats_ref[h, 1:2, tokens])).astype(BF16)
        )
    for n, (h, p) in enumerate(cases):
        far_keys = far_set(fars, part(h, DH), 0)
        dq = dot(keys_ref[n], score_grads[n], 0, 0)
        dq = dq + dot(far_keys, grad_ref[h, :, part(p, pair)], 0, 0)
        dq = (dq * SCALE).astype(BF16).T
        for k in range(2):
            ads[2 * p + k][rows:, part(h, DH)] = dq[part(k, rows)]
    grads = []
    for n, (h, p) in enumerate(cases):
        q, g = [both(qgs, p, part(m, rows), part(h, DH)) for m in range(2)]
        near = slice(0, 3 * rows)
        grads.append((dot(score_grads[n][near], q) * SCALE, dot(probs[n][near], g)))
    for h in range(width // DH):
        for m in range(2):
            for p in range(2):
                pooled = grads[2 * h + 1 - p][m][pair:]
                for k in range(2):
                    dkvs[2 * p + k][part(m, rows), part(h, DH)] = grads[2 * h + p][m][
                        part(k, rows)
                    ] + spread(pooled[part(k, rows // 2)], 2)


def carry_kernel(*refs):
    dkvs, (near_ref, far2_ref, far3_ref) = refs[:PLANE], refs[PLANE : PLANE + 3]
    extra, outs = refs[PLANE + 3 : -PLANE], refs[-PLANE:]
    rows, width = near_ref.shape[0] // 2, near_ref.shape[1]
    size = rows // PLANE
    wide = lambda block, size: jnp.concatenate(
        [block[part(n, size), :].astype(F32) for n in range(2 * PLANE)], 1
    )
    upper = far2_ref[...].astype(F32) + far3_ref[...].astype(F32)
    for ref in extra:
        upper = upper + ref[...].astype(F32)
    whole = wide(near_ref, size) + spread(wide(upper, size // 2), 2)
    carried = spread(whole, 4)
    for n in range(2 * PLANE):
        m, r = divmod(n, PLANE)
        outs[r][part(m, rows), :] = (
            dkvs[r][part(m, rows), :] + carried[:, part(n, width)]
        ).astype(BF16)


def output_kernel(*refs):
    ads, w_ref, own_out, others = refs[:PLANE], refs[PLANE], refs[PLANE + 1], refs[PLANE + 2 :]
    rows, width = ads[0].shape[0] // 2, ads[0].shape[1]
    half = own_out.shape[1]
    head = lax.axis_index("head")
    total = None
    for r in range(PLANE):
        term = dot(ads[r][:rows, :], w_ref[columns(r, width), :])
        total = term if total is None else total + term

    def write(own, other):
        own_out[...] = own
        for n, out in enumerate(others):
            out[...] = other[part(n, rows // PIECES)].astype(BF16)

    @pl.when(head == 0)
    def _():
        write(total[:, :half], total[:, half:])

    @pl.when(head == 1)
    def _():
        write(total[:, half:], total[:, :half])


def join_kernel(own_ref, *refs):
    others, refs = refs[:PIECES], refs[PIECES:]
    ads, dkvs = refs[:PLANE], refs[PLANE : 2 * PLANE]
    o_out, gq_out, gk_out, gv_out, total, sems = refs[2 * PLANE :]
    rows, width = ads[0].shape[0] // 2, ads[0].shape[1]
    pairs = []
    for r in range(PLANE):
        here = columns(r, width)
        pairs.append((dkvs[r].at[part(0, rows), :], gk_out.at[:, here]))
        pairs.append((dkvs[r].at[part(1, rows), :], gv_out.at[:, here]))
        pairs.append((ads[r].at[part(1, rows), :], gq_out.at[:, here]))
    copies = start_all(pairs, sems)
    for n, other in enumerate(others):
        piece = part(n, rows // PIECES)
        total[piece, :] = (own_ref[piece, :] + other[...].astype(F32)).astype(BF16)
    last = pltpu.make_async_copy(total, o_out, sems.at[len(pairs)])
    last.start()
    for copy in copies + [last]:
        copy.wait()


def plane_exchange(blocks):
    return [blocks[0]] + [xor_permute(blocks[r], r) for r in range(1, PLANE)]


def pool_both(block):
    shaped = block.reshape((2, block.shape[0] // 4, 2) + block.shape[1:]).astype(F32)
    return ((shaped[:, :, 0] + shaped[:, :, 1]) * 0.5).astype(BF16).reshape(
        (block.shape[0] // 2,) + block.shape[1:]
    )


def spread_both(block):
    halved = block.astype(F32) * 0.5
    return jnp.repeat(halved, 2, axis=0)


def join_both(blocks):
    halves = [b.reshape((2, b.shape[0] // 2) + b.shape[1:]) for b in blocks]
    joined = jnp.concatenate(halves, 1)
    return joined.reshape((-1,) + joined.shape[2:])


def part_both(block, parts):
    shaped = block.reshape((2, parts, block.shape[0] // (2 * parts)) + block.shape[1:])
    return [shaped[:, n].reshape((-1,) + block.shape[1:]) for n in range(parts)]


def body(queries, key_rows, value_rows, out_weight, cotangent):
    rows, features = queries.shape
    width = features // PLANE
    top_rounds = lax.axis_size("ctx").bit_length() - 1 - 4
    shape = lambda *dims, t=BF16: jax.ShapeDtypeStruct(dims, t)
    dma = lambda n: pltpu.SemaphoreType.DMA((n,))
    blocks = [shape(2 * rows, width)] * PLANE

    other_cotangent = xor_permute(cotangent, 1, "head")
    key_values = call(
        key_value_kernel, blocks, key_rows, value_rows,
        hbm=(0, 1), scratch=[dma(2 * PLANE)], cost_us=8, name="pack_keys_values",
    )
    key_values = plane_exchange(key_values)
    query_grads = call(
        cotangent_kernel, blocks, queries, cotangent, other_cotangent, out_weight,
        hbm=(0, 1), scratch=[pltpu.VMEM(cotangent.shape, BF16), dma(1 + PLANE)],
        cost_us=3.0, name="grad_attended",
    )
    query_grads = plane_exchange(query_grads)
    near, pooled = call(
        far_kernel, [shape(2 * rows, width), shape(rows, width)], *key_values,
        after=(query_grads[0],), name="pool_plane",
    )
    fars = [xor_permute(near, PLANE), xor_permute(pooled, 2 * PLANE), xor_permute(pooled, 3 * PLANE)]
    if top_rounds > 0:
        span = pool_both(join_both([pooled, pool_both(fars[0]), fars[1], fars[2]]))
        for n in range(top_rounds):
            fars.append(xor_permute(span, 4 * PLANE << n))
            span = pool_both(join_both([span, fars[-1]]))
    far_rows = sum(far.shape[0] for far in fars[1:]) // 2
    heads, tokens = width // DH, PLANE * rows
    weights, dots, sums, stats, near_keys = call(
        near_kernel,
        [shape(heads, 4 * rows, tokens, t=F32)] * 2
        + [shape(heads, DH, tokens, t=F32), shape(heads, 2, tokens, t=F32)]
        + [shape(2 * heads, 4 * rows, DH)],
        *key_values, *query_grads, fars[0], cost_us=2.0, name="near_attention",
    )
    results = call(
        lambda *refs: far_grad_kernel(len(fars) - 1, *refs),
        blocks + [shape(heads, far_rows, tokens), shape(heads, 2, tokens, t=F32)]
        + [shape(*far.shape) for far in fars],
        *query_grads, *fars[1:], weights, dots, sums, stats, cost_us=2.0, name="far_attention",
    )
    ads, kept, far_grads = results[:PLANE], results[PLANE : PLANE + 2], list(results[PLANE + 2 :])
    first = PLANE + len(fars) + 4
    results = call(
        lambda *refs: plane_kernel(len(fars) - 1, *refs),
        blocks + [shape(2 * rows, width, t=F32)] * PLANE,
        *query_grads, *fars[1:], near_keys, weights, dots, *kept, *ads,
        aliases={first + r: r for r in range(PLANE)}, cost_us=2.3, name="plane_grads",
    )
    att_dq, dkv = results[:PLANE], results[PLANE:]
    extra = []
    if top_rounds > 0:
        up = None
        for n in reversed(range(top_rounds)):
            send = far_grads[3 + n].astype(F32)
            if up is not None:
                own_up, their_up = part_both(spread_both(up), 2)
                send = send + their_up
            back = xor_permute(send.astype(BF16), 4 * PLANE << n).astype(F32)
            up = back if up is None else back + own_up
        ups = part_both(spread_both(up), PLANE)
        extra = [ups[0].astype(BF16)]
        far_grads[0] = (far_grads[0].astype(F32) + spread_both(ups[1])).astype(BF16)
        far_grads[1] = (far_grads[1].astype(F32) + ups[2]).astype(BF16)
        far_grads[2] = (far_grads[2].astype(F32) + ups[3]).astype(BF16)
    backs = [xor_permute(far_grads[n], (n + 1) * PLANE) for n in range(3)]
    att_dq = plane_exchange(att_dq)
    dkv = call(carry_kernel, blocks, *dkv, *backs, *extra, cost_us=5.0, name="carry")
    own_sum, *other_sum = call(
        output_kernel,
        [shape(rows, features, t=F32)] + [shape(rows // PIECES, features)] * PIECES,
        *att_dq, out_weight, after=(dkv[0],), cost_us=0.01, name="project",
    )
    dkv = plane_exchange(dkv)
    other_sum = [xor_permute(piece, 1, "head") for piece in other_sum]
    output, grad_queries, grad_keys, grad_values = call(
        join_kernel, [shape(rows, features)] * 4, own_sum, *other_sum, *att_dq, *dkv,
        hbm_out=True, scratch=[pltpu.VMEM((rows, features), BF16), dma(3 * PLANE + 1)],
        name="join",
    )
    return (output, grad_queries, grad_keys, grad_values)


def solution(mesh):
    rows = P("ctx", "head")
    return jax.shard_map(
        body,
        mesh=mesh,
        in_specs=(rows, rows, rows, P("head", None), rows),
        out_specs=(rows, rows, rows, rows),
        check_vma=False,
    )
```

```python
import jax
import jax.numpy as jnp
from jax import lax
from jax.experimental import pallas as pl
from jax.experimental.pallas import tpu as pltpu
from jax.sharding import PartitionSpec as P

DH = 128
PLANE = 4
PIECES = 2
ORDER = (1, 2, 3)
SCALE = DH ** (-0.5)
SCALE2 = SCALE * 1.4426950408889634
BF16 = jnp.bfloat16
F32 = jnp.float32


def xor_permute(block, mask, axis="ctx"):
    count = lax.axis_size(axis)
    return lax.ppermute(block, axis, [(i, i ^ mask) for i in range(count)])


def dot(a, b, contract_a=1, contract_b=0):
    return lax.dot_general(
        a, b, (((contract_a,), (contract_b,)), ((), ())), preferred_element_type=F32
    )


def pool_matrix(rows):
    out = lax.broadcasted_iota(jnp.int32, (rows // 2, rows), 0)
    src = lax.broadcasted_iota(jnp.int32, (rows // 2, rows), 1)
    return jnp.where(src // 2 == out, 0.5, 0.0).astype(BF16)


def spread_matrix(rows, times):
    out = lax.broadcasted_iota(jnp.int32, (rows * times, rows), 0)
    src = lax.broadcasted_iota(jnp.int32, (rows * times, rows), 1)
    return jnp.where(out // times == src, 1.0 / times, 0.0).astype(BF16)


def pool(block):
    return dot(pool_matrix(block.shape[0]), block).astype(BF16)


def spread(block, times):
    return dot(spread_matrix(block.shape[0], times), block.astype(BF16))


def call(kernel, outs, *args, after=(), aliases={}, hbm=(), hbm_out=False, scratch=(), cost_us=1.0, name=None):
    vmem = pl.BlockSpec(memory_space=pltpu.VMEM)
    in_hbm = pl.BlockSpec(memory_space=pltpu.HBM)
    space = pltpu.HBM if hbm_out else pltpu.VMEM
    args = [
        pltpu.with_memory_space_constraint(a, pltpu.HBM) if n in hbm else a
        for n, a in enumerate(args)
    ]
    count = len(args)
    return pl.pallas_call(
        lambda *refs: kernel(*refs[:count], *refs[count + len(after) :]),
        out_shape=[space(out.shape, out.dtype) for out in outs],
        in_specs=[in_hbm if n in hbm else vmem for n in range(count)]
        + [pl.BlockSpec(memory_space=pl.ANY)] * len(after),
        scratch_shapes=scratch,
        input_output_aliases=aliases,
        out_specs=[in_hbm if hbm_out else vmem] * len(outs),
        compiler_params=pltpu.CompilerParams(vmem_limit_bytes=24 * 1024 * 1024),
        cost_estimate=pl.CostEstimate(
            flops=int(cost_us * 1e9), bytes_accessed=0, transcendentals=0
        ),
        name=name,
    )(*args, *after)


def part(n, width):
    return slice(n * width, (n + 1) * width)


def start_all(pairs, sems):
    copies = [pltpu.make_async_copy(a, b, sems.at[n]) for n, (a, b) in enumerate(pairs)]
    for copy in copies:
        copy.start()
    return copies


def columns(r, width):
    place = (lax.axis_index("ctx") & (PLANE - 1)) ^ r
    return pl.ds(pl.multiple_of(place * width, width), width)


def key_value_kernel(k_ref, v_ref, *refs):
    outs, sems = refs[:PLANE], refs[PLANE]
    rows, width = k_ref.shape[0], k_ref.shape[1] // PLANE
    pairs = []
    for r in range(PLANE):
        pairs.append((k_ref.at[:, columns(r, width)], outs[r].at[part(0, rows), :]))
        pairs.append((v_ref.at[:, columns(r, width)], outs[r].at[part(1, rows), :]))
    for copy in start_all(pairs, sems):
        copy.wait()


def cotangent_kernel(q_ref, own_ref, other_ref, w_ref, *refs):
    outs, own, sems = refs[:PLANE], *refs[PLANE:]
    rows, width = q_ref.shape[0], q_ref.shape[1] // PLANE
    half = own_ref.shape[1]
    head = lax.axis_index("head")
    own_at = pl.ds(pl.multiple_of(head * half, half), half)
    other_at = pl.ds(pl.multiple_of((1 - head) * half, half), half)
    here = [columns(r, width) for r in range(PLANE)]
    pairs = [(own_ref, own)]
    pairs += [(q_ref.at[:, here[r]], outs[r].at[part(0, rows), :]) for r in range(PLANE)]
    copies = start_all(pairs, sems)
    copies[0].wait()
    for r in range(PLANE):
        outs[r][rows:, :] = (
            dot(own[...], w_ref[here[r], own_at], 1, 1)
            + dot(other_ref[...], w_ref[here[r], other_at], 1, 1)
        ).astype(BF16)
    for copy in copies[1:]:
        copy.wait()


def average_matrix(rows, times):
    out = lax.broadcasted_iota(jnp.int32, (rows // times, rows), 0)
    src = lax.broadcasted_iota(jnp.int32, (rows // times, rows), 1)
    return jnp.where(src // times == out, 1.0 / times, 0.0).astype(BF16)


def far_kernel(*refs):
    kvs, outs = refs[:PLANE], refs[PLANE:]
    rows, width = kvs[0].shape[0] // 2, kvs[0].shape[1]
    wide = jnp.concatenate([kv[part(m, rows), :] for m in range(2) for kv in kvs], 1)
    pooled = dot(
        jnp.concatenate([average_matrix(rows, 4), average_matrix(rows, 8)], 0), wide
    ).astype(BF16)
    for out, first, size in zip(outs, (0, rows // 4), (rows // 4, rows // 8)):
        for n in range(2 * PLANE):
            out[part(n, size), :] = pooled[first : first + size, part(n, width)]


def both(blocks, p, rows, lanes):
    return jnp.concatenate([blocks[r][rows, lanes] for r in (2 * p, 2 * p + 1)], 0)


def near_set(kvs, p, lanes, m):
    rows = part(m, kvs[0].shape[0] // 2)
    other = [pool(kv[rows, lanes]) for kv in kvs[2 - 2 * p : 4 - 2 * p]]
    return jnp.concatenate([both(kvs, p, rows, lanes)] + other, 0)


def far_set(fars, lanes, m):
    return jnp.concatenate([far[part(m, far.shape[0] // 2), lanes] for far in fars], 0)


def token_rows(qgs, m, lanes):
    rows = part(m, qgs[0].shape[0] // 2)
    return jnp.concatenate([qg[rows, lanes] for qg in qgs], 0)


def near_kernel(*refs):
    kvs, qgs, first = refs[:PLANE], refs[PLANE : 2 * PLANE], refs[2 * PLANE]
    weight_out, dots_out, sums_out, stats_out, keys_out = refs[2 * PLANE + 1 :]
    rows, width = qgs[0].shape[0] // 2, qgs[0].shape[1]
    cases = [(h, p) for h in range(width // DH) for p in range(2)]
    tokens = [part(p, 2 * rows) for h, p in cases]
    keys, values = [
        [
            jnp.concatenate(
                [near_set(kvs, p, part(h, DH), m), first[part(m, first.shape[0] // 2), part(h, DH)]], 0
            )
            for h, p in cases
        ]
        for m in range(2)
    ]
    scores = [
        dot(k, both(qgs, p, part(0, rows), part(h, DH)), 1, 1) * SCALE2
        for k, (h, p) in zip(keys, cases)
    ]
    for (h, p), v, t in zip(cases, values, tokens):
        dots_out[h, :, t] = dot(v, both(qgs, p, part(1, rows), part(h, DH)), 1, 1)
    for n, ((h, p), t) in enumerate(zip(cases, tokens)):
        row_max = jnp.max(scores[n], 0, keepdims=True)
        weights = jnp.exp2(scores[n] - row_max)
        weight_out[h, :, t] = weights
        sums_out[h, :, t] = dot(values[n], weights.astype(BF16), 0, 0)
        stats_out[h, 0:1, t] = row_max
        stats_out[h, 1:2, t] = jnp.sum(weights, 0, keepdims=True)
        keys_out[n] = keys[n]


def far_grad_kernel(n_far, *refs):
    qgs, fars = refs[:PLANE], refs[PLANE : PLANE + n_far]
    weight_ref, dots_ref, sums_ref, stats_ref = refs[PLANE + n_far : PLANE + n_far + 4]
    outs = refs[PLANE + n_far + 4 :]
    ads, grad_out, stats_out, far_out = outs[:PLANE], outs[PLANE], outs[PLANE + 1], outs[PLANE + 2 :]
    rows, width = qgs[0].shape[0] // 2, qgs[0].shape[1]
    first = slice(3 * rows, weight_ref.shape[1])
    first_rows = weight_ref.shape[1] - 3 * rows
    heads = range(width // DH)
    lanes = [part(h, DH) for h in heads]
    queries = [token_rows(qgs, 0, at) for at in lanes]
    grads = [token_rows(qgs, 1, at) for at in lanes]
    keys = [far_set(fars, at, 0) for at in lanes]
    values = [far_set(fars, at, 1) for at in lanes]
    scores = [dot(k, q, 1, 1) * SCALE2 for k, q in zip(keys, queries)]
    dots = [dot(v, g, 1, 1) for v, g in zip(values, grads)]
    weights, near_parts, inverses, sums = [], [], [], []
    for h in heads:
        near_max = stats_ref[h, 0:1, :]
        row_max = jnp.maximum(near_max, jnp.max(scores[h], 0, keepdims=True))
        weights.append(jnp.exp2(scores[h] - row_max))
        near_parts.append(jnp.exp2(near_max - row_max))
        sums.append(dot(values[h], weights[h].astype(BF16), 0, 0))
        inverses.append(
            1.0 / (stats_ref[h, 1:2, :] * near_parts[h] + jnp.sum(weights[h], 0, keepdims=True))
        )
    score_grads, probs = [], []
    for h in heads:
        attended = ((sums_ref[h] * near_parts[h] + sums[h]) * inverses[h]).astype(BF16)
        delta = jnp.sum(grads[h].T.astype(F32) * attended.astype(F32), 0, keepdims=True)
        near_scale = near_parts[h] * inverses[h]
        near_probs = weight_ref[h, first, :] * near_scale
        far_probs = weights[h] * inverses[h]
        score_grads.append(
            jnp.concatenate(
                [
                    (near_probs * (dots_ref[h, first, :] - delta)).astype(BF16),
                    (far_probs * (dots[h] - delta)).astype(BF16),
                ],
                0,
            )
        )
        probs.append(jnp.concatenate([near_probs.astype(BF16), far_probs.astype(BF16)], 0))
        grad_out[h] = score_grads[h][first_rows:]
        stats_out[h, 0:1, :] = near_scale
        stats_out[h, 1:2, :] = delta
        attended = attended.T
        for r in range(PLANE):
            ads[r][:rows, lanes[h]] = attended[part(r, rows)]
    for h in heads:
        for m, whole in enumerate(
            (dot(score_grads[h], queries[h]) * SCALE, dot(probs[h], grads[h]))
        ):
            at = 0
            for far in far_out:
                size = far.shape[0] // 2
                far[part(m, size), lanes[h]] = whole[at : at + size].astype(BF16)
                at += size


def plane_kernel(n_far, *refs):
    qgs, fars = refs[:PLANE], refs[PLANE : PLANE + n_far]
    keys_ref, weight_ref, dots_ref, grad_ref, stats_ref = refs[PLANE + n_far : PLANE + n_far + 5]
    refs = refs[2 * PLANE + n_far + 5 :]
    ads, dkvs = refs[:PLANE], refs[PLANE:]
    rows, width = qgs[0].shape[0] // 2, qgs[0].shape[1]
    pair = 2 * rows
    cases = [(h, p) for h in range(width // DH) for p in range(2)]
    score_grads, probs = [], []
    for h, p in cases:
        tokens = part(p, pair)
        probabilities = weight_ref[h, :, tokens] * stats_ref[h, 0:1, tokens]
        probs.append(probabilities.astype(BF16))
        score_grads.append(
            (probabilities * (dots_ref[h, :, tokens] - stats_ref[h, 1:2, tokens])).astype(BF16)
        )
    for n, (h, p) in enumerate(cases):
        far_keys = far_set(fars, part(h, DH), 0)
        dq = dot(keys_ref[n], score_grads[n], 0, 0)
        dq = dq + dot(far_keys, grad_ref[h, :, part(p, pair)], 0, 0)
        dq = (dq * SCALE).astype(BF16).T
        for k in range(2):
            ads[2 * p + k][rows:, part(h, DH)] = dq[part(k, rows)]
    grads = []
    for n, (h, p) in enumerate(cases):
        q, g = [both(qgs, p, part(m, rows), part(h, DH)) for m in range(2)]
        near = slice(0, 3 * rows)
        grads.append((dot(score_grads[n][near], q) * SCALE, dot(probs[n][near], g)))
    places = [
        (h, m, p, k) for h in range(width // DH) for m in range(2) for p in range(2) for k in range(2)
    ]
    pooled = [
        grads[2 * h + 1 - p][m][pair + k * rows // 2 : pair + (k + 1) * rows // 2]
        for h, m, p, k in places
    ]
    carried = spread(jnp.concatenate(pooled, 1), 2)
    for n, (h, m, p, k) in enumerate(places):
        dkvs[2 * p + k][part(m, rows), part(h, DH)] = (
            grads[2 * h + p][m][part(k, rows)] + carried[:, part(n, DH)]
        )


def carry_kernel(*refs):
    dkvs, far_refs, outs = refs[:PLANE], refs[PLANE:-PLANE], refs[-PLANE:]
    rows, width = dkvs[0].shape[0] // 2, dkvs[0].shape[1]
    wide, matrix = [], []
    for far in far_refs:
        size = far.shape[0] // (2 * PLANE)
        wide.append(jnp.concatenate([far[part(n, size), :] for n in range(2 * PLANE)], 1))
        matrix.append(spread_matrix(size, rows // size))
    carried = dot(jnp.concatenate(matrix, 1), jnp.concatenate(wide, 0))
    for n in range(2 * PLANE):
        m, r = divmod(n, PLANE)
        outs[r][part(m, rows), :] = (
            dkvs[r][part(m, rows), :] + carried[:, part(n, width)]
        ).astype(BF16)


def output_kernel(*refs):
    ads, w_ref, own_out, others = refs[:PLANE], refs[PLANE], refs[PLANE + 1], refs[PLANE + 2 :]
    rows, width = ads[0].shape[0] // 2, ads[0].shape[1]
    half = own_out.shape[1]
    head = lax.axis_index("head")
    total = None
    for r in range(PLANE):
        term = dot(ads[r][:rows, :], w_ref[columns(r, width), :])
        total = term if total is None else total + term

    def write(own, other):
        own_out[...] = own
        for n, out in enumerate(others):
            out[...] = other[part(n, rows // PIECES)].astype(BF16)

    @pl.when(head == 0)
    def _():
        write(total[:, :half], total[:, half:])

    @pl.when(head == 1)
    def _():
        write(total[:, half:], total[:, :half])


def join_kernel(own_ref, *refs):
    others, refs = refs[:PIECES], refs[PIECES:]
    ads, dkvs = refs[:PLANE], refs[PLANE : 2 * PLANE]
    o_out, gq_out, gk_out, gv_out, total, sems = refs[2 * PLANE :]
    rows, width = ads[0].shape[0] // 2, ads[0].shape[1]
    pairs = []
    for r in range(PLANE):
        here = columns(r, width)
        pairs.append((dkvs[r].at[part(0, rows), :], gk_out.at[:, here]))
        pairs.append((dkvs[r].at[part(1, rows), :], gv_out.at[:, here]))
        pairs.append((ads[r].at[part(1, rows), :], gq_out.at[:, here]))
    copies = start_all(pairs, sems)
    for n, other in enumerate(others):
        piece = part(n, rows // PIECES)
        total[piece, :] = (own_ref[piece, :] + other[...].astype(F32)).astype(BF16)
    last = pltpu.make_async_copy(total, o_out, sems.at[len(pairs)])
    last.start()
    for copy in copies + [last]:
        copy.wait()


def plane_exchange(blocks):
    return [blocks[0]] + [xor_permute(blocks[r], r) for r in range(1, PLANE)]


def pool_both(block):
    shaped = block.reshape((2, block.shape[0] // 4, 2) + block.shape[1:]).astype(F32)
    return ((shaped[:, :, 0] + shaped[:, :, 1]) * 0.5).astype(BF16).reshape(
        (block.shape[0] // 2,) + block.shape[1:]
    )


def spread_both(block):
    halved = block.astype(F32) * 0.5
    return jnp.repeat(halved, 2, axis=0)


def join_both(blocks):
    halves = [b.reshape((2, b.shape[0] // 2) + b.shape[1:]) for b in blocks]
    joined = jnp.concatenate(halves, 1)
    return joined.reshape((-1,) + joined.shape[2:])


def part_both(block, parts):
    shaped = block.reshape((2, parts, block.shape[0] // (2 * parts)) + block.shape[1:])
    return [shaped[:, n].reshape((-1,) + block.shape[1:]) for n in range(parts)]


def body(queries, key_rows, value_rows, out_weight, cotangent):
    rows, features = queries.shape
    width = features // PLANE
    top_rounds = lax.axis_size("ctx").bit_length() - 1 - 4
    shape = lambda *dims, t=BF16: jax.ShapeDtypeStruct(dims, t)
    dma = lambda n: pltpu.SemaphoreType.DMA((n,))
    blocks = [shape(2 * rows, width)] * PLANE

    other_cotangent = xor_permute(cotangent, 1, "head")
    key_values = call(
        key_value_kernel, blocks, key_rows, value_rows,
        hbm=(0, 1), scratch=[dma(2 * PLANE)], cost_us=8, name="pack_keys_values",
    )
    key_values = plane_exchange(key_values)
    query_grads = call(
        cotangent_kernel, blocks, queries, cotangent, other_cotangent, out_weight,
        hbm=(0, 1), scratch=[pltpu.VMEM(cotangent.shape, BF16), dma(1 + PLANE)],
        cost_us=3.0, name="grad_attended",
    )
    query_grads = plane_exchange(query_grads)
    near, pooled = call(
        far_kernel, [shape(2 * rows, width), shape(rows, width)], *key_values,
        after=(query_grads[0],), name="pool_plane",
    )
    fars = [xor_permute(near if n == 1 else pooled, n * PLANE) for n in ORDER]
    if top_rounds > 0:
        got = dict(zip(ORDER, fars))
        span = pool_both(join_both([pooled, pool_both(got[1]), got[2], got[3]]))
        for n in range(top_rounds):
            fars.append(xor_permute(span, 4 * PLANE << n))
            span = pool_both(join_both([span, fars[-1]]))
    far_rows = sum(far.shape[0] for far in fars[1:]) // 2
    heads, tokens = width // DH, PLANE * rows
    near_rows = 3 * rows + fars[0].shape[0] // 2
    weights, dots, sums, stats, near_keys = call(
        near_kernel,
        [shape(heads, near_rows, tokens, t=F32)] * 2
        + [shape(heads, DH, tokens, t=F32), shape(heads, 2, tokens, t=F32)]
        + [shape(2 * heads, near_rows, DH)],
        *key_values, *query_grads, fars[0], cost_us=2.0, name="near_attention",
    )
    results = call(
        lambda *refs: far_grad_kernel(len(fars) - 1, *refs),
        blocks + [shape(heads, far_rows, tokens), shape(heads, 2, tokens, t=F32)]
        + [shape(*far.shape) for far in fars],
        *query_grads, *fars[1:], weights, dots, sums, stats, cost_us=2.0, name="far_attention",
    )
    ads, kept, far_grads = results[:PLANE], results[PLANE : PLANE + 2], list(results[PLANE + 2 :])
    first = PLANE + len(fars) + 4
    results = call(
        lambda *refs: plane_kernel(len(fars) - 1, *refs),
        blocks + [shape(2 * rows, width, t=F32)] * PLANE,
        *query_grads, *fars[1:], near_keys, weights, dots, *kept, *ads,
        aliases={first + r: r for r in range(PLANE)}, cost_us=2.3, name="plane_grads",
    )
    att_dq, dkv = results[:PLANE], results[PLANE:]
    extra = []
    if top_rounds > 0:
        up = None
        for n in reversed(range(top_rounds)):
            send = far_grads[3 + n].astype(F32)
            if up is not None:
                own_up, their_up = part_both(spread_both(up), 2)
                send = send + their_up
            back = xor_permute(send.astype(BF16), 4 * PLANE << n).astype(F32)
            up = back if up is None else back + own_up
        ups = part_both(spread_both(up), PLANE)
        extra = [ups[0].astype(BF16)]
        ups[1] = spread_both(ups[1])
        for at, n in enumerate(ORDER):
            far_grads[at] = (far_grads[at].astype(F32) + ups[n]).astype(BF16)
    backs = [xor_permute(far_grads[at], n * PLANE) for at, n in enumerate(ORDER)]
    att_dq = plane_exchange(att_dq)
    dkv = call(carry_kernel, blocks, *dkv, *backs, *extra, cost_us=5.0, name="carry")
    own_sum, *other_sum = call(
        output_kernel,
        [shape(rows, features, t=F32)] + [shape(rows // PIECES, features)] * PIECES,
        *att_dq, out_weight, after=(dkv[0],), cost_us=0.01, name="project",
    )
    dkv = plane_exchange(dkv)
    other_sum = [xor_permute(piece, 1, "head") for piece in other_sum]
    output, grad_queries, grad_keys, grad_values = call(
        join_kernel, [shape(rows, features)] * 4, own_sum, *other_sum, *att_dq, *dkv,
        hbm_out=True, scratch=[pltpu.VMEM((rows, features), BF16), dma(3 * PLANE + 1)],
        name="join",
    )
    return (output, grad_queries, grad_keys, grad_values)


def solution(mesh):
    rows = P("ctx", "head")
    return jax.shard_map(
        body,
        mesh=mesh,
        in_specs=(rows, rows, rows, P("head", None), rows),
        out_specs=(rows, rows, rows, rows),
        check_vma=False,
    )
```

```python
import jax
import jax.numpy as jnp
from jax import lax
from jax.experimental import pallas as pl
from jax.experimental.pallas import tpu as pltpu
from jax.sharding import PartitionSpec as P

DH = 128
PLANE = 4
PIECES = 2
FARTHEST = (3, 1, 2, 0)
ORDER = (1, 2, 3)
SCALE = DH ** (-0.5)
SCALE2 = SCALE * 1.4426950408889634
BF16 = jnp.bfloat16
F32 = jnp.float32


def xor_permute(block, mask, axis="ctx"):
    count = lax.axis_size(axis)
    return lax.ppermute(block, axis, [(i, i ^ mask) for i in range(count)])


def dot(a, b, contract_a=1, contract_b=0):
    return lax.dot_general(
        a, b, (((contract_a,), (contract_b,)), ((), ())), preferred_element_type=F32
    )


def pool_matrix(rows):
    out = lax.broadcasted_iota(jnp.int32, (rows // 2, rows), 0)
    src = lax.broadcasted_iota(jnp.int32, (rows // 2, rows), 1)
    return jnp.where(src // 2 == out, 0.5, 0.0).astype(BF16)


def spread_matrix(rows, times):
    out = lax.broadcasted_iota(jnp.int32, (rows * times, rows), 0)
    src = lax.broadcasted_iota(jnp.int32, (rows * times, rows), 1)
    return jnp.where(out // times == src, 1.0 / times, 0.0).astype(BF16)


def pool(block):
    return dot(pool_matrix(block.shape[0]), block).astype(BF16)


def spread(block, times):
    return dot(spread_matrix(block.shape[0], times), block.astype(BF16))


def call(kernel, outs, *args, planes=(), after=(), aliases={}, hbm=(), hbm_out=False, scratch=(), cost_us=1.0, name=None):
    vmem = pl.BlockSpec(memory_space=pltpu.VMEM)
    in_hbm = pl.BlockSpec(memory_space=pltpu.HBM)
    space = pltpu.HBM if hbm_out else pltpu.VMEM
    args = [
        pltpu.with_memory_space_constraint(a, pltpu.HBM) if n in hbm else a
        for n, a in enumerate(args)
    ]
    count = len(args)
    order = list(range(count))
    for first in planes:
        order[first : first + PLANE] = [first + r for r in FARTHEST]
    places = [order.index(n) for n in range(count)]

    def run(*refs):
        kernel(*[refs[at] for at in places], *refs[count + len(after) :])

    return pl.pallas_call(
        run,
        out_shape=[space(out.shape, out.dtype) for out in outs],
        in_specs=[in_hbm if n in hbm else vmem for n in order]
        + [pl.BlockSpec(memory_space=pl.ANY)] * len(after),
        scratch_shapes=scratch,
        input_output_aliases={places[n]: out for n, out in aliases.items()},
        out_specs=[in_hbm if hbm_out else vmem] * len(outs),
        compiler_params=pltpu.CompilerParams(vmem_limit_bytes=24 * 1024 * 1024),
        cost_estimate=pl.CostEstimate(
            flops=int(cost_us * 1e9), bytes_accessed=0, transcendentals=0
        ),
        name=name,
    )(*[args[n] for n in order], *after)


def part(n, width):
    return slice(n * width, (n + 1) * width)


def start_all(pairs, sems):
    copies = [pltpu.make_async_copy(a, b, sems.at[n]) for n, (a, b) in enumerate(pairs)]
    for copy in copies:
        copy.start()
    return copies


def columns(r, width):
    place = (lax.axis_index("ctx") & (PLANE - 1)) ^ r
    return pl.ds(pl.multiple_of(place * width, width), width)


def key_value_kernel(k_ref, v_ref, *refs):
    outs, sems = refs[:PLANE], refs[PLANE]
    rows, width = k_ref.shape[0], k_ref.shape[1] // PLANE
    pairs = []
    for r in range(PLANE):
        pairs.append((k_ref.at[:, columns(r, width)], outs[r].at[part(0, rows), :]))
        pairs.append((v_ref.at[:, columns(r, width)], outs[r].at[part(1, rows), :]))
    for copy in start_all(pairs, sems):
        copy.wait()


def cotangent_kernel(q_ref, own_ref, other_ref, w_ref, *outs):
    rows, width = q_ref.shape[0], q_ref.shape[1] // PLANE
    half = own_ref.shape[1]
    head = lax.axis_index("head")
    own_at = pl.ds(pl.multiple_of(head * half, half), half)
    other_at = pl.ds(pl.multiple_of((1 - head) * half, half), half)
    for r in range(PLANE):
        here = columns(r, width)
        outs[r][:rows, :] = q_ref[:, here]
        outs[r][rows:, :] = (
            dot(own_ref[...], w_ref[here, own_at], 1, 1)
            + dot(other_ref[...], w_ref[here, other_at], 1, 1)
        ).astype(BF16)


def average_matrix(rows, times):
    out = lax.broadcasted_iota(jnp.int32, (rows // times, rows), 0)
    src = lax.broadcasted_iota(jnp.int32, (rows // times, rows), 1)
    return jnp.where(src // times == out, 1.0 / times, 0.0).astype(BF16)


def far_kernel(*refs):
    kvs, outs = refs[:PLANE], refs[PLANE:]
    rows, width = kvs[0].shape[0] // 2, kvs[0].shape[1]
    wide = jnp.concatenate([kv[part(m, rows), :] for m in range(2) for kv in kvs], 1)
    pooled = dot(
        jnp.concatenate([average_matrix(rows, 4), average_matrix(rows, 8)], 0), wide
    ).astype(BF16)
    for out, first, size in zip(outs, (0, rows // 4, rows // 4), (rows // 4, rows // 8, rows // 8)):
        for n in range(2 * PLANE):
            out[part(n, size), :] = pooled[first : first + size, part(n, width)]


def both(blocks, p, rows, lanes):
    return jnp.concatenate([blocks[r][rows, lanes] for r in (2 * p, 2 * p + 1)], 0)


def near_set(kvs, p, lanes, m):
    rows = part(m, kvs[0].shape[0] // 2)
    other = [pool(kv[rows, lanes]) for kv in kvs[2 - 2 * p : 4 - 2 * p]]
    return jnp.concatenate([both(kvs, p, rows, lanes)] + other, 0)


def far_set(fars, lanes, m):
    return jnp.concatenate([far[part(m, far.shape[0] // 2), lanes] for far in fars], 0)


def token_rows(qgs, m, lanes):
    rows = part(m, qgs[0].shape[0] // 2)
    return jnp.concatenate([qg[rows, lanes] for qg in qgs], 0)


def near_kernel(*refs):
    kvs, qgs, first = refs[:PLANE], refs[PLANE : 2 * PLANE], refs[2 * PLANE]
    weight_out, dots_out, sums_out, stats_out, keys_out = refs[2 * PLANE + 1 :]
    rows, width = qgs[0].shape[0] // 2, qgs[0].shape[1]
    cases = [(h, p) for h in range(width // DH) for p in range(2)]
    tokens = [part(p, 2 * rows) for h, p in cases]
    keys, values = [
        [
            jnp.concatenate(
                [near_set(kvs, p, part(h, DH), m), first[part(m, first.shape[0] // 2), part(h, DH)]], 0
            )
            for h, p in cases
        ]
        for m in range(2)
    ]
    scores = [
        dot(k, both(qgs, p, part(0, rows), part(h, DH)), 1, 1) * SCALE2
        for k, (h, p) in zip(keys, cases)
    ]
    for (h, p), v, t in zip(cases, values, tokens):
        dots_out[h, :, t] = dot(v, both(qgs, p, part(1, rows), part(h, DH)), 1, 1)
    for n, ((h, p), t) in enumerate(zip(cases, tokens)):
        row_max = jnp.max(scores[n], 0, keepdims=True)
        weights = jnp.exp2(scores[n] - row_max)
        weight_out[h, :, t] = weights
        sums_out[h, :, t] = dot(values[n], weights.astype(BF16), 0, 0)
        stats_out[h, 0:1, t] = row_max
        stats_out[h, 1:2, t] = jnp.sum(weights, 0, keepdims=True)
        keys_out[n] = keys[n]


def far_grad_kernel(n_far, *refs):
    qgs, fars = refs[:PLANE], refs[PLANE : PLANE + n_far]
    weight_ref, dots_ref, sums_ref, stats_ref = refs[PLANE + n_far : PLANE + n_far + 4]
    outs = refs[PLANE + n_far + 4 :]
    ads, grad_out, stats_out, far_out = outs[:PLANE], outs[PLANE], outs[PLANE + 1], outs[PLANE + 2 :]
    rows, width = qgs[0].shape[0] // 2, qgs[0].shape[1]
    first = slice(3 * rows, weight_ref.shape[1])
    first_rows = weight_ref.shape[1] - 3 * rows
    heads = range(width // DH)
    lanes = [part(h, DH) for h in heads]
    queries = [token_rows(qgs, 0, at) for at in lanes]
    grads = [token_rows(qgs, 1, at) for at in lanes]
    keys = [far_set(fars, at, 0) for at in lanes]
    values = [far_set(fars, at, 1) for at in lanes]
    scores = [dot(k, q, 1, 1) * SCALE2 for k, q in zip(keys, queries)]
    dots = [dot(v, g, 1, 1) for v, g in zip(values, grads)]
    weights, near_parts, inverses, sums = [], [], [], []
    for h in heads:
        near_max = stats_ref[h, 0:1, :]
        row_max = jnp.maximum(near_max, jnp.max(scores[h], 0, keepdims=True))
        weights.append(jnp.exp2(scores[h] - row_max))
        near_parts.append(jnp.exp2(near_max - row_max))
        sums.append(dot(values[h], weights[h].astype(BF16), 0, 0))
        inverses.append(
            1.0 / (stats_ref[h, 1:2, :] * near_parts[h] + jnp.sum(weights[h], 0, keepdims=True))
        )
    score_grads, probs = [], []
    for h in heads:
        attended = ((sums_ref[h] * near_parts[h] + sums[h]) * inverses[h]).astype(BF16)
        delta = jnp.sum(grads[h].T.astype(F32) * attended.astype(F32), 0, keepdims=True)
        near_scale = near_parts[h] * inverses[h]
        near_probs = weight_ref[h, first, :] * near_scale
        far_probs = weights[h] * inverses[h]
        score_grads.append(
            jnp.concatenate(
                [
                    (near_probs * (dots_ref[h, first, :] - delta)).astype(BF16),
                    (far_probs * (dots[h] - delta)).astype(BF16),
                ],
                0,
            )
        )
        probs.append(jnp.concatenate([near_probs.astype(BF16), far_probs.astype(BF16)], 0))
        grad_out[h] = score_grads[h][first_rows:]
        stats_out[h, 0:1, :] = near_scale
        stats_out[h, 1:2, :] = delta
        attended = attended.T
        for r in range(PLANE):
            ads[r][:rows, lanes[h]] = attended[part(r, rows)]
    for h in heads:
        for m, whole in enumerate(
            (dot(score_grads[h], queries[h]) * SCALE, dot(probs[h], grads[h]))
        ):
            at = 0
            for far in far_out:
                size = far.shape[0] // 2
                far[part(m, size), lanes[h]] = whole[at : at + size].astype(BF16)
                at += size


def plane_kernel(n_far, *refs):
    qgs, fars = refs[:PLANE], refs[PLANE : PLANE + n_far]
    keys_ref, weight_ref, dots_ref, grad_ref, stats_ref = refs[PLANE + n_far : PLANE + n_far + 5]
    refs = refs[2 * PLANE + n_far + 5 :]
    ads, dkvs = refs[:PLANE], refs[PLANE:]
    rows, width = qgs[0].shape[0] // 2, qgs[0].shape[1]
    pair = 2 * rows
    cases = [(h, p) for h in range(width // DH) for p in range(2)]
    score_grads, probs = [], []
    for h, p in cases:
        tokens = part(p, pair)
        probabilities = weight_ref[h, :, tokens] * stats_ref[h, 0:1, tokens]
        probs.append(probabilities.astype(BF16))
        score_grads.append(
            (probabilities * (dots_ref[h, :, tokens] - stats_ref[h, 1:2, tokens])).astype(BF16)
        )
    for n, (h, p) in enumerate(cases):
        far_keys = far_set(fars, part(h, DH), 0)
        dq = dot(keys_ref[n], score_grads[n], 0, 0)
        dq = dq + dot(far_keys, grad_ref[h, :, part(p, pair)], 0, 0)
        dq = (dq * SCALE).astype(BF16).T
        for k in range(2):
            ads[2 * p + k][rows:, part(h, DH)] = dq[part(k, rows)]
    grads = []
    for n, (h, p) in enumerate(cases):
        q, g = [both(qgs, p, part(m, rows), part(h, DH)) for m in range(2)]
        near = slice(0, 3 * rows)
        grads.append((dot(score_grads[n][near], q) * SCALE, dot(probs[n][near], g)))
    places = [
        (h, m, p, k) for h in range(width // DH) for m in range(2) for p in range(2) for k in range(2)
    ]
    pooled = [
        grads[2 * h + 1 - p][m][pair + k * rows // 2 : pair + (k + 1) * rows // 2]
        for h, m, p, k in places
    ]
    carried = spread(jnp.concatenate(pooled, 1), 2)
    for n, (h, m, p, k) in enumerate(places):
        dkvs[2 * p + k][part(m, rows), part(h, DH)] = (
            grads[2 * h + p][m][part(k, rows)] + carried[:, part(n, DH)]
        )


def carry_kernel(*refs):
    dkvs, far_refs, outs = refs[:PLANE], refs[PLANE:-PLANE], refs[-PLANE:]
    rows, width = dkvs[0].shape[0] // 2, dkvs[0].shape[1]
    wide, matrix = [], []
    for far in far_refs:
        size = far.shape[0] // (2 * PLANE)
        wide.append(jnp.concatenate([far[part(n, size), :] for n in range(2 * PLANE)], 1))
        matrix.append(spread_matrix(size, rows // size))
    carried = dot(jnp.concatenate(matrix, 1), jnp.concatenate(wide, 0))
    for n in range(2 * PLANE):
        m, r = divmod(n, PLANE)
        outs[r][part(m, rows), :] = (
            dkvs[r][part(m, rows), :] + carried[:, part(n, width)]
        ).astype(BF16)


def output_kernel(*refs):
    ads, w_ref, own_out, others = refs[:PLANE], refs[PLANE], refs[PLANE + 1], refs[PLANE + 2 :]
    rows, width = ads[0].shape[0] // 2, ads[0].shape[1]
    half = own_out.shape[1]
    head = lax.axis_index("head")
    total = None
    for r in range(PLANE):
        term = dot(ads[r][:rows, :], w_ref[columns(r, width), :])
        total = term if total is None else total + term

    def write(own, other):
        own_out[...] = own
        for n, out in enumerate(others):
            out[...] = other[part(n, rows // PIECES)].astype(BF16)

    @pl.when(head == 0)
    def _():
        write(total[:, :half], total[:, half:])

    @pl.when(head == 1)
    def _():
        write(total[:, half:], total[:, :half])


def join_kernel(own_ref, *refs):
    others, refs = refs[:PIECES], refs[PIECES:]
    ads, dkvs = refs[:PLANE], refs[PLANE : 2 * PLANE]
    o_out, gq_out, gk_out, gv_out, total, sems = refs[2 * PLANE :]
    rows, width = ads[0].shape[0] // 2, ads[0].shape[1]
    pairs = []
    for r in range(PLANE):
        here = columns(r, width)
        pairs.append((dkvs[r].at[part(0, rows), :], gk_out.at[:, here]))
        pairs.append((dkvs[r].at[part(1, rows), :], gv_out.at[:, here]))
        pairs.append((ads[r].at[part(1, rows), :], gq_out.at[:, here]))
    copies = start_all(pairs, sems)
    for n, other in enumerate(others):
        piece = part(n, rows // PIECES)
        total[piece, :] = (own_ref[piece, :] + other[...].astype(F32)).astype(BF16)
    last = pltpu.make_async_copy(total, o_out, sems.at[len(pairs)])
    last.start()
    for copy in copies + [last]:
        copy.wait()


def plane_exchange(blocks):
    return [blocks[0]] + [xor_permute(blocks[r], r) for r in range(1, PLANE)]


def pool_both(block):
    shaped = block.reshape((2, block.shape[0] // 4, 2) + block.shape[1:]).astype(F32)
    return ((shaped[:, :, 0] + shaped[:, :, 1]) * 0.5).astype(BF16).reshape(
        (block.shape[0] // 2,) + block.shape[1:]
    )


def spread_both(block):
    halved = block.astype(F32) * 0.5
    return jnp.repeat(halved, 2, axis=0)


def join_both(blocks):
    halves = [b.reshape((2, b.shape[0] // 2) + b.shape[1:]) for b in blocks]
    joined = jnp.concatenate(halves, 1)
    return joined.reshape((-1,) + joined.shape[2:])


def part_both(block, parts):
    shaped = block.reshape((2, parts, block.shape[0] // (2 * parts)) + block.shape[1:])
    return [shaped[:, n].reshape((-1,) + block.shape[1:]) for n in range(parts)]


def body(queries, key_rows, value_rows, out_weight, cotangent):
    rows, features = queries.shape
    width = features // PLANE
    top_rounds = lax.axis_size("ctx").bit_length() - 1 - 4
    shape = lambda *dims, t=BF16: jax.ShapeDtypeStruct(dims, t)
    dma = lambda n: pltpu.SemaphoreType.DMA((n,))
    blocks = [shape(2 * rows, width)] * PLANE

    other_cotangent = xor_permute(cotangent, 1, "head")
    key_values = call(
        key_value_kernel, blocks, key_rows, value_rows,
        hbm=(0, 1), scratch=[dma(2 * PLANE)], cost_us=8, name="pack_keys_values",
    )
    key_values = plane_exchange(key_values)
    query_grads = call(
        cotangent_kernel, blocks, queries, cotangent, other_cotangent, out_weight,
        cost_us=3.0, name="grad_attended",
    )
    query_grads = plane_exchange(query_grads)
    near, pooled, pooled3 = call(
        far_kernel, [shape(2 * rows, width)] + [shape(rows, width)] * 2, *key_values, planes=(0,),
        after=(query_grads[0],), cost_us=1.0, name="pool_plane",
    )
    fars = [xor_permute({1: near, 2: pooled, 3: pooled3}[n], n * PLANE) for n in ORDER]
    if top_rounds > 0:
        got = dict(zip(ORDER, fars))
        span = pool_both(join_both([pooled, pool_both(got[1]), got[2], got[3]]))
        for n in range(top_rounds):
            fars.append(xor_permute(span, 4 * PLANE << n))
            span = pool_both(join_both([span, fars[-1]]))
    far_rows = sum(far.shape[0] for far in fars[1:]) // 2
    heads, tokens = width // DH, PLANE * rows
    near_rows = 3 * rows + fars[0].shape[0] // 2
    weights, dots, sums, stats, near_keys = call(
        near_kernel,
        [shape(heads, near_rows, tokens, t=F32)] * 2
        + [shape(heads, DH, tokens, t=F32), shape(heads, 2, tokens, t=F32)]
        + [shape(2 * heads, near_rows, DH)],
        *key_values, *query_grads, fars[0], planes=(0, PLANE), cost_us=2.0, name="near_attention",
    )
    results = call(
        lambda *refs: far_grad_kernel(len(fars) - 1, *refs),
        blocks + [shape(heads, far_rows, tokens), shape(heads, 2, tokens, t=F32)]
        + [shape(*far.shape) for far in fars],
        *query_grads, *fars[1:], weights, dots, sums, stats, planes=(0,), cost_us=2.0, name="far_attention",
    )
    ads, kept, far_grads = results[:PLANE], results[PLANE : PLANE + 2], list(results[PLANE + 2 :])
    first = PLANE + len(fars) + 4
    results = call(
        lambda *refs: plane_kernel(len(fars) - 1, *refs),
        blocks + [shape(2 * rows, width, t=F32)] * PLANE,
        *query_grads, *fars[1:], near_keys, weights, dots, *kept, *ads,
        aliases={first + r: r for r in range(PLANE)}, cost_us=2.3, name="plane_grads",
    )
    att_dq, dkv = results[:PLANE], results[PLANE:]
    extra = []
    if top_rounds > 0:
        up = None
        for n in reversed(range(top_rounds)):
            send = far_grads[3 + n].astype(F32)
            if up is not None:
                own_up, their_up = part_both(spread_both(up), 2)
                send = send + their_up
            back = xor_permute(send.astype(BF16), 4 * PLANE << n).astype(F32)
            up = back if up is None else back + own_up
        ups = part_both(spread_both(up), PLANE)
        extra = [ups[0].astype(BF16)]
        ups[1] = spread_both(ups[1])
        for at, n in enumerate(ORDER):
            far_grads[at] = (far_grads[at].astype(F32) + ups[n]).astype(BF16)
    backs = [xor_permute(far_grads[at], n * PLANE) for at, n in enumerate(ORDER)]
    att_dq = plane_exchange(att_dq)
    dkv = call(carry_kernel, blocks, *dkv, *backs, *extra, cost_us=5.0, name="carry")
    own_sum, *other_sum = call(
        output_kernel,
        [shape(rows, features, t=F32)] + [shape(rows // PIECES, features)] * PIECES,
        *att_dq, out_weight, planes=(0,), after=(dkv[0],), cost_us=0.01, name="project",
    )
    dkv = plane_exchange(dkv)
    other_sum = [xor_permute(piece, 1, "head") for piece in other_sum]
    output, grad_queries, grad_keys, grad_values = call(
        join_kernel, [shape(rows, features)] * 4, own_sum, *other_sum, *att_dq, *dkv, planes=(1 + PIECES, 1 + PIECES + PLANE),
        hbm_out=True, scratch=[pltpu.VMEM((rows, features), BF16), dma(3 * PLANE + 1)],
        cost_us=1.0, name="join",
    )
    return (output, grad_queries, grad_keys, grad_values)


def solution(mesh):
    rows = P("ctx", "head")
    return jax.shard_map(
        body,
        mesh=mesh,
        in_specs=(rows, rows, rows, P("head", None), rows),
        out_specs=(rows, rows, rows, rows),
        check_vma=False,
    )
```

```python
import jax
import jax.numpy as jnp
from jax import lax
from jax.experimental import pallas as pl
from jax.experimental.pallas import tpu as pltpu
from jax.sharding import PartitionSpec as P

DH = 128
PLANE = 4
PIECES = 2
OKV = (3, 1, 2, 0)
OQG = (2, 1, 3, 0)
OAD = (3, 1, 2, 0)
ODKV = (2, 3, 1, 0)
ORDER = (1, 2, 3)
SCALE = DH ** (-0.5)
SCALE2 = SCALE * 1.4426950408889634
BF16 = jnp.bfloat16
F32 = jnp.float32


def xor_permute(block, mask, axis="ctx"):
    count = lax.axis_size(axis)
    return lax.ppermute(block, axis, [(i, i ^ mask) for i in range(count)])


def dot(a, b, contract_a=1, contract_b=0):
    return lax.dot_general(
        a, b, (((contract_a,), (contract_b,)), ((), ())), preferred_element_type=F32
    )


def pool_matrix(rows):
    out = lax.broadcasted_iota(jnp.int32, (rows // 2, rows), 0)
    src = lax.broadcasted_iota(jnp.int32, (rows // 2, rows), 1)
    return jnp.where(src // 2 == out, 0.5, 0.0).astype(BF16)


def spread_matrix(rows, times):
    out = lax.broadcasted_iota(jnp.int32, (rows * times, rows), 0)
    src = lax.broadcasted_iota(jnp.int32, (rows * times, rows), 1)
    return jnp.where(out // times == src, 1.0 / times, 0.0).astype(BF16)


def pool(block):
    return dot(pool_matrix(block.shape[0]), block).astype(BF16)


def spread(block, times):
    return dot(spread_matrix(block.shape[0], times), block.astype(BF16))


def call(kernel, outs, *args, planes=(), after=(), aliases={}, hbm=(), hbm_out=False, scratch=(), cost_us=1.0, name=None):
    vmem = pl.BlockSpec(memory_space=pltpu.VMEM)
    in_hbm = pl.BlockSpec(memory_space=pltpu.HBM)
    space = pltpu.HBM if hbm_out else pltpu.VMEM
    args = [
        pltpu.with_memory_space_constraint(a, pltpu.HBM) if n in hbm else a
        for n, a in enumerate(args)
    ]
    count = len(args)
    order = list(range(count))
    for first in planes:
        order[first[0] : first[0] + PLANE] = [first[0] + r for r in first[1]]
    places = [order.index(n) for n in range(count)]

    def run(*refs):
        kernel(*[refs[at] for at in places], *refs[count + len(after) :])

    return pl.pallas_call(
        run,
        out_shape=[space(out.shape, out.dtype) for out in outs],
        in_specs=[in_hbm if n in hbm else vmem for n in order]
        + [pl.BlockSpec(memory_space=pl.ANY)] * len(after),
        scratch_shapes=scratch,
        input_output_aliases={places[n]: out for n, out in aliases.items()},
        out_specs=[in_hbm if hbm_out else vmem] * len(outs),
        compiler_params=pltpu.CompilerParams(vmem_limit_bytes=24 * 1024 * 1024),
        cost_estimate=pl.CostEstimate(
            flops=int(cost_us * 1e9), bytes_accessed=0, transcendentals=0
        ),
        name=name,
    )(*[args[n] for n in order], *after)


def part(n, width):
    return slice(n * width, (n + 1) * width)


def start_all(pairs, sems):
    copies = [pltpu.make_async_copy(a, b, sems.at[n]) for n, (a, b) in enumerate(pairs)]
    for copy in copies:
        copy.start()
    return copies


def columns(r, width):
    place = (lax.axis_index("ctx") & (PLANE - 1)) ^ r
    return pl.ds(pl.multiple_of(place * width, width), width)


def key_value_kernel(k_ref, v_ref, *refs):
    outs, sems = refs[:PLANE], refs[PLANE]
    rows, width = k_ref.shape[0], k_ref.shape[1] // PLANE
    pairs = []
    for r in range(PLANE):
        pairs.append((k_ref.at[:, columns(r, width)], outs[r].at[part(0, rows), :]))
        pairs.append((v_ref.at[:, columns(r, width)], outs[r].at[part(1, rows), :]))
    for copy in start_all(pairs, sems):
        copy.wait()


def cotangent_kernel(q_ref, own_ref, other_ref, w_ref, *outs):
    rows, width = q_ref.shape[0], q_ref.shape[1] // PLANE
    half = own_ref.shape[1]
    head = lax.axis_index("head")
    own_at = pl.ds(pl.multiple_of(head * half, half), half)
    other_at = pl.ds(pl.multiple_of((1 - head) * half, half), half)
    for r in range(PLANE):
        here = columns(r, width)
        outs[r][:rows, :] = q_ref[:, here]
        outs[r][rows:, :] = (
            dot(own_ref[...], w_ref[here, own_at], 1, 1)
            + dot(other_ref[...], w_ref[here, other_at], 1, 1)
        ).astype(BF16)


def average_matrix(rows, times):
    out = lax.broadcasted_iota(jnp.int32, (rows // times, rows), 0)
    src = lax.broadcasted_iota(jnp.int32, (rows // times, rows), 1)
    return jnp.where(src // times == out, 1.0 / times, 0.0).astype(BF16)


def far_kernel(*refs):
    kvs, outs = refs[:PLANE], refs[PLANE:]
    rows, width = kvs[0].shape[0] // 2, kvs[0].shape[1]
    wide = jnp.concatenate([kv[part(m, rows), :] for m in range(2) for kv in kvs], 1)
    pooled = dot(
        jnp.concatenate([average_matrix(rows, 4), average_matrix(rows, 8)], 0), wide
    ).astype(BF16)
    for out, first, size in zip(outs, (0, rows // 4, rows // 4), (rows // 4, rows // 8, rows // 8)):
        for n in range(2 * PLANE):
            out[part(n, size), :] = pooled[first : first + size, part(n, width)]


def both(blocks, p, rows, lanes):
    return jnp.concatenate([blocks[r][rows, lanes] for r in (2 * p, 2 * p + 1)], 0)


def near_set(kvs, p, lanes, m):
    rows = part(m, kvs[0].shape[0] // 2)
    other = [pool(kv[rows, lanes]) for kv in kvs[2 - 2 * p : 4 - 2 * p]]
    return jnp.concatenate([both(kvs, p, rows, lanes)] + other, 0)


def far_set(fars, lanes, m):
    return jnp.concatenate([far[part(m, far.shape[0] // 2), lanes] for far in fars], 0)


def token_rows(qgs, m, lanes):
    rows = part(m, qgs[0].shape[0] // 2)
    return jnp.concatenate([qg[rows, lanes] for qg in qgs], 0)


def near_kernel(*refs):
    kvs, qgs, first = refs[:PLANE], refs[PLANE : 2 * PLANE], refs[2 * PLANE]
    weight_out, dots_out, sums_out, stats_out, keys_out = refs[2 * PLANE + 1 :]
    rows, width = qgs[0].shape[0] // 2, qgs[0].shape[1]
    cases = [(h, p) for h in range(width // DH) for p in range(2)]
    tokens = [part(p, 2 * rows) for h, p in cases]
    keys, values = [
        [
            jnp.concatenate(
                [near_set(kvs, p, part(h, DH), m), first[part(m, first.shape[0] // 2), part(h, DH)]], 0
            )
            for h, p in cases
        ]
        for m in range(2)
    ]
    scores = [
        dot(k, both(qgs, p, part(0, rows), part(h, DH)), 1, 1) * SCALE2
        for k, (h, p) in zip(keys, cases)
    ]
    for (h, p), v, t in zip(cases, values, tokens):
        dots_out[h, :, t] = dot(v, both(qgs, p, part(1, rows), part(h, DH)), 1, 1)
    for n, ((h, p), t) in enumerate(zip(cases, tokens)):
        row_max = jnp.max(scores[n], 0, keepdims=True)
        weights = jnp.exp2(scores[n] - row_max)
        weight_out[h, :, t] = weights
        sums_out[h, :, t] = dot(values[n], weights.astype(BF16), 0, 0)
        stats_out[h, 0:1, t] = row_max
        stats_out[h, 1:2, t] = jnp.sum(weights, 0, keepdims=True)
        keys_out[n] = keys[n]


def far_grad_kernel(n_far, *refs):
    qgs, fars = refs[:PLANE], refs[PLANE : PLANE + n_far]
    weight_ref, dots_ref, sums_ref, stats_ref = refs[PLANE + n_far : PLANE + n_far + 4]
    outs = refs[PLANE + n_far + 4 :]
    ads, grad_out, stats_out, far_out = outs[:PLANE], outs[PLANE], outs[PLANE + 1], outs[PLANE + 2 :]
    rows, width = qgs[0].shape[0] // 2, qgs[0].shape[1]
    first = slice(3 * rows, weight_ref.shape[1])
    first_rows = weight_ref.shape[1] - 3 * rows
    heads = range(width // DH)
    lanes = [part(h, DH) for h in heads]
    queries = [token_rows(qgs, 0, at) for at in lanes]
    grads = [token_rows(qgs, 1, at) for at in lanes]
    keys = [far_set(fars, at, 0) for at in lanes]
    values = [far_set(fars, at, 1) for at in lanes]
    scores = [dot(k, q, 1, 1) * SCALE2 for k, q in zip(keys, queries)]
    dots = [dot(v, g, 1, 1) for v, g in zip(values, grads)]
    weights, near_parts, inverses, sums = [], [], [], []
    for h in heads:
        near_max = stats_ref[h, 0:1, :]
        row_max = jnp.maximum(near_max, jnp.max(scores[h], 0, keepdims=True))
        weights.append(jnp.exp2(scores[h] - row_max))
        near_parts.append(jnp.exp2(near_max - row_max))
        sums.append(dot(values[h], weights[h].astype(BF16), 0, 0))
        inverses.append(
            1.0 / (stats_ref[h, 1:2, :] * near_parts[h] + jnp.sum(weights[h], 0, keepdims=True))
        )
    score_grads, probs = [], []
    for h in heads:
        attended = ((sums_ref[h] * near_parts[h] + sums[h]) * inverses[h]).astype(BF16)
        delta = jnp.sum(grads[h].T.astype(F32) * attended.astype(F32), 0, keepdims=True)
        near_scale = near_parts[h] * inverses[h]
        near_probs = weight_ref[h, first, :] * near_scale
        far_probs = weights[h] * inverses[h]
        score_grads.append(
            jnp.concatenate(
                [
                    (near_probs * (dots_ref[h, first, :] - delta)).astype(BF16),
                    (far_probs * (dots[h] - delta)).astype(BF16),
                ],
                0,
            )
        )
        probs.append(jnp.concatenate([near_probs.astype(BF16), far_probs.astype(BF16)], 0))
        grad_out[h] = score_grads[h][first_rows:]
        stats_out[h, 0:1, :] = near_scale
        stats_out[h, 1:2, :] = delta
        attended = attended.T
        for r in range(PLANE):
            ads[r][:rows, lanes[h]] = attended[part(r, rows)]
    for h in heads:
        for m, whole in enumerate(
            (dot(score_grads[h], queries[h]) * SCALE, dot(probs[h], grads[h]))
        ):
            at = 0
            for far in far_out:
                size = far.shape[0] // 2
                far[part(m, size), lanes[h]] = whole[at : at + size].astype(BF16)
                at += size


def plane_kernel(n_far, *refs):
    qgs, fars = refs[:PLANE], refs[PLANE : PLANE + n_far]
    keys_ref, weight_ref, dots_ref, grad_ref, stats_ref = refs[PLANE + n_far : PLANE + n_far + 5]
    refs = refs[2 * PLANE + n_far + 5 :]
    ads, dkvs = refs[:PLANE], refs[PLANE:]
    rows, width = qgs[0].shape[0] // 2, qgs[0].shape[1]
    pair = 2 * rows
    cases = [(h, p) for h in range(width // DH) for p in range(2)]
    score_grads, probs = [], []
    for h, p in cases:
        tokens = part(p, pair)
        probabilities = weight_ref[h, :, tokens] * stats_ref[h, 0:1, tokens]
        probs.append(probabilities.astype(BF16))
        score_grads.append(
            (probabilities * (dots_ref[h, :, tokens] - stats_ref[h, 1:2, tokens])).astype(BF16)
        )
    for n, (h, p) in enumerate(cases):
        far_keys = far_set(fars, part(h, DH), 0)
        dq = dot(keys_ref[n], score_grads[n], 0, 0)
        dq = dq + dot(far_keys, grad_ref[h, :, part(p, pair)], 0, 0)
        dq = (dq * SCALE).astype(BF16).T
        for k in range(2):
            ads[2 * p + k][rows:, part(h, DH)] = dq[part(k, rows)]
    grads = []
    for n, (h, p) in enumerate(cases):
        q, g = [both(qgs, p, part(m, rows), part(h, DH)) for m in range(2)]
        near = slice(0, 3 * rows)
        grads.append((dot(score_grads[n][near], q) * SCALE, dot(probs[n][near], g)))
    places = [
        (h, m, p, k) for h in range(width // DH) for m in range(2) for p in range(2) for k in range(2)
    ]
    pooled = [
        grads[2 * h + 1 - p][m][pair + k * rows // 2 : pair + (k + 1) * rows // 2]
        for h, m, p, k in places
    ]
    carried = spread(jnp.concatenate(pooled, 1), 2)
    for n, (h, m, p, k) in enumerate(places):
        dkvs[2 * p + k][part(m, rows), part(h, DH)] = (
            grads[2 * h + p][m][part(k, rows)] + carried[:, part(n, DH)]
        )


def carry_kernel(*refs):
    dkvs, far_refs, outs = refs[:PLANE], refs[PLANE:-PLANE], refs[-PLANE:]
    rows, width = dkvs[0].shape[0] // 2, dkvs[0].shape[1]
    wide, matrix = [], []
    for far in far_refs:
        size = far.shape[0] // (2 * PLANE)
        wide.append(jnp.concatenate([far[part(n, size), :] for n in range(2 * PLANE)], 1))
        matrix.append(spread_matrix(size, rows // size))
    carried = dot(jnp.concatenate(matrix, 1), jnp.concatenate(wide, 0))
    for n in range(2 * PLANE):
        m, r = divmod(n, PLANE)
        outs[r][part(m, rows), :] = (
            dkvs[r][part(m, rows), :] + carried[:, part(n, width)]
        ).astype(BF16)


def output_kernel(*refs):
    ads, w_ref, own_out, others = refs[:PLANE], refs[PLANE], refs[PLANE + 1], refs[PLANE + 2 :]
    rows, width = ads[0].shape[0] // 2, ads[0].shape[1]
    half = own_out.shape[1]
    head = lax.axis_index("head")
    total = None
    for r in range(PLANE):
        term = dot(ads[r][:rows, :], w_ref[columns(r, width), :])
        total = term if total is None else total + term

    def write(own, other):
        own_out[...] = own
        for n, out in enumerate(others):
            out[...] = other[part(n, rows // PIECES)].astype(BF16)

    @pl.when(head == 0)
    def _():
        write(total[:, :half], total[:, half:])

    @pl.when(head == 1)
    def _():
        write(total[:, half:], total[:, :half])


def join_kernel(own_ref, *refs):
    others, refs = refs[:PIECES], refs[PIECES:]
    ads, dkvs = refs[:PLANE], refs[PLANE : 2 * PLANE]
    o_out, gq_out, gk_out, gv_out, total, sems = refs[2 * PLANE :]
    rows, width = ads[0].shape[0] // 2, ads[0].shape[1]
    pairs = []
    for r in range(PLANE):
        here = columns(r, width)
        pairs.append((dkvs[r].at[part(0, rows), :], gk_out.at[:, here]))
        pairs.append((dkvs[r].at[part(1, rows), :], gv_out.at[:, here]))
        pairs.append((ads[r].at[part(1, rows), :], gq_out.at[:, here]))
    copies = start_all(pairs, sems)
    for n, other in enumerate(others):
        piece = part(n, rows // PIECES)
        total[piece, :] = (own_ref[piece, :] + other[...].astype(F32)).astype(BF16)
    last = pltpu.make_async_copy(total, o_out, sems.at[len(pairs)])
    last.start()
    for copy in copies + [last]:
        copy.wait()


def plane_exchange(blocks):
    return [blocks[0]] + [xor_permute(blocks[r], r) for r in range(1, PLANE)]


def pool_both(block):
    shaped = block.reshape((2, block.shape[0] // 4, 2) + block.shape[1:]).astype(F32)
    return ((shaped[:, :, 0] + shaped[:, :, 1]) * 0.5).astype(BF16).reshape(
        (block.shape[0] // 2,) + block.shape[1:]
    )


def spread_both(block):
    halved = block.astype(F32) * 0.5
    return jnp.repeat(halved, 2, axis=0)


def join_both(blocks):
    halves = [b.reshape((2, b.shape[0] // 2) + b.shape[1:]) for b in blocks]
    joined = jnp.concatenate(halves, 1)
    return joined.reshape((-1,) + joined.shape[2:])


def part_both(block, parts):
    shaped = block.reshape((2, parts, block.shape[0] // (2 * parts)) + block.shape[1:])
    return [shaped[:, n].reshape((-1,) + block.shape[1:]) for n in range(parts)]


def body(queries, key_rows, value_rows, out_weight, cotangent):
    rows, features = queries.shape
    width = features // PLANE
    top_rounds = lax.axis_size("ctx").bit_length() - 1 - 4
    shape = lambda *dims, t=BF16: jax.ShapeDtypeStruct(dims, t)
    dma = lambda n: pltpu.SemaphoreType.DMA((n,))
    blocks = [shape(2 * rows, width)] * PLANE

    other_cotangent = xor_permute(cotangent, 1, "head")
    key_values = call(
        key_value_kernel, blocks, key_rows, value_rows,
        hbm=(0, 1), scratch=[dma(2 * PLANE)], cost_us=8, name="pack_keys_values",
    )
    key_values = plane_exchange(key_values)
    query_grads = call(
        cotangent_kernel, blocks, queries, cotangent, other_cotangent, out_weight,
        cost_us=3.0, name="grad_attended",
    )
    query_grads = plane_exchange(query_grads)
    near, pooled, pooled3 = call(
        far_kernel, [shape(2 * rows, width)] + [shape(rows, width)] * 2, *key_values, planes=((0, OKV),),
        after=(query_grads[0],), cost_us=1.0, name="pool_plane",
    )
    fars = [xor_permute({1: near, 2: pooled, 3: pooled3}[n], n * PLANE) for n in ORDER]
    if top_rounds > 0:
        got = dict(zip(ORDER, fars))
        span = pool_both(join_both([pooled, pool_both(got[1]), got[2], got[3]]))
        for n in range(top_rounds):
            fars.append(xor_permute(span, 4 * PLANE << n))
            span = pool_both(join_both([span, fars[-1]]))
    far_rows = sum(far.shape[0] for far in fars[1:]) // 2
    heads, tokens = width // DH, PLANE * rows
    near_rows = 3 * rows + fars[0].shape[0] // 2
    weights, dots, sums, stats, near_keys = call(
        near_kernel,
        [shape(heads, near_rows, tokens, t=F32)] * 2
        + [shape(heads, DH, tokens, t=F32), shape(heads, 2, tokens, t=F32)]
        + [shape(2 * heads, near_rows, DH)],
        *key_values, *query_grads, fars[0], planes=((0, OKV), (PLANE, OQG)), cost_us=2.0, name="near_attention",
    )
    results = call(
        lambda *refs: far_grad_kernel(len(fars) - 1, *refs),
        blocks + [shape(heads, far_rows, tokens), shape(heads, 2, tokens, t=F32)]
        + [shape(*far.shape) for far in fars],
        *query_grads, *fars[1:], weights, dots, sums, stats, planes=((0, OQG),), cost_us=2.0, name="far_attention",
    )
    ads, kept, far_grads = results[:PLANE], results[PLANE : PLANE + 2], list(results[PLANE + 2 :])
    first = PLANE + len(fars) + 4
    results = call(
        lambda *refs: plane_kernel(len(fars) - 1, *refs),
        blocks + [shape(2 * rows, width, t=F32)] * PLANE,
        *query_grads, *fars[1:], near_keys, weights, dots, *kept, *ads,
        aliases={first + r: r for r in range(PLANE)}, cost_us=2.3, name="plane_grads",
    )
    att_dq, dkv = results[:PLANE], results[PLANE:]
    extra = []
    if top_rounds > 0:
        up = None
        for n in reversed(range(top_rounds)):
            send = far_grads[3 + n].astype(F32)
            if up is not None:
                own_up, their_up = part_both(spread_both(up), 2)
                send = send + their_up
            back = xor_permute(send.astype(BF16), 4 * PLANE << n).astype(F32)
            up = back if up is None else back + own_up
        ups = part_both(spread_both(up), PLANE)
        extra = [ups[0].astype(BF16)]
        ups[1] = spread_both(ups[1])
        for at, n in enumerate(ORDER):
            far_grads[at] = (far_grads[at].astype(F32) + ups[n]).astype(BF16)
    backs = [xor_permute(far_grads[at], n * PLANE) for at, n in enumerate(ORDER)]
    att_dq = plane_exchange(att_dq)
    dkv = call(carry_kernel, blocks, *dkv, *backs, *extra, cost_us=5.0, name="carry")
    own_sum, *other_sum = call(
        output_kernel,
        [shape(rows, features, t=F32)] + [shape(rows // PIECES, features)] * PIECES,
        *att_dq, out_weight, planes=((0, OAD),), after=(dkv[0],), cost_us=0.01, name="project",
    )
    dkv = plane_exchange(dkv)
    other_sum = [xor_permute(piece, 1, "head") for piece in other_sum]
    output, grad_queries, grad_keys, grad_values = call(
        join_kernel, [shape(rows, features)] * 4, own_sum, *other_sum, *att_dq, *dkv, planes=((1 + PIECES, OAD), (1 + PIECES + PLANE, ODKV)),
        hbm_out=True, scratch=[pltpu.VMEM((rows, features), BF16), dma(3 * PLANE + 1)],
        cost_us=1.0, name="join",
    )
    return (output, grad_queries, grad_keys, grad_values)


def solution(mesh):
    rows = P("ctx", "head")
    return jax.shard_map(
        body,
        mesh=mesh,
        in_specs=(rows, rows, rows, P("head", None), rows),
        out_specs=(rows, rows, rows, rows),
        check_vma=False,
    )
```

```python
import jax
import jax.numpy as jnp
from jax import lax
from jax.experimental import pallas as pl
from jax.experimental.pallas import tpu as pltpu
from jax.sharding import PartitionSpec as P

DH = 128
PLANE = 4
PIECES = 2
OKV = (3, 1, 2, 0)
OQG = (2, 1, 3, 0)
OAD = (3, 1, 2, 0)
ODKV = (2, 3, 1, 0)
ORDER = (1, 2, 3)
SCALE = DH ** (-0.5)
SCALE2 = SCALE * 1.4426950408889634
BF16 = jnp.bfloat16
F32 = jnp.float32


def xor_permute(block, mask, axis="ctx"):
    count = lax.axis_size(axis)
    return lax.ppermute(block, axis, [(i, i ^ mask) for i in range(count)])


def dot(a, b, contract_a=1, contract_b=0):
    return lax.dot_general(
        a, b, (((contract_a,), (contract_b,)), ((), ())), preferred_element_type=F32
    )


def pool_matrix(rows):
    out = lax.broadcasted_iota(jnp.int32, (rows // 2, rows), 0)
    src = lax.broadcasted_iota(jnp.int32, (rows // 2, rows), 1)
    return jnp.where(src // 2 == out, 0.5, 0.0).astype(BF16)


def spread_matrix(rows, times):
    out = lax.broadcasted_iota(jnp.int32, (rows * times, rows), 0)
    src = lax.broadcasted_iota(jnp.int32, (rows * times, rows), 1)
    return jnp.where(out // times == src, 1.0 / times, 0.0).astype(BF16)


def pool(block):
    return dot(pool_matrix(block.shape[0]), block).astype(BF16)


def spread(block, times):
    return dot(spread_matrix(block.shape[0], times), block.astype(BF16))


def call(kernel, outs, *args, planes=(), after=(), aliases={}, hbm=(), hbm_out=False, scratch=(), cost_us=1.0, name=None):
    vmem = pl.BlockSpec(memory_space=pltpu.VMEM)
    in_hbm = pl.BlockSpec(memory_space=pltpu.HBM)
    space = pltpu.HBM if hbm_out else pltpu.VMEM
    args = [
        pltpu.with_memory_space_constraint(a, pltpu.HBM) if n in hbm else a
        for n, a in enumerate(args)
    ]
    count = len(args)
    order = list(range(count))
    for first in planes:
        order[first[0] : first[0] + PLANE] = [first[0] + r for r in first[1]]
    places = [order.index(n) for n in range(count)]

    def run(*refs):
        kernel(*[refs[at] for at in places], *refs[count + len(after) :])

    return pl.pallas_call(
        run,
        out_shape=[space(out.shape, out.dtype) for out in outs],
        in_specs=[in_hbm if n in hbm else vmem for n in order]
        + [pl.BlockSpec(memory_space=pl.ANY)] * len(after),
        scratch_shapes=scratch,
        input_output_aliases={places[n]: out for n, out in aliases.items()},
        out_specs=[in_hbm if hbm_out else vmem] * len(outs),
        compiler_params=pltpu.CompilerParams(vmem_limit_bytes=24 * 1024 * 1024),
        cost_estimate=pl.CostEstimate(
            flops=int(cost_us * 1e9), bytes_accessed=0, transcendentals=0
        ),
        name=name,
    )(*[args[n] for n in order], *after)


def part(n, width):
    return slice(n * width, (n + 1) * width)


def start_all(pairs, sems):
    copies = [pltpu.make_async_copy(a, b, sems.at[n]) for n, (a, b) in enumerate(pairs)]
    for copy in copies:
        copy.start()
    return copies


def columns(r, width):
    place = (lax.axis_index("ctx") & (PLANE - 1)) ^ r
    return pl.ds(pl.multiple_of(place * width, width), width)


def key_value_kernel(k_ref, v_ref, *refs):
    outs, sems = refs[:-1], refs[-1]
    rows, width = k_ref.shape[0], k_ref.shape[1] // PLANE
    pairs = []
    for r, out in enumerate(outs, 1):
        pairs.append((k_ref.at[:, columns(r, width)], out.at[part(0, rows), :]))
        pairs.append((v_ref.at[:, columns(r, width)], out.at[part(1, rows), :]))
    for copy in start_all(pairs, sems):
        copy.wait()


def cotangent_kernel(q_ref, own_ref, other_ref, w_ref, k_ref, v_ref, *refs):
    outs, kv_out, sems = refs[:PLANE], refs[PLANE], refs[PLANE + 1]
    mine = columns(0, w_ref.shape[0] // PLANE)
    copies = start_all(
        [(ref.at[:, mine], kv_out.at[part(m, q_ref.shape[0]), :]) for m, ref in enumerate((k_ref, v_ref))],
        sems,
    )
    rows, width = q_ref.shape[0], q_ref.shape[1] // PLANE
    half = own_ref.shape[1]
    head = lax.axis_index("head")
    own_at = pl.ds(pl.multiple_of(head * half, half), half)
    other_at = pl.ds(pl.multiple_of((1 - head) * half, half), half)
    for r in range(PLANE):
        here = columns(r, width)
        outs[r][:rows, :] = q_ref[:, here]
        outs[r][rows:, :] = (
            dot(own_ref[...], w_ref[here, own_at], 1, 1)
            + dot(other_ref[...], w_ref[here, other_at], 1, 1)
        ).astype(BF16)
    for copy in copies:
        copy.wait()


def average_matrix(rows, times):
    out = lax.broadcasted_iota(jnp.int32, (rows // times, rows), 0)
    src = lax.broadcasted_iota(jnp.int32, (rows // times, rows), 1)
    return jnp.where(src // times == out, 1.0 / times, 0.0).astype(BF16)


def far_kernel(*refs):
    kvs, outs = refs[:PLANE], refs[PLANE:]
    rows, width = kvs[0].shape[0] // 2, kvs[0].shape[1]
    wide = jnp.concatenate([kv[part(m, rows), :] for m in range(2) for kv in kvs], 1)
    pooled = dot(
        jnp.concatenate([average_matrix(rows, 4), average_matrix(rows, 8)], 0), wide
    ).astype(BF16)
    for out, first, size in zip(outs, (0, rows // 4, rows // 4), (rows // 4, rows // 8, rows // 8)):
        for n in range(2 * PLANE):
            out[part(n, size), :] = pooled[first : first + size, part(n, width)]


def both(blocks, p, rows, lanes):
    return jnp.concatenate([blocks[r][rows, lanes] for r in (2 * p, 2 * p + 1)], 0)


def near_set(kvs, p, lanes, m):
    rows = part(m, kvs[0].shape[0] // 2)
    other = [pool(kv[rows, lanes]) for kv in kvs[2 - 2 * p : 4 - 2 * p]]
    return jnp.concatenate([both(kvs, p, rows, lanes)] + other, 0)


def far_set(fars, lanes, m):
    return jnp.concatenate([far[part(m, far.shape[0] // 2), lanes] for far in fars], 0)


def token_rows(qgs, m, lanes):
    rows = part(m, qgs[0].shape[0] // 2)
    return jnp.concatenate([qg[rows, lanes] for qg in qgs], 0)


def near_kernel(*refs):
    kvs, qgs, first = refs[:PLANE], refs[PLANE : 2 * PLANE], refs[2 * PLANE]
    weight_out, dots_out, sums_out, stats_out, keys_out, turned_out = refs[2 * PLANE + 1 :]
    rows, width = qgs[0].shape[0] // 2, qgs[0].shape[1]
    cases = [(h, p) for h in range(width // DH) for p in range(2)]
    tokens = [part(p, 2 * rows) for h, p in cases]
    keys, values = [
        [
            jnp.concatenate(
                [near_set(kvs, p, part(h, DH), m), first[part(m, first.shape[0] // 2), part(h, DH)]], 0
            )
            for h, p in cases
        ]
        for m in range(2)
    ]
    scores = [
        dot(k, both(qgs, p, part(0, rows), part(h, DH)), 1, 1) * SCALE2
        for k, (h, p) in zip(keys, cases)
    ]
    for (h, p), v, t in zip(cases, values, tokens):
        dots_out[h, :, t] = dot(v, both(qgs, p, part(1, rows), part(h, DH)), 1, 1)
    for n, ((h, p), t) in enumerate(zip(cases, tokens)):
        row_max = jnp.max(scores[n], 0, keepdims=True)
        weights = jnp.exp2(scores[n] - row_max)
        weight_out[h, :, t] = weights
        sums_out[h, :, t] = dot(values[n], weights.astype(BF16), 0, 0)
        stats_out[h, 0:1, t] = row_max
        stats_out[h, 1:2, t] = jnp.sum(weights, 0, keepdims=True)
        keys_out[n] = keys[n]
        turned_out[h, :, t] = both(qgs, p, part(1, rows), part(h, DH)).T


def far_grad_kernel(n_far, *refs):
    qgs, fars = refs[:PLANE], refs[PLANE : PLANE + n_far]
    weight_ref, dots_ref, sums_ref, stats_ref, turned_ref = refs[PLANE + n_far : PLANE + n_far + 5]
    outs = refs[PLANE + n_far + 5 :]
    ads, grad_out, stats_out, far_out = outs[:PLANE], outs[PLANE], outs[PLANE + 1], outs[PLANE + 2 :]
    rows, width = qgs[0].shape[0] // 2, qgs[0].shape[1]
    first = slice(3 * rows, weight_ref.shape[1])
    first_rows = weight_ref.shape[1] - 3 * rows
    heads = range(width // DH)
    lanes = [part(h, DH) for h in heads]
    queries = [token_rows(qgs, 0, at) for at in lanes]
    grads = [token_rows(qgs, 1, at) for at in lanes]
    keys = [far_set(fars, at, 0) for at in lanes]
    values = [far_set(fars, at, 1) for at in lanes]
    scores = [dot(k, q, 1, 1) * SCALE2 for k, q in zip(keys, queries)]
    dots = [dot(v, g, 1, 1) for v, g in zip(values, grads)]
    weights, near_parts, inverses, sums = [], [], [], []
    for h in heads:
        near_max = stats_ref[h, 0:1, :]
        row_max = jnp.maximum(near_max, jnp.max(scores[h], 0, keepdims=True))
        weights.append(jnp.exp2(scores[h] - row_max))
        near_parts.append(jnp.exp2(near_max - row_max))
        sums.append(dot(values[h], weights[h].astype(BF16), 0, 0))
        inverses.append(
            1.0 / (stats_ref[h, 1:2, :] * near_parts[h] + jnp.sum(weights[h], 0, keepdims=True))
        )
    score_grads, probs = [], []
    for h in heads:
        attended = ((sums_ref[h] * near_parts[h] + sums[h]) * inverses[h]).astype(BF16)
        delta = jnp.sum(turned_ref[h].astype(F32) * attended.astype(F32), 0, keepdims=True)
        near_scale = near_parts[h] * inverses[h]
        near_probs = weight_ref[h, first, :] * near_scale
        far_probs = weights[h] * inverses[h]
        score_grads.append(
            jnp.concatenate(
                [
                    (near_probs * (dots_ref[h, first, :] - delta)).astype(BF16),
                    (far_probs * (dots[h] - delta)).astype(BF16),
                ],
                0,
            )
        )
        probs.append(jnp.concatenate([near_probs.astype(BF16), far_probs.astype(BF16)], 0))
        grad_out[h] = score_grads[h][first_rows:]
        stats_out[h, 0:1, :] = near_scale
        stats_out[h, 1:2, :] = delta
        attended = attended.T
        for r in range(PLANE):
            ads[r][:rows, lanes[h]] = attended[part(r, rows)]
    for h in heads:
        for m, whole in enumerate(
            (dot(score_grads[h], queries[h]) * SCALE, dot(probs[h], grads[h]))
        ):
            at = 0
            for far in far_out:
                size = far.shape[0] // 2
                far[part(m, size), lanes[h]] = whole[at : at + size].astype(BF16)
                at += size


def plane_kernel(n_far, *refs):
    qgs, fars = refs[:PLANE], refs[PLANE : PLANE + n_far]
    keys_ref, weight_ref, dots_ref, grad_ref, stats_ref = refs[PLANE + n_far : PLANE + n_far + 5]
    refs = refs[2 * PLANE + n_far + 5 :]
    ads, dkvs = refs[:PLANE], refs[PLANE:]
    rows, width = qgs[0].shape[0] // 2, qgs[0].shape[1]
    pair = 2 * rows
    cases = [(h, p) for h in range(width // DH) for p in range(2)]
    score_grads, probs = [], []
    for h, p in cases:
        tokens = part(p, pair)
        probabilities = weight_ref[h, :, tokens] * stats_ref[h, 0:1, tokens]
        probs.append(probabilities.astype(BF16))
        score_grads.append(
            (probabilities * (dots_ref[h, :, tokens] - stats_ref[h, 1:2, tokens])).astype(BF16)
        )
    for n, (h, p) in enumerate(cases):
        far_keys = far_set(fars, part(h, DH), 0)
        dq = dot(keys_ref[n], score_grads[n], 0, 0)
        dq = dq + dot(far_keys, grad_ref[h, :, part(p, pair)], 0, 0)
        dq = (dq * SCALE).astype(BF16).T
        for k in range(2):
            ads[2 * p + k][rows:, part(h, DH)] = dq[part(k, rows)]
    grads = []
    for n, (h, p) in enumerate(cases):
        q, g = [both(qgs, p, part(m, rows), part(h, DH)) for m in range(2)]
        near = slice(0, 3 * rows)
        grads.append((dot(score_grads[n][near], q) * SCALE, dot(probs[n][near], g)))
    places = [
        (h, m, p, k) for h in range(width // DH) for m in range(2) for p in range(2) for k in range(2)
    ]
    pooled = [
        grads[2 * h + 1 - p][m][pair + k * rows // 2 : pair + (k + 1) * rows // 2]
        for h, m, p, k in places
    ]
    carried = spread(jnp.concatenate(pooled, 1), 2)
    for n, (h, m, p, k) in enumerate(places):
        dkvs[2 * p + k][part(m, rows), part(h, DH)] = (
            grads[2 * h + p][m][part(k, rows)] + carried[:, part(n, DH)]
        )


def carry_kernel(*refs):
    dkvs, far_refs, outs = refs[:PLANE], refs[PLANE:-PLANE], refs[-PLANE:]
    rows, width = dkvs[0].shape[0] // 2, dkvs[0].shape[1]
    wide, matrix = [], []
    for far in far_refs:
        size = far.shape[0] // (2 * PLANE)
        wide.append(jnp.concatenate([far[part(n, size), :] for n in range(2 * PLANE)], 1))
        matrix.append(spread_matrix(size, rows // size))
    carried = dot(jnp.concatenate(matrix, 1), jnp.concatenate(wide, 0))
    for n in range(2 * PLANE):
        m, r = divmod(n, PLANE)
        outs[r][part(m, rows), :] = (
            dkvs[r][part(m, rows), :] + carried[:, part(n, width)]
        ).astype(BF16)


def output_kernel(*refs):
    ads, w_ref, own_out, others = refs[:PLANE], refs[PLANE], refs[PLANE + 1], refs[PLANE + 2 :]
    rows, width = ads[0].shape[0] // 2, ads[0].shape[1]
    half = own_out.shape[1]
    head = lax.axis_index("head")
    total = None
    for r in range(PLANE):
        term = dot(ads[r][:rows, :], w_ref[columns(r, width), :])
        total = term if total is None else total + term

    def write(own, other):
        own_out[...] = own
        for n, out in enumerate(others):
            out[...] = other[part(n, rows // PIECES)].astype(BF16)

    @pl.when(head == 0)
    def _():
        write(total[:, :half], total[:, half:])

    @pl.when(head == 1)
    def _():
        write(total[:, half:], total[:, :half])


def join_kernel(own_ref, *refs):
    others, refs = refs[:PIECES], refs[PIECES:]
    ads, dkvs = refs[:PLANE], refs[PLANE : 2 * PLANE]
    o_out, gq_out, gk_out, gv_out, total, sems = refs[2 * PLANE :]
    rows, width = ads[0].shape[0] // 2, ads[0].shape[1]
    pairs = []
    for r in range(PLANE):
        here = columns(r, width)
        pairs.append((dkvs[r].at[part(0, rows), :], gk_out.at[:, here]))
        pairs.append((dkvs[r].at[part(1, rows), :], gv_out.at[:, here]))
        pairs.append((ads[r].at[part(1, rows), :], gq_out.at[:, here]))
    copies = start_all(pairs, sems)
    for n, other in enumerate(others):
        piece = part(n, rows // PIECES)
        total[piece, :] = (own_ref[piece, :] + other[...].astype(F32)).astype(BF16)
    last = pltpu.make_async_copy(total, o_out, sems.at[len(pairs)])
    last.start()
    for copy in copies + [last]:
        copy.wait()


def plane_exchange(blocks):
    return [blocks[0]] + [xor_permute(blocks[r], r) for r in range(1, PLANE)]


def pool_both(block):
    shaped = block.reshape((2, block.shape[0] // 4, 2) + block.shape[1:]).astype(F32)
    return ((shaped[:, :, 0] + shaped[:, :, 1]) * 0.5).astype(BF16).reshape(
        (block.shape[0] // 2,) + block.shape[1:]
    )


def spread_both(block):
    halved = block.astype(F32) * 0.5
    return jnp.repeat(halved, 2, axis=0)


def join_both(blocks):
    halves = [b.reshape((2, b.shape[0] // 2) + b.shape[1:]) for b in blocks]
    joined = jnp.concatenate(halves, 1)
    return joined.reshape((-1,) + joined.shape[2:])


def part_both(block, parts):
    shaped = block.reshape((2, parts, block.shape[0] // (2 * parts)) + block.shape[1:])
    return [shaped[:, n].reshape((-1,) + block.shape[1:]) for n in range(parts)]


def body(queries, key_rows, value_rows, out_weight, cotangent):
    rows, features = queries.shape
    width = features // PLANE
    top_rounds = lax.axis_size("ctx").bit_length() - 1 - 4
    shape = lambda *dims, t=BF16: jax.ShapeDtypeStruct(dims, t)
    dma = lambda n: pltpu.SemaphoreType.DMA((n,))
    blocks = [shape(2 * rows, width)] * PLANE

    other_cotangent = xor_permute(cotangent, 1, "head")
    key_values = call(
        key_value_kernel, blocks[1:], key_rows, value_rows,
        hbm=(0, 1), scratch=[dma(2 * PLANE - 2)], cost_us=8, name="pack_keys_values",
    )
    *query_grads, own_keys_values = call(
        cotangent_kernel, blocks + blocks[:1], queries, cotangent, other_cotangent, out_weight,
        key_rows, value_rows, hbm=(4, 5), scratch=[dma(2)], cost_us=3.0, name="grad_attended",
    )
    key_values = plane_exchange([own_keys_values, *key_values])
    query_grads = plane_exchange(query_grads)
    near, pooled, pooled3 = call(
        far_kernel, [shape(2 * rows, width)] + [shape(rows, width)] * 2, *key_values, planes=((0, OKV),),
        after=(query_grads[0],), cost_us=1.0, name="pool_plane",
    )
    fars = [xor_permute({1: near, 2: pooled, 3: pooled3}[n], n * PLANE) for n in ORDER]
    if top_rounds > 0:
        got = dict(zip(ORDER, fars))
        span = pool_both(join_both([pooled, pool_both(got[1]), got[2], got[3]]))
        for n in range(top_rounds):
            fars.append(xor_permute(span, 4 * PLANE << n))
            span = pool_both(join_both([span, fars[-1]]))
    far_rows = sum(far.shape[0] for far in fars[1:]) // 2
    heads, tokens = width // DH, PLANE * rows
    near_rows = 3 * rows + fars[0].shape[0] // 2
    weights, dots, sums, stats, near_keys, turned = call(
        near_kernel,
        [shape(heads, near_rows, tokens, t=F32)] * 2
        + [shape(heads, DH, tokens, t=F32), shape(heads, 2, tokens, t=F32)]
        + [shape(2 * heads, near_rows, DH), shape(heads, DH, tokens)],
        *key_values, *query_grads, fars[0], planes=((0, OKV), (PLANE, OQG)), cost_us=2.0, name="near_attention",
    )
    results = call(
        lambda *refs: far_grad_kernel(len(fars) - 1, *refs),
        blocks + [shape(heads, far_rows, tokens), shape(heads, 2, tokens, t=F32)]
        + [shape(*far.shape) for far in fars],
        *query_grads, *fars[1:], weights, dots, sums, stats, turned, planes=((0, OQG),), cost_us=2.0, name="far_attention",
    )
    ads, kept, far_grads = results[:PLANE], results[PLANE : PLANE + 2], list(results[PLANE + 2 :])
    first = PLANE + len(fars) + 4
    results = call(
        lambda *refs: plane_kernel(len(fars) - 1, *refs),
        blocks + [shape(2 * rows, width, t=F32)] * PLANE,
        *query_grads, *fars[1:], near_keys, weights, dots, *kept, *ads,
        aliases={first + r: r for r in range(PLANE)}, cost_us=2.3, name="plane_grads",
    )
    att_dq, dkv = results[:PLANE], results[PLANE:]
    extra = []
    if top_rounds > 0:
        up = None
        for n in reversed(range(top_rounds)):
            send = far_grads[3 + n].astype(F32)
            if up is not None:
                own_up, their_up = part_both(spread_both(up), 2)
                send = send + their_up
            back = xor_permute(send.astype(BF16), 4 * PLANE << n).astype(F32)
            up = back if up is None else back + own_up
        ups = part_both(spread_both(up), PLANE)
        extra = [ups[0].astype(BF16)]
        ups[1] = spread_both(ups[1])
        for at, n in enumerate(ORDER):
            far_grads[at] = (far_grads[at].astype(F32) + ups[n]).astype(BF16)
    backs = [xor_permute(far_grads[at], n * PLANE) for at, n in enumerate(ORDER)]
    att_dq = plane_exchange(att_dq)
    dkv = call(carry_kernel, blocks, *dkv, *backs[1:], backs[0], *extra, cost_us=5.0, name="carry")
    own_sum, *other_sum = call(
        output_kernel,
        [shape(rows, features, t=F32)] + [shape(rows // PIECES, features)] * PIECES,
        *att_dq, out_weight, planes=((0, OAD),), after=(dkv[0],), cost_us=0.01, name="project",
    )
    dkv = plane_exchange(dkv)
    other_sum = [xor_permute(piece, 1, "head") for piece in other_sum]
    output, grad_queries, grad_keys, grad_values = call(
        join_kernel, [shape(rows, features)] * 4, own_sum, *other_sum, *att_dq, *dkv, planes=((1 + PIECES, OAD), (1 + PIECES + PLANE, ODKV)),
        hbm_out=True, scratch=[pltpu.VMEM((rows, features), BF16), dma(3 * PLANE + 1)],
        cost_us=1.0, name="join",
    )
    return (output, grad_queries, grad_keys, grad_values)


def solution(mesh):
    rows = P("ctx", "head")
    return jax.shard_map(
        body,
        mesh=mesh,
        in_specs=(rows, rows, rows, P("head", None), rows),
        out_specs=(rows, rows, rows, rows),
        check_vma=False,
    )
```

```python
import jax
import jax.numpy as jnp
from jax import lax
from jax.experimental import pallas as pl
from jax.experimental.pallas import tpu as pltpu
from jax.sharding import PartitionSpec as P

DH = 128
PLANE = 4
PIECES = 2
OKV = (3, 1, 2, 0)
OQG = (2, 1, 3, 0)
OAD = (3, 1, 2, 0)
ODKV = (2, 3, 1, 0)
ORDER = (1, 2, 3)
SCALE = DH ** (-0.5)
SCALE2 = SCALE * 1.4426950408889634
BF16 = jnp.bfloat16
F32 = jnp.float32


def xor_permute(block, mask, axis="ctx"):
    count = lax.axis_size(axis)
    return lax.ppermute(block, axis, [(i, i ^ mask) for i in range(count)])


def dot(a, b, contract_a=1, contract_b=0):
    return lax.dot_general(
        a, b, (((contract_a,), (contract_b,)), ((), ())), preferred_element_type=F32
    )


def pool_matrix(rows):
    out = lax.broadcasted_iota(jnp.int32, (rows // 2, rows), 0)
    src = lax.broadcasted_iota(jnp.int32, (rows // 2, rows), 1)
    return jnp.where(src // 2 == out, 0.5, 0.0).astype(BF16)


def spread_matrix(rows, times):
    out = lax.broadcasted_iota(jnp.int32, (rows * times, rows), 0)
    src = lax.broadcasted_iota(jnp.int32, (rows * times, rows), 1)
    return jnp.where(out // times == src, 1.0 / times, 0.0).astype(BF16)


def pool(block):
    return dot(pool_matrix(block.shape[0]), block).astype(BF16)


def spread(block, times):
    return dot(spread_matrix(block.shape[0], times), block.astype(BF16))


def call(kernel, outs, *args, planes=(), after=(), aliases={}, hbm=(), hbm_out=False, scratch=(), cost_us=1.0, name=None):
    vmem = pl.BlockSpec(memory_space=pltpu.VMEM)
    in_hbm = pl.BlockSpec(memory_space=pltpu.HBM)
    out_hbm = range(len(outs)) if hbm_out is True else hbm_out or ()
    args = [
        pltpu.with_memory_space_constraint(a, pltpu.HBM) if n in hbm else a
        for n, a in enumerate(args)
    ]
    count = len(args)
    order = list(range(count))
    for first in planes:
        order[first[0] : first[0] + PLANE] = [first[0] + r for r in first[1]]
    places = [order.index(n) for n in range(count)]

    def run(*refs):
        kernel(*[refs[at] for at in places], *refs[count + len(after) :])

    return pl.pallas_call(
        run,
        out_shape=[
            (pltpu.HBM if n in out_hbm else pltpu.VMEM)(out.shape, out.dtype)
            for n, out in enumerate(outs)
        ],
        in_specs=[in_hbm if n in hbm else vmem for n in order]
        + [pl.BlockSpec(memory_space=pl.ANY)] * len(after),
        scratch_shapes=scratch,
        input_output_aliases={places[n]: out for n, out in aliases.items()},
        out_specs=[in_hbm if n in out_hbm else vmem for n in range(len(outs))],
        compiler_params=pltpu.CompilerParams(vmem_limit_bytes=24 * 1024 * 1024),
        cost_estimate=pl.CostEstimate(
            flops=int(cost_us * 1e9), bytes_accessed=0, transcendentals=0
        ),
        name=name,
    )(*[args[n] for n in order], *after)


def part(n, width):
    return slice(n * width, (n + 1) * width)


def start_all(pairs, sems):
    copies = [pltpu.make_async_copy(a, b, sems.at[n]) for n, (a, b) in enumerate(pairs)]
    for copy in copies:
        copy.start()
    return copies


def columns(r, width):
    place = (lax.axis_index("ctx") & (PLANE - 1)) ^ r
    return pl.ds(pl.multiple_of(place * width, width), width)


def key_value_kernel(k_ref, v_ref, *refs):
    outs, sems = refs[:-1], refs[-1]
    rows, width = k_ref.shape[0], k_ref.shape[1] // PLANE
    pairs = []
    for r, out in enumerate(outs, 1):
        pairs.append((k_ref.at[:, columns(r, width)], out.at[part(0, rows), :]))
        pairs.append((v_ref.at[:, columns(r, width)], out.at[part(1, rows), :]))
    for copy in start_all(pairs, sems):
        copy.wait()


def cotangent_kernel(q_ref, own_ref, other_ref, w_ref, k_ref, v_ref, *refs):
    outs, kv_out, sems = refs[:PLANE], refs[PLANE], refs[PLANE + 1]
    mine = columns(0, w_ref.shape[0] // PLANE)
    copies = start_all(
        [(ref.at[:, mine], kv_out.at[part(m, q_ref.shape[0]), :]) for m, ref in enumerate((k_ref, v_ref))],
        sems,
    )
    rows, width = q_ref.shape[0], q_ref.shape[1] // PLANE
    half = own_ref.shape[1]
    head = lax.axis_index("head")
    own_at = pl.ds(pl.multiple_of(head * half, half), half)
    other_at = pl.ds(pl.multiple_of((1 - head) * half, half), half)
    for r in range(PLANE):
        here = columns(r, width)
        outs[r][:rows, :] = q_ref[:, here]
        outs[r][rows:, :] = (
            dot(own_ref[...], w_ref[here, own_at], 1, 1)
            + dot(other_ref[...], w_ref[here, other_at], 1, 1)
        ).astype(BF16)
    for copy in copies:
        copy.wait()


def average_matrix(rows, times):
    out = lax.broadcasted_iota(jnp.int32, (rows // times, rows), 0)
    src = lax.broadcasted_iota(jnp.int32, (rows // times, rows), 1)
    return jnp.where(src // times == out, 1.0 / times, 0.0).astype(BF16)


def far_kernel(*refs):
    kvs, outs = refs[:PLANE], refs[PLANE:]
    rows, width = kvs[0].shape[0] // 2, kvs[0].shape[1]
    wide = jnp.concatenate([kv[part(m, rows), :] for m in range(2) for kv in kvs], 1)
    pooled = dot(
        jnp.concatenate([average_matrix(rows, 4), average_matrix(rows, 8)], 0), wide
    ).astype(BF16)
    for out, first, size in zip(outs, (0, rows // 4, rows // 4), (rows // 4, rows // 8, rows // 8)):
        for n in range(2 * PLANE):
            out[part(n, size), :] = pooled[first : first + size, part(n, width)]


def both(blocks, p, rows, lanes):
    return jnp.concatenate([blocks[r][rows, lanes] for r in (2 * p, 2 * p + 1)], 0)


def near_set(kvs, p, lanes, m):
    rows = part(m, kvs[0].shape[0] // 2)
    other = [pool(kv[rows, lanes]) for kv in kvs[2 - 2 * p : 4 - 2 * p]]
    return jnp.concatenate([both(kvs, p, rows, lanes)] + other, 0)


def far_set(fars, lanes, m):
    return jnp.concatenate([far[part(m, far.shape[0] // 2), lanes] for far in fars], 0)


def token_rows(qgs, m, lanes):
    rows = part(m, qgs[0].shape[0] // 2)
    return jnp.concatenate([qg[rows, lanes] for qg in qgs], 0)


def near_kernel(*refs):
    kvs, qgs, first = refs[:PLANE], refs[PLANE : 2 * PLANE], refs[2 * PLANE]
    weight_out, dots_out, sums_out, stats_out, keys_out, turned_out = refs[2 * PLANE + 1 :]
    rows, width = qgs[0].shape[0] // 2, qgs[0].shape[1]
    cases = [(h, p) for h in range(width // DH) for p in range(2)]
    tokens = [part(p, 2 * rows) for h, p in cases]
    keys, values = [
        [
            jnp.concatenate(
                [near_set(kvs, p, part(h, DH), m), first[part(m, first.shape[0] // 2), part(h, DH)]], 0
            )
            for h, p in cases
        ]
        for m in range(2)
    ]
    scores = [
        dot(k, both(qgs, p, part(0, rows), part(h, DH)), 1, 1) * SCALE2
        for k, (h, p) in zip(keys, cases)
    ]
    for (h, p), v, t in zip(cases, values, tokens):
        dots_out[h, :, t] = dot(v, both(qgs, p, part(1, rows), part(h, DH)), 1, 1)
    for n, ((h, p), t) in enumerate(zip(cases, tokens)):
        row_max = jnp.max(scores[n], 0, keepdims=True)
        weights = jnp.exp2(scores[n] - row_max)
        weight_out[h, :, t] = weights
        sums_out[h, :, t] = dot(values[n], weights.astype(BF16), 0, 0)
        stats_out[h, 0:1, t] = row_max
        stats_out[h, 1:2, t] = jnp.sum(weights, 0, keepdims=True)
        keys_out[n] = keys[n]
        turned_out[h, :, t] = both(qgs, p, part(1, rows), part(h, DH)).T


def far_grad_kernel(n_far, *refs):
    qgs, fars = refs[:PLANE], refs[PLANE : PLANE + n_far]
    weight_ref, dots_ref, sums_ref, stats_ref, turned_ref = refs[PLANE + n_far : PLANE + n_far + 5]
    outs = refs[PLANE + n_far + 5 :]
    ads, grad_out, stats_out, far_out = outs[:PLANE], outs[PLANE], outs[PLANE + 1], outs[PLANE + 2 :]
    rows, width = qgs[0].shape[0] // 2, qgs[0].shape[1]
    first = slice(3 * rows, weight_ref.shape[1])
    first_rows = weight_ref.shape[1] - 3 * rows
    heads = range(width // DH)
    lanes = [part(h, DH) for h in heads]
    queries = [token_rows(qgs, 0, at) for at in lanes]
    grads = [token_rows(qgs, 1, at) for at in lanes]
    keys = [far_set(fars, at, 0) for at in lanes]
    values = [far_set(fars, at, 1) for at in lanes]
    scores = [dot(k, q, 1, 1) * SCALE2 for k, q in zip(keys, queries)]
    dots = [dot(v, g, 1, 1) for v, g in zip(values, grads)]
    weights, near_parts, inverses, sums = [], [], [], []
    for h in heads:
        near_max = stats_ref[h, 0:1, :]
        row_max = jnp.maximum(near_max, jnp.max(scores[h], 0, keepdims=True))
        weights.append(jnp.exp2(scores[h] - row_max))
        near_parts.append(jnp.exp2(near_max - row_max))
        sums.append(dot(values[h], weights[h].astype(BF16), 0, 0))
        inverses.append(
            1.0 / (stats_ref[h, 1:2, :] * near_parts[h] + jnp.sum(weights[h], 0, keepdims=True))
        )
    score_grads, probs = [], []
    for h in heads:
        attended = ((sums_ref[h] * near_parts[h] + sums[h]) * inverses[h]).astype(BF16)
        delta = jnp.sum(turned_ref[h].astype(F32) * attended.astype(F32), 0, keepdims=True)
        near_scale = near_parts[h] * inverses[h]
        near_probs = weight_ref[h, first, :] * near_scale
        far_probs = weights[h] * inverses[h]
        score_grads.append(
            jnp.concatenate(
                [
                    (near_probs * (dots_ref[h, first, :] - delta)).astype(BF16),
                    (far_probs * (dots[h] - delta)).astype(BF16),
                ],
                0,
            )
        )
        probs.append(jnp.concatenate([near_probs.astype(BF16), far_probs.astype(BF16)], 0))
        grad_out[h] = score_grads[h][first_rows:]
        stats_out[h, 0:1, :] = near_scale
        stats_out[h, 1:2, :] = delta
        attended = attended.T
        for r in range(PLANE):
            ads[r][:rows, lanes[h]] = attended[part(r, rows)]
    for h in heads:
        for m, whole in enumerate(
            (dot(score_grads[h], queries[h]) * SCALE, dot(probs[h], grads[h]))
        ):
            at = 0
            for far in far_out:
                size = far.shape[0] // 2
                far[part(m, size), lanes[h]] = whole[at : at + size].astype(BF16)
                at += size


def plane_kernel(n_far, *refs):
    qgs, fars = refs[:PLANE], refs[PLANE : PLANE + n_far]
    keys_ref, weight_ref, dots_ref, grad_ref, stats_ref = refs[PLANE + n_far : PLANE + n_far + 5]
    refs = refs[2 * PLANE + n_far + 5 :]
    ads, dkvs = refs[:PLANE], refs[PLANE:]
    rows, width = qgs[0].shape[0] // 2, qgs[0].shape[1]
    pair = 2 * rows
    cases = [(h, p) for h in range(width // DH) for p in range(2)]
    score_grads, probs = [], []
    for h, p in cases:
        tokens = part(p, pair)
        probabilities = weight_ref[h, :, tokens] * stats_ref[h, 0:1, tokens]
        probs.append(probabilities.astype(BF16))
        score_grads.append(
            (probabilities * (dots_ref[h, :, tokens] - stats_ref[h, 1:2, tokens])).astype(BF16)
        )
    for n, (h, p) in enumerate(cases):
        far_keys = far_set(fars, part(h, DH), 0)
        dq = dot(keys_ref[n], score_grads[n], 0, 0)
        dq = dq + dot(far_keys, grad_ref[h, :, part(p, pair)], 0, 0)
        dq = (dq * SCALE).astype(BF16).T
        for k in range(2):
            ads[2 * p + k][rows:, part(h, DH)] = dq[part(k, rows)]
    grads = []
    for n, (h, p) in enumerate(cases):
        q, g = [both(qgs, p, part(m, rows), part(h, DH)) for m in range(2)]
        near = slice(0, 3 * rows)
        grads.append((dot(score_grads[n][near], q) * SCALE, dot(probs[n][near], g)))
    places = [
        (h, m, p, k) for h in range(width // DH) for m in range(2) for p in range(2) for k in range(2)
    ]
    pooled = [
        grads[2 * h + 1 - p][m][pair + k * rows // 2 : pair + (k + 1) * rows // 2]
        for h, m, p, k in places
    ]
    carried = spread(jnp.concatenate(pooled, 1), 2)
    for n, (h, m, p, k) in enumerate(places):
        dkvs[2 * p + k][part(m, rows), part(h, DH)] = (
            grads[2 * h + p][m][part(k, rows)] + carried[:, part(n, DH)]
        )


def carry_kernel(*refs):
    dkvs, far_refs, outs = refs[:PLANE], refs[PLANE:-PLANE], refs[-PLANE:]
    rows, width = dkvs[0].shape[0] // 2, dkvs[0].shape[1]
    wide, matrix = [], []
    for far in far_refs:
        size = far.shape[0] // (2 * PLANE)
        wide.append(jnp.concatenate([far[part(n, size), :] for n in range(2 * PLANE)], 1))
        matrix.append(spread_matrix(size, rows // size))
    carried = dot(jnp.concatenate(matrix, 1), jnp.concatenate(wide, 0))
    for n in range(2 * PLANE):
        m, r = divmod(n, PLANE)
        outs[r][part(m, rows), :] = (
            dkvs[r][part(m, rows), :] + carried[:, part(n, width)]
        ).astype(BF16)


def output_kernel(*refs):
    ads, w_ref, gq_out, own_out = refs[:PLANE], *refs[PLANE : PLANE + 3]
    others, sems = refs[PLANE + 3 : -1], refs[-1]
    rows, width = ads[0].shape[0] // 2, ads[0].shape[1]
    half = own_out.shape[1]
    head = lax.axis_index("head")
    copies = start_all(
        [(ads[r].at[part(1, rows), :], gq_out.at[:, columns(r, width)]) for r in range(PLANE)],
        sems,
    )
    total = None
    for r in range(PLANE):
        term = dot(ads[r][:rows, :], w_ref[columns(r, width), :])
        total = term if total is None else total + term

    def write(own, other):
        own_out[...] = own
        for n, out in enumerate(others):
            out[...] = other[part(n, rows // PIECES)].astype(BF16)

    @pl.when(head == 0)
    def _():
        write(total[:, :half], total[:, half:])

    @pl.when(head == 1)
    def _():
        write(total[:, half:], total[:, :half])

    for copy in copies:
        copy.wait()


def join_kernel(own_ref, *refs):
    others, refs = refs[:PIECES], refs[PIECES:]
    dkvs = refs[:PLANE]
    o_out, gk_out, gv_out, total, sems = refs[PLANE:]
    rows, width = dkvs[0].shape[0] // 2, dkvs[0].shape[1]
    pairs = []
    for r in range(PLANE):
        here = columns(r, width)
        pairs.append((dkvs[r].at[part(0, rows), :], gk_out.at[:, here]))
        pairs.append((dkvs[r].at[part(1, rows), :], gv_out.at[:, here]))
    copies = start_all(pairs, sems)
    for n, other in enumerate(others):
        piece = part(n, rows // PIECES)
        total[piece, :] = (own_ref[piece, :] + other[...].astype(F32)).astype(BF16)
    last = pltpu.make_async_copy(total, o_out, sems.at[len(pairs)])
    last.start()
    for copy in copies + [last]:
        copy.wait()


def plane_exchange(blocks):
    return [blocks[0]] + [xor_permute(blocks[r], r) for r in range(1, PLANE)]


def pool_both(block):
    shaped = block.reshape((2, block.shape[0] // 4, 2) + block.shape[1:]).astype(F32)
    return ((shaped[:, :, 0] + shaped[:, :, 1]) * 0.5).astype(BF16).reshape(
        (block.shape[0] // 2,) + block.shape[1:]
    )


def spread_both(block):
    halved = block.astype(F32) * 0.5
    return jnp.repeat(halved, 2, axis=0)


def join_both(blocks):
    halves = [b.reshape((2, b.shape[0] // 2) + b.shape[1:]) for b in blocks]
    joined = jnp.concatenate(halves, 1)
    return joined.reshape((-1,) + joined.shape[2:])


def part_both(block, parts):
    shaped = block.reshape((2, parts, block.shape[0] // (2 * parts)) + block.shape[1:])
    return [shaped[:, n].reshape((-1,) + block.shape[1:]) for n in range(parts)]


def body(queries, key_rows, value_rows, out_weight, cotangent):
    rows, features = queries.shape
    width = features // PLANE
    top_rounds = lax.axis_size("ctx").bit_length() - 1 - 4
    shape = lambda *dims, t=BF16: jax.ShapeDtypeStruct(dims, t)
    dma = lambda n: pltpu.SemaphoreType.DMA((n,))
    blocks = [shape(2 * rows, width)] * PLANE

    other_cotangent = xor_permute(cotangent, 1, "head")
    key_values = call(
        key_value_kernel, blocks[1:], key_rows, value_rows,
        hbm=(0, 1), scratch=[dma(2 * PLANE - 2)], cost_us=8, name="pack_keys_values",
    )
    *query_grads, own_keys_values = call(
        cotangent_kernel, blocks + blocks[:1], queries, cotangent, other_cotangent, out_weight,
        key_rows, value_rows, hbm=(4, 5), scratch=[dma(2)], cost_us=3.0, name="grad_attended",
    )
    key_values = plane_exchange([own_keys_values, *key_values])
    query_grads = plane_exchange(query_grads)
    near, pooled, pooled3 = call(
        far_kernel, [shape(2 * rows, width)] + [shape(rows, width)] * 2, *key_values, planes=((0, OKV),),
        after=(query_grads[0],), cost_us=1.0, name="pool_plane",
    )
    fars = [xor_permute({1: near, 2: pooled, 3: pooled3}[n], n * PLANE) for n in ORDER]
    if top_rounds > 0:
        got = dict(zip(ORDER, fars))
        span = pool_both(join_both([pooled, pool_both(got[1]), got[2], got[3]]))
        for n in range(top_rounds):
            fars.append(xor_permute(span, 4 * PLANE << n))
            span = pool_both(join_both([span, fars[-1]]))
    far_rows = sum(far.shape[0] for far in fars[1:]) // 2
    heads, tokens = width // DH, PLANE * rows
    near_rows = 3 * rows + fars[0].shape[0] // 2
    weights, dots, sums, stats, near_keys, turned = call(
        near_kernel,
        [shape(heads, near_rows, tokens, t=F32)] * 2
        + [shape(heads, DH, tokens, t=F32), shape(heads, 2, tokens, t=F32)]
        + [shape(2 * heads, near_rows, DH), shape(heads, DH, tokens)],
        *key_values, *query_grads, fars[0], planes=((0, OKV), (PLANE, OQG)), cost_us=2.0, name="near_attention",
    )
    results = call(
        lambda *refs: far_grad_kernel(len(fars) - 1, *refs),
        blocks + [shape(heads, far_rows, tokens), shape(heads, 2, tokens, t=F32)]
        + [shape(*far.shape) for far in fars],
        *query_grads, *fars[1:], weights, dots, sums, stats, turned, planes=((0, OQG),), cost_us=2.0, name="far_attention",
    )
    ads, kept, far_grads = results[:PLANE], results[PLANE : PLANE + 2], list(results[PLANE + 2 :])
    first = PLANE + len(fars) + 4
    results = call(
        lambda *refs: plane_kernel(len(fars) - 1, *refs),
        blocks + [shape(2 * rows, width, t=F32)] * PLANE,
        *query_grads, *fars[1:], near_keys, weights, dots, *kept, *ads,
        aliases={first + r: r for r in range(PLANE)}, cost_us=2.3, name="plane_grads",
    )
    att_dq, dkv = results[:PLANE], results[PLANE:]
    extra = []
    if top_rounds > 0:
        up = None
        for n in reversed(range(top_rounds)):
            send = far_grads[3 + n].astype(F32)
            if up is not None:
                own_up, their_up = part_both(spread_both(up), 2)
                send = send + their_up
            back = xor_permute(send.astype(BF16), 4 * PLANE << n).astype(F32)
            up = back if up is None else back + own_up
        ups = part_both(spread_both(up), PLANE)
        extra = [ups[0].astype(BF16)]
        ups[1] = spread_both(ups[1])
        for at, n in enumerate(ORDER):
            far_grads[at] = (far_grads[at].astype(F32) + ups[n]).astype(BF16)
    backs = [xor_permute(far_grads[at], n * PLANE) for at, n in enumerate(ORDER)]
    att_dq = plane_exchange(att_dq)
    dkv = call(carry_kernel, blocks, *dkv, *backs[1:], backs[0], *extra, cost_us=5.0, name="carry")
    grad_queries, own_sum, *other_sum = call(
        output_kernel,
        [shape(rows, features), shape(rows, features, t=F32)]
        + [shape(rows // PIECES, features)] * PIECES,
        *att_dq, out_weight, planes=((0, OAD),), after=(dkv[0],),
        hbm_out=(0,), scratch=[dma(PLANE)], cost_us=0.01, name="project",
    )
    dkv = plane_exchange(dkv)
    other_sum = [xor_permute(piece, 1, "head") for piece in other_sum]
    output, grad_keys, grad_values = call(
        join_kernel, [shape(rows, features)] * 3, own_sum, *other_sum, *dkv,
        planes=((1 + PIECES, ODKV),),
        hbm_out=True, scratch=[pltpu.VMEM((rows, features), BF16), dma(2 * PLANE + 1)],
        cost_us=1.0, name="join",
    )
    return (output, grad_queries, grad_keys, grad_values)


def solution(mesh):
    rows = P("ctx", "head")
    return jax.shard_map(
        body,
        mesh=mesh,
        in_specs=(rows, rows, rows, P("head", None), rows),
        out_specs=(rows, rows, rows, rows),
        check_vma=False,
    )
```

```python
import jax
import jax.numpy as jnp
from jax import lax
from jax.experimental import pallas as pl
from jax.experimental.pallas import tpu as pltpu
from jax.sharding import PartitionSpec as P

DH = 128
PLANE = 4
PIECES = 2
OKV = (3, 1, 2, 0)
OQG = (2, 1, 3, 0)
OAD = (3, 1, 2, 0)
ODKV = (2, 3, 1, 0)
ORDER = (1, 2, 3)
SCALE = DH ** (-0.5)
SCALE2 = SCALE * 1.4426950408889634
BF16 = jnp.bfloat16
F32 = jnp.float32


def xor_permute(block, mask, axis="ctx"):
    count = lax.axis_size(axis)
    return lax.ppermute(block, axis, [(i, i ^ mask) for i in range(count)])


def dot(a, b, contract_a=1, contract_b=0):
    return lax.dot_general(
        a, b, (((contract_a,), (contract_b,)), ((), ())), preferred_element_type=F32
    )


def pool_matrix(rows):
    out = lax.broadcasted_iota(jnp.int32, (rows // 2, rows), 0)
    src = lax.broadcasted_iota(jnp.int32, (rows // 2, rows), 1)
    return jnp.where(src // 2 == out, 0.5, 0.0).astype(BF16)


def spread_matrix(rows, times):
    out = lax.broadcasted_iota(jnp.int32, (rows * times, rows), 0)
    src = lax.broadcasted_iota(jnp.int32, (rows * times, rows), 1)
    return jnp.where(out // times == src, 1.0 / times, 0.0).astype(BF16)


def pool(block):
    return dot(pool_matrix(block.shape[0]), block).astype(BF16)


def spread(block, times):
    return dot(spread_matrix(block.shape[0], times), block.astype(BF16))


def call(kernel, outs, *args, planes=(), after=(), aliases={}, hbm=(), hbm_out=False, scratch=(), cost_us=1.0, name=None):
    vmem = pl.BlockSpec(memory_space=pltpu.VMEM)
    in_hbm = pl.BlockSpec(memory_space=pltpu.HBM)
    out_hbm = range(len(outs)) if hbm_out is True else hbm_out or ()
    args = [
        pltpu.with_memory_space_constraint(a, pltpu.HBM) if n in hbm else a
        for n, a in enumerate(args)
    ]
    count = len(args)
    order = list(range(count))
    for first in planes:
        order[first[0] : first[0] + PLANE] = [first[0] + r for r in first[1]]
    places = [order.index(n) for n in range(count)]

    def run(*refs):
        kernel(*[refs[at] for at in places], *refs[count + len(after) :])

    return pl.pallas_call(
        run,
        out_shape=[
            (pltpu.HBM if n in out_hbm else pltpu.VMEM)(out.shape, out.dtype)
            for n, out in enumerate(outs)
        ],
        in_specs=[in_hbm if n in hbm else vmem for n in order]
        + [pl.BlockSpec(memory_space=pl.ANY)] * len(after),
        scratch_shapes=scratch,
        input_output_aliases={places[n]: out for n, out in aliases.items()},
        out_specs=[in_hbm if n in out_hbm else vmem for n in range(len(outs))],
        compiler_params=pltpu.CompilerParams(vmem_limit_bytes=24 * 1024 * 1024),
        cost_estimate=pl.CostEstimate(
            flops=int(cost_us * 1e9), bytes_accessed=0, transcendentals=0
        ),
        name=name,
    )(*[args[n] for n in order], *after)


def part(n, width):
    return slice(n * width, (n + 1) * width)


def start_all(pairs, sems):
    copies = [pltpu.make_async_copy(a, b, sems.at[n]) for n, (a, b) in enumerate(pairs)]
    for copy in copies:
        copy.start()
    return copies


def columns(r, width):
    place = (lax.axis_index("ctx") & (PLANE - 1)) ^ r
    return pl.ds(pl.multiple_of(place * width, width), width)


def key_value_kernel(k_ref, v_ref, *refs):
    outs, sems = refs[:-1], refs[-1]
    rows, width = k_ref.shape[0], k_ref.shape[1] // PLANE
    pairs = []
    for r, out in enumerate(outs, 1):
        pairs.append((k_ref.at[:, columns(r, width)], out.at[part(0, rows), :]))
        pairs.append((v_ref.at[:, columns(r, width)], out.at[part(1, rows), :]))
    for copy in start_all(pairs, sems):
        copy.wait()


def cotangent_kernel(q_ref, own_ref, other_ref, w_ref, k_ref, v_ref, *refs):
    outs, kv_out, sems = refs[:PLANE], refs[PLANE], refs[PLANE + 1]
    mine = columns(0, w_ref.shape[0] // PLANE)
    copies = start_all(
        [(ref.at[:, mine], kv_out.at[part(m, q_ref.shape[0]), :]) for m, ref in enumerate((k_ref, v_ref))],
        sems,
    )
    rows, width = q_ref.shape[0], q_ref.shape[1] // PLANE
    half = own_ref.shape[1]
    head = lax.axis_index("head")
    own_at = pl.ds(pl.multiple_of(head * half, half), half)
    other_at = pl.ds(pl.multiple_of((1 - head) * half, half), half)
    for r in range(PLANE):
        here = columns(r, width)
        outs[r][:rows, :] = q_ref[:, here]
        outs[r][rows:, :] = (
            dot(own_ref[...], w_ref[here, own_at], 1, 1)
            + dot(other_ref[...], w_ref[here, other_at], 1, 1)
        ).astype(BF16)
    for copy in copies:
        copy.wait()


def average_matrix(rows, times):
    out = lax.broadcasted_iota(jnp.int32, (rows // times, rows), 0)
    src = lax.broadcasted_iota(jnp.int32, (rows // times, rows), 1)
    return jnp.where(src // times == out, 1.0 / times, 0.0).astype(BF16)


def far_kernel(*refs):
    kvs, outs = refs[:PLANE], refs[PLANE:]
    rows, width = kvs[0].shape[0] // 2, kvs[0].shape[1]
    wide = jnp.concatenate([kv[part(m, rows), :] for m in range(2) for kv in kvs], 1)
    pooled = dot(
        jnp.concatenate([average_matrix(rows, 4), average_matrix(rows, 8)], 0), wide
    ).astype(BF16)
    for out, first, size in zip(outs, (0, rows // 4, rows // 4), (rows // 4, rows // 8, rows // 8)):
        for n in range(2 * PLANE):
            out[part(n, size), :] = pooled[first : first + size, part(n, width)]


def both(blocks, p, rows, lanes):
    return jnp.concatenate([blocks[r][rows, lanes] for r in (2 * p, 2 * p + 1)], 0)


def near_set(kvs, p, lanes, m):
    rows = part(m, kvs[0].shape[0] // 2)
    other = [pool(kv[rows, lanes]) for kv in kvs[2 - 2 * p : 4 - 2 * p]]
    return jnp.concatenate([both(kvs, p, rows, lanes)] + other, 0)


def far_set(fars, lanes, m):
    return jnp.concatenate([far[part(m, far.shape[0] // 2), lanes] for far in fars], 0)


def token_rows(qgs, m, lanes):
    rows = part(m, qgs[0].shape[0] // 2)
    return jnp.concatenate([qg[rows, lanes] for qg in qgs], 0)


def near_kernel(*refs):
    kvs, qgs, first = refs[:PLANE], refs[PLANE : 2 * PLANE], refs[2 * PLANE]
    weight_out, dots_out, sums_out, stats_out, keys_out, turned_out = refs[2 * PLANE + 1 :]
    rows, width = qgs[0].shape[0] // 2, qgs[0].shape[1]
    cases = [(h, p) for h in range(width // DH) for p in range(2)]
    tokens = [part(p, 2 * rows) for h, p in cases]
    keys, values = [
        [
            jnp.concatenate(
                [near_set(kvs, p, part(h, DH), m), first[part(m, first.shape[0] // 2), part(h, DH)]], 0
            )
            for h, p in cases
        ]
        for m in range(2)
    ]
    scores = [
        dot(k, both(qgs, p, part(0, rows), part(h, DH)), 1, 1) * SCALE2
        for k, (h, p) in zip(keys, cases)
    ]
    for (h, p), v, t in zip(cases, values, tokens):
        dots_out[h, :, t] = dot(v, both(qgs, p, part(1, rows), part(h, DH)), 1, 1)
    for n, ((h, p), t) in enumerate(zip(cases, tokens)):
        row_max = jnp.max(scores[n], 0, keepdims=True)
        weights = jnp.exp2(scores[n] - row_max)
        weight_out[h, :, t] = weights
        sums_out[h, :, t] = dot(values[n], weights.astype(BF16), 0, 0)
        stats_out[h, 0:1, t] = row_max
        stats_out[h, 1:2, t] = jnp.sum(weights, 0, keepdims=True)
        keys_out[n] = keys[n]
        turned_out[h, :, t] = both(qgs, p, part(1, rows), part(h, DH)).T


def far_grad_kernel(n_far, *refs):
    qgs, fars = refs[:PLANE], refs[PLANE : PLANE + n_far]
    weight_ref, dots_ref, sums_ref, stats_ref, turned_ref = refs[PLANE + n_far : PLANE + n_far + 5]
    outs = refs[PLANE + n_far + 5 :]
    ads, grad_out, stats_out, far_out = outs[:PLANE], outs[PLANE], outs[PLANE + 1], outs[PLANE + 2 :]
    rows, width = qgs[0].shape[0] // 2, qgs[0].shape[1]
    first = slice(3 * rows, weight_ref.shape[1])
    first_rows = weight_ref.shape[1] - 3 * rows
    heads = range(width // DH)
    lanes = [part(h, DH) for h in heads]
    queries = [token_rows(qgs, 0, at) for at in lanes]
    grads = [token_rows(qgs, 1, at) for at in lanes]
    keys = [far_set(fars, at, 0) for at in lanes]
    values = [far_set(fars, at, 1) for at in lanes]
    scores = [dot(k, q, 1, 1) * SCALE2 for k, q in zip(keys, queries)]
    dots = [dot(v, g, 1, 1) for v, g in zip(values, grads)]
    weights, near_parts, inverses, sums = [], [], [], []
    for h in heads:
        near_max = stats_ref[h, 0:1, :]
        row_max = jnp.maximum(near_max, jnp.max(scores[h], 0, keepdims=True))
        weights.append(jnp.exp2(scores[h] - row_max))
        near_parts.append(jnp.exp2(near_max - row_max))
        sums.append(dot(values[h], weights[h].astype(BF16), 0, 0))
        inverses.append(
            1.0 / (stats_ref[h, 1:2, :] * near_parts[h] + jnp.sum(weights[h], 0, keepdims=True))
        )
    score_grads, probs = [], []
    for h in heads:
        attended = ((sums_ref[h] * near_parts[h] + sums[h]) * inverses[h]).astype(BF16)
        delta = jnp.sum(turned_ref[h].astype(F32) * attended.astype(F32), 0, keepdims=True)
        near_scale = near_parts[h] * inverses[h]
        near_probs = weight_ref[h, first, :] * near_scale
        far_probs = weights[h] * inverses[h]
        score_grads.append(
            jnp.concatenate(
                [
                    (near_probs * (dots_ref[h, first, :] - delta)).astype(BF16),
                    (far_probs * (dots[h] - delta)).astype(BF16),
                ],
                0,
            )
        )
        probs.append(jnp.concatenate([near_probs.astype(BF16), far_probs.astype(BF16)], 0))
        grad_out[h] = score_grads[h][first_rows:]
        stats_out[h, 0:1, :] = near_scale
        stats_out[h, 1:2, :] = delta
        attended = attended.T
        for r in range(PLANE):
            ads[r][:rows, lanes[h]] = attended[part(r, rows)]
    for h in heads:
        for m, whole in enumerate(
            (dot(score_grads[h], queries[h]) * SCALE, dot(probs[h], grads[h]))
        ):
            at = 0
            for far in far_out:
                size = far.shape[0] // 2
                far[part(m, size), lanes[h]] = whole[at : at + size].astype(BF16)
                at += size


def plane_kernel(n_far, *refs):
    qgs, fars = refs[:PLANE], refs[PLANE : PLANE + n_far]
    keys_ref, weight_ref, dots_ref, grad_ref, stats_ref = refs[PLANE + n_far : PLANE + n_far + 5]
    refs = refs[2 * PLANE + n_far + 5 :]
    ads, dkvs = refs[:PLANE], refs[PLANE:]
    rows, width = qgs[0].shape[0] // 2, qgs[0].shape[1]
    pair = 2 * rows
    cases = [(h, p) for h in range(width // DH) for p in range(2)]
    score_grads, probs = [], []
    for h, p in cases:
        tokens = part(p, pair)
        probabilities = weight_ref[h, :, tokens] * stats_ref[h, 0:1, tokens]
        probs.append(probabilities.astype(BF16))
        score_grads.append(
            (probabilities * (dots_ref[h, :, tokens] - stats_ref[h, 1:2, tokens])).astype(BF16)
        )
    for n, (h, p) in enumerate(cases):
        far_keys = far_set(fars, part(h, DH), 0)
        dq = dot(keys_ref[n], score_grads[n], 0, 0)
        dq = dq + dot(far_keys, grad_ref[h, :, part(p, pair)], 0, 0)
        dq = (dq * SCALE).astype(BF16).T
        for k in range(2):
            ads[2 * p + k][rows:, part(h, DH)] = dq[part(k, rows)]
    grads = []
    for n, (h, p) in enumerate(cases):
        q, g = [both(qgs, p, part(m, rows), part(h, DH)) for m in range(2)]
        near = slice(0, 3 * rows)
        grads.append((dot(score_grads[n][near], q) * SCALE, dot(probs[n][near], g)))
    places = [
        (h, m, p, k) for h in range(width // DH) for m in range(2) for p in range(2) for k in range(2)
    ]
    pooled = [
        grads[2 * h + 1 - p][m][pair + k * rows // 2 : pair + (k + 1) * rows // 2]
        for h, m, p, k in places
    ]
    carried = spread(jnp.concatenate(pooled, 1), 2)
    for n, (h, m, p, k) in enumerate(places):
        dkvs[2 * p + k][part(m, rows), part(h, DH)] = (
            grads[2 * h + p][m][part(k, rows)] + carried[:, part(n, DH)]
        )


def carry_kernel(*refs):
    dkvs, far_refs, outs = refs[:PLANE], refs[PLANE:-PLANE], refs[-PLANE:]
    rows, width = dkvs[0].shape[0] // 2, dkvs[0].shape[1]
    wide, matrix = [], []
    for far in far_refs:
        size = far.shape[0] // (2 * PLANE)
        wide.append(jnp.concatenate([far[part(n, size), :] for n in range(2 * PLANE)], 1))
        matrix.append(spread_matrix(size, rows // size))
    carried = dot(jnp.concatenate(matrix, 1), jnp.concatenate(wide, 0))
    for n in range(2 * PLANE):
        m, r = divmod(n, PLANE)
        outs[r][part(m, rows), :] = (
            dkvs[r][part(m, rows), :] + carried[:, part(n, width)]
        ).astype(BF16)


def output_kernel(*refs):
    ads, w_ref, dkv_ref = refs[:PLANE], *refs[PLANE : PLANE + 2]
    gq_out, gk_out, gv_out, own_out = refs[PLANE + 2 : PLANE + 6]
    others, sems = refs[PLANE + 6 : -1], refs[-1]
    rows, width = ads[0].shape[0] // 2, ads[0].shape[1]
    half = own_out.shape[1]
    head = lax.axis_index("head")
    pairs = [(ads[r].at[part(1, rows), :], gq_out.at[:, columns(r, width)]) for r in range(PLANE)]
    for m, out in enumerate((gk_out, gv_out)):
        pairs.append((dkv_ref.at[part(m, rows), :], out.at[:, columns(0, width)]))
    copies = start_all(pairs, sems)
    total = None
    for r in range(PLANE):
        term = dot(ads[r][:rows, :], w_ref[columns(r, width), :])
        total = term if total is None else total + term

    def write(own, other):
        own_out[...] = own
        for n, out in enumerate(others):
            out[...] = other[part(n, rows // PIECES)].astype(BF16)

    @pl.when(head == 0)
    def _():
        write(total[:, :half], total[:, half:])

    @pl.when(head == 1)
    def _():
        write(total[:, half:], total[:, :half])

    for copy in copies:
        copy.wait()


def join_kernel(own_ref, *refs):
    others, refs = refs[:PIECES], refs[PIECES:]
    dkvs = refs[: PLANE - 1]
    o_out, gk_out, gv_out, total, sems = refs[PLANE + 1 :]
    rows, width = dkvs[0].shape[0] // 2, dkvs[0].shape[1]
    pairs = []
    for r, dkv in zip(ODKV, dkvs):
        here = columns(r, width)
        pairs.append((dkv.at[part(0, rows), :], gk_out.at[:, here]))
        pairs.append((dkv.at[part(1, rows), :], gv_out.at[:, here]))
    copies = start_all(pairs, sems)
    for n, other in enumerate(others):
        piece = part(n, rows // PIECES)
        total[piece, :] = (own_ref[piece, :] + other[...].astype(F32)).astype(BF16)
    last = pltpu.make_async_copy(total, o_out, sems.at[len(pairs)])
    last.start()
    for copy in copies + [last]:
        copy.wait()


def plane_exchange(blocks):
    return [blocks[0]] + [xor_permute(blocks[r], r) for r in range(1, PLANE)]


def pool_both(block):
    shaped = block.reshape((2, block.shape[0] // 4, 2) + block.shape[1:]).astype(F32)
    return ((shaped[:, :, 0] + shaped[:, :, 1]) * 0.5).astype(BF16).reshape(
        (block.shape[0] // 2,) + block.shape[1:]
    )


def spread_both(block):
    halved = block.astype(F32) * 0.5
    return jnp.repeat(halved, 2, axis=0)


def join_both(blocks):
    halves = [b.reshape((2, b.shape[0] // 2) + b.shape[1:]) for b in blocks]
    joined = jnp.concatenate(halves, 1)
    return joined.reshape((-1,) + joined.shape[2:])


def part_both(block, parts):
    shaped = block.reshape((2, parts, block.shape[0] // (2 * parts)) + block.shape[1:])
    return [shaped[:, n].reshape((-1,) + block.shape[1:]) for n in range(parts)]


def body(queries, key_rows, value_rows, out_weight, cotangent):
    rows, features = queries.shape
    width = features // PLANE
    top_rounds = lax.axis_size("ctx").bit_length() - 1 - 4
    shape = lambda *dims, t=BF16: jax.ShapeDtypeStruct(dims, t)
    dma = lambda n: pltpu.SemaphoreType.DMA((n,))
    blocks = [shape(2 * rows, width)] * PLANE

    other_cotangent = xor_permute(cotangent, 1, "head")
    key_values = call(
        key_value_kernel, blocks[1:], key_rows, value_rows,
        hbm=(0, 1), scratch=[dma(2 * PLANE - 2)], cost_us=8, name="pack_keys_values",
    )
    *query_grads, own_keys_values = call(
        cotangent_kernel, blocks + blocks[:1], queries, cotangent, other_cotangent, out_weight,
        key_rows, value_rows, hbm=(4, 5), scratch=[dma(2)], cost_us=3.0, name="grad_attended",
    )
    key_values = plane_exchange([own_keys_values, *key_values])
    query_grads = plane_exchange(query_grads)
    near, pooled, pooled3 = call(
        far_kernel, [shape(2 * rows, width)] + [shape(rows, width)] * 2, *key_values, planes=((0, OKV),),
        after=(query_grads[0],), cost_us=1.0, name="pool_plane",
    )
    fars = [xor_permute({1: near, 2: pooled, 3: pooled3}[n], n * PLANE) for n in ORDER]
    if top_rounds > 0:
        got = dict(zip(ORDER, fars))
        span = pool_both(join_both([pooled, pool_both(got[1]), got[2], got[3]]))
        for n in range(top_rounds):
            fars.append(xor_permute(span, 4 * PLANE << n))
            span = pool_both(join_both([span, fars[-1]]))
    far_rows = sum(far.shape[0] for far in fars[1:]) // 2
    heads, tokens = width // DH, PLANE * rows
    near_rows = 3 * rows + fars[0].shape[0] // 2
    weights, dots, sums, stats, near_keys, turned = call(
        near_kernel,
        [shape(heads, near_rows, tokens, t=F32)] * 2
        + [shape(heads, DH, tokens, t=F32), shape(heads, 2, tokens, t=F32)]
        + [shape(2 * heads, near_rows, DH), shape(heads, DH, tokens)],
        *key_values, *query_grads, fars[0], planes=((0, OKV), (PLANE, OQG)), cost_us=2.0, name="near_attention",
    )
    results = call(
        lambda *refs: far_grad_kernel(len(fars) - 1, *refs),
        blocks + [shape(heads, far_rows, tokens), shape(heads, 2, tokens, t=F32)]
        + [shape(*far.shape) for far in fars],
        *query_grads, *fars[1:], weights, dots, sums, stats, turned, planes=((0, OQG),), cost_us=2.0, name="far_attention",
    )
    ads, kept, far_grads = results[:PLANE], results[PLANE : PLANE + 2], list(results[PLANE + 2 :])
    first = PLANE + len(fars) + 4
    results = call(
        lambda *refs: plane_kernel(len(fars) - 1, *refs),
        blocks + [shape(2 * rows, width, t=F32)] * PLANE,
        *query_grads, *fars[1:], near_keys, weights, dots, *kept, *ads,
        aliases={first + r: r for r in range(PLANE)}, cost_us=2.3, name="plane_grads",
    )
    att_dq, dkv = results[:PLANE], results[PLANE:]
    extra = []
    if top_rounds > 0:
        up = None
        for n in reversed(range(top_rounds)):
            send = far_grads[3 + n].astype(F32)
            if up is not None:
                own_up, their_up = part_both(spread_both(up), 2)
                send = send + their_up
            back = xor_permute(send.astype(BF16), 4 * PLANE << n).astype(F32)
            up = back if up is None else back + own_up
        ups = part_both(spread_both(up), PLANE)
        extra = [ups[0].astype(BF16)]
        ups[1] = spread_both(ups[1])
        for at, n in enumerate(ORDER):
            far_grads[at] = (far_grads[at].astype(F32) + ups[n]).astype(BF16)
    backs = [xor_permute(far_grads[at], n * PLANE) for at, n in enumerate(ORDER)]
    att_dq = plane_exchange(att_dq)
    dkv = call(carry_kernel, blocks, *dkv, *backs[1:], backs[0], *extra, cost_us=5.0, name="carry")
    grad_queries, grad_keys, grad_values, own_sum, *other_sum = call(
        output_kernel,
        [shape(rows, features)] * 3 + [shape(rows, features, t=F32)]
        + [shape(rows // PIECES, features)] * PIECES,
        *att_dq, out_weight, dkv[0], planes=((0, OAD),),
        hbm_out=(0, 1, 2), scratch=[dma(PLANE + 2)], cost_us=0.01, name="project",
    )
    dkv = plane_exchange(dkv)
    other_sum = [xor_permute(piece, 1, "head") for piece in other_sum]
    output, grad_keys, grad_values = call(
        join_kernel, [shape(rows, features)] * 3, own_sum, *other_sum,
        *[dkv[r] for r in ODKV[:-1]], grad_keys, grad_values,
        hbm=(PIECES + PLANE, PIECES + PLANE + 1),
        aliases={PIECES + PLANE: 1, PIECES + PLANE + 1: 2},
        hbm_out=True, scratch=[pltpu.VMEM((rows, features), BF16), dma(2 * PLANE - 1)],
        cost_us=1.0, name="join",
    )
    return (output, grad_queries, grad_keys, grad_values)


def solution(mesh):
    rows = P("ctx", "head")
    return jax.shard_map(
        body,
        mesh=mesh,
        in_specs=(rows, rows, rows, P("head", None), rows),
        out_specs=(rows, rows, rows, rows),
        check_vma=False,
    )
```
